32 devices in a mesh: runs: 2 (over y), gx: 4 (over z), gy: 2 (over x), gz: 2 (over core).
Axes of the slice: x: 2, y: 2, z: 4, core: 2. Of those that a mesh axis runs over, the one named last changes fastest.
Arguments:
- velocity_start: float32 [3, 64, 32, 256], P(None, ('runs', 'gx'), 'gy', 'gz'), parts along dimension 1, may hold values from -6 to 6
- stress_start: float32 [6, 64, 32, 256], P(None, ('runs', 'gx'), 'gy', 'gz'), parts along dimension 1, may hold values from -6 to 6
- material: float32 [3, 64, 32, 256], P(None, ('runs', 'gx'), 'gy', 'gz'), parts along dimension 1, may hold values from 0.5 to 2
- force_site: int32 [2], P('runs'), parts along dimension 0, may hold values from 0 to 262143
- force_wavelet: float32 [4, 3], P('runs'), parts along dimension 0, may hold values from -8 to 8
- save_cells: int32 [8, 2, 2, 1024], P(('runs', 'gx'), 'gy', 'gz'), parts along dimension 0, may hold values from 0 to 16383
- save_writer: int32 [8, 2, 2, 1024, 1], P(('runs', 'gx'), 'gy', 'gz'), parts along dimension 0, may hold values from 0 to 7; in each aligned block of 1024 rows (0 to 1023, 1024 to 2047, ..., all dimensions but the last counted through in order) at most 256 rows name the same one
Outputs:
- velocity: float32 [3, 64, 32, 256], P(None, ('runs', 'gx'), 'gy', 'gz'), parts along dimension 1
- strain_saved: float32 [4, 12, 16384], P(('runs', 'gz'), None, ('gx', 'gy')), parts along dimension 0
The draws below stay inside these ranges and needn't reach their ends.
There are 2 independent parts, one for each index of `runs`. The reference program is written for one: setup_inputs(seed, part) draws one part's arguments, and reference() takes and returns one part's arrays. A program takes and returns all parts, laid end to end along the dimension named above; each array names one. Nothing has to cross between parts.
Inputs may be any that keep to these rules, and one draw needn't show every extreme that they name: `force_site`: flat index x 32 * 256 + y * 256 + z of the site. `save_cells`: flat index of the grid point within the device's block of 8 x 16 x 128 points, x slowest and depth fastest; several save points may share a grid point. `save_writer`: writer a * 2 + b among the devices (a, b) that hold the same depth index; among the 1024 save points of one device at most 256 name the same writer, and in every draw some device names some writer exactly 256 times.
All inputs are finite; a program needn't handle non-finite values.
Results may differ from the reference program's by a relative error of at most 0.0003.
Values sent between devices are 32-bit elements; how exact they have to be, the bound alone decides.
No kernel may reach another device: no remote copies, remote signals or barrier semaphores. Data moves between devices by JAX's collectives and lax.ppermute only.
A program may use at most 64 MiB of HBM per device.

```python
import math
import jax
import jax.numpy as jnp
import numpy as np
from jax import lax

CX = 8
CY = 16
CZ = 128
STEPS = 2
SLOT = 1024
NX = 32
NY = 32
NZ = 256
CAP = 256
N_GX = 4
N_GY = 2
N_GZ = 2


def plant(entries, rng, smallest, high):
    longest = entries.shape.index(max(entries.shape))
    spots = []
    for shift in (0, 1):
        where = [jax.random.randint(jax.random.fold_in(rng, axis), (), 0, length) for axis, length in enumerate(entries.shape)]
        where[longest] = (where[longest] + shift) % entries.shape[longest]
        spots.append(tuple(where))
    return entries.at[spots[0]].set(smallest).at[spots[1]].set(high)


def steps_of(own_key, shape, cuts, smallest, largest):
    level = 1.0
    for axis_at, parts in cuts:
        steps = jax.random.uniform(jax.random.fold_in(jax.random.fold_in(own_key, 6), axis_at), (parts,), jnp.float32, smallest / len(cuts), largest / len(cuts))
        level = level * jnp.repeat(jnp.exp(steps), shape[axis_at] // parts).reshape((-1,) + (1,) * (len(shape) - 1 - axis_at))
    return level


def deal_out(own_key, own, number, rows, count, top, bound, lean):
    sequence = jax.random.permutation(own_key, count)
    heavy_load, usual = load_shares(count, rows * top, bound, lean, True), load_shares(count, rows * top, bound, lean, False)
    places = jnp.arange(count)

    def named(tallies, turn):
        used = int((tallies > 0).sum())
        fixed = max(1, used // 4)
        passed = fixed + (places - fixed + turn * (used - fixed)) % max(1, count - fixed)
        return jnp.zeros((count,), jnp.int32).at[sequence[jnp.where(places < fixed, places, passed)]].set(jnp.asarray(tallies, jnp.int32))

    tallies = jnp.where(number % 4 == 0, named(heavy_load, number // 4), named(usual, number - number // 4 - 1))
    mixed = jax.random.permutation(jax.random.fold_in(own, 3), count)
    source_of, receiver = mixed[0:count // 2 * 2:2], mixed[1:count // 2 * 2:2]
    slack = jnp.minimum(tallies[source_of] - 1, bound - tallies[receiver]) // 2
    slack = jnp.where((source_of == sequence[0]) | (receiver == sequence[0]) | (tallies[receiver] == 0), 0, jnp.maximum(slack, 0))
    passed = jax.random.randint(jax.random.fold_in(own, 4), (count // 2,), 0, 1 << 20) % (slack + 1)
    tallies = tallies.at[source_of].add(-passed).at[receiver].add(passed)
    members = jnp.searchsorted(jnp.cumsum(tallies), jnp.arange(rows * top), side="right").astype(jnp.int32)
    grid = members.reshape(top, rows).T
    grid = grid[jax.random.permutation(jax.random.fold_in(own, 1), rows)]
    turn = jax.random.randint(jax.random.fold_in(own, 2), (rows, 1), 0, top)
    return jnp.take_along_axis(grid, (jnp.arange(top)[None, :] + turn) % top, axis=1)


def load_shares(number_of, total, reach, skew, full):
    weights = [(1 << 20) // math.isqrt(grade ** skew) + 1 for grade in range(1, number_of + 1)]
    largest = reach if full else min(reach, max(-(-total // number_of), total * weights[0] // sum(weights)))
    least = 1 if total - largest >= number_of - 1 else 0
    given, rest = [largest] + [least] * (number_of - 1), total - largest - least * (number_of - 1)
    while rest > 0:
        free = [i for i in range(1, number_of) if given[i] < largest] or [i for i in range(1, number_of) if given[i] < reach]
        pool, budget = sum([weights[i] for i in free]), rest
        for i in free:
            addition = min(reach - given[i], max(1, budget * weights[i] // pool), rest)
            given[i] = given[i] + addition
            rest = rest - addition
    return np.array(given)


def normal_values(stream_key, dims, deviation, limit, split=(), held_as=jnp.bfloat16):
    values = jax.random.normal(stream_key, dims, jnp.float32) * deviation
    if len(split) > 0:
        values = steps_of(stream_key, dims, split, -0.22, 0.18) * values
    return jnp.clip(values, min=-limit, max=limit).astype(held_as)


def setup_inputs(seed: int = 0, part: int = 0) -> dict:
    key_list = jax.random.split(jax.random.key(seed), 8)
    part_keys = jax.random.split(jax.random.fold_in(key_list[7], part), 8)
    velocity_start = normal_values(part_keys[0], (3, NX, NY, NZ), 1.0, 6.0, ((1, 4), (2, 2), (3, 2)), jnp.float32)
    stress_start = normal_values(part_keys[1], (6, NX, NY, NZ), 1.0, 6.0, ((1, 4), (2, 2), (3, 2)), jnp.float32)
    material = jnp.clip(jnp.exp(math.log(2.0) - 1.3862944 * jax.random.uniform(part_keys[2], (3, NX, NY, NZ), jnp.float32) ** steps_of(part_keys[2], (3, NX, NY, NZ), ((1, 4), (2, 2), (3, 2)), -0.2, 0.2)), 0.5, 2.0)
    force_site = jax.random.randint(part_keys[3], (1,), 0, NX * NY * NZ).astype(jnp.int32)
    force_wavelet = jnp.clip(jax.random.uniform(part_keys[4], (STEPS, 3), jnp.float32, -8.0, 8.0), -8.0, 8.0)
    save_cells = plant(jax.random.randint(part_keys[5], (N_GX, N_GY, N_GZ, SLOT), 0, CX * CY * CZ), jax.random.fold_in(part_keys[5], 1), 0, (CX * CY * CZ) - 1).astype(jnp.int32)
    save_writer_keys = jax.random.split(jax.random.fold_in(part_keys[6], 1), N_GX * N_GY * N_GZ * SLOT // SLOT)
    save_writer_turns = jax.random.permutation(jax.random.fold_in(part_keys[6], 3), N_GX * N_GY * N_GZ * SLOT // SLOT)
    save_writer = jax.vmap(lambda own, number: deal_out(jax.random.fold_in(part_keys[6], 2), own, number, SLOT, N_GX * N_GY, 1, CAP, 2))(save_writer_keys, save_writer_turns).reshape((N_GX, N_GY, N_GZ, SLOT, 1))
    return {"velocity_start": velocity_start, "stress_start": stress_start, "material": material, "force_site": force_site, "force_wavelet": force_wavelet, "save_cells": save_cells, "save_writer": save_writer}


INNER = 9.0 / 8.0
OUTER = -1.0 / 24.0
TIME_STEP = 0.12


def shifted(values, offset, dimension):
    config = [(0, 0, 0)] * values.ndim
    config[dimension] = (offset, -offset, 0)
    return lax.pad(values, jnp.zeros((), values.dtype), config)


def forward(values, dimension):
    return INNER * (shifted(values, -1, dimension) - values) + OUTER * (shifted(values, -2, dimension) - shifted(values, 1, dimension))


def backward(values, dimension):
    return INNER * (values - shifted(values, 1, dimension)) + OUTER * (shifted(values, -1, dimension) - shifted(values, 2, dimension))


def velocity_rates(stress):
    return jnp.stack([
        forward(stress[0], 0) + backward(stress[3], 1) + backward(stress[4], 2),
        backward(stress[3], 0) + forward(stress[1], 1) + backward(stress[5], 2),
        backward(stress[4], 0) + backward(stress[5], 1) + forward(stress[2], 2)])


def velocity_gradients(velocity):
    return jnp.stack([
        backward(velocity[0], 0), backward(velocity[1], 1), backward(velocity[2], 2),
        forward(velocity[0], 1) + forward(velocity[1], 0),
        forward(velocity[0], 2) + forward(velocity[2], 0),
        forward(velocity[1], 2) + forward(velocity[2], 1)])


def stress_update(stress, gradients, lame_first, shear):
    volume = gradients[0] + gradients[1] + gradients[2]
    normal = stress[:3] + TIME_STEP * (2.0 * shear * gradients[:3] + lame_first * volume)
    sliding = stress[3:] + TIME_STEP * shear * gradients[3:]
    return jnp.concatenate([normal, sliding], axis=0)


def strain_of(points, lame_points, shear_points):
    trace_sum = points[0] + points[1] + points[2]
    shrink = lame_points / (3.0 * lame_points + 2.0 * shear_points) * trace_sum
    normal = (points[:3] - shrink) / (2.0 * shear_points)
    sliding = points[3:] / (2.0 * shear_points)
    return jnp.concatenate([normal, sliding], axis=0)


def bucket_slots(writers, width, capacity):
    onehot = (writers[:, None] == jnp.arange(width, dtype=jnp.int32)[None, :]).astype(jnp.int32)
    before = jnp.cumsum(onehot, axis=0) - onehot
    position = jnp.sum(before * onehot, axis=1).astype(jnp.int32)
    return (writers * capacity + position).astype(jnp.int32)


def blocks(field):
    return field.reshape(N_GX, CX, N_GY, CY, N_GZ, CZ).transpose(0, 2, 4, 1, 3, 5).reshape(N_GX, N_GY, N_GZ, CX * CY * CZ)


def reference(velocity_start, stress_start, material, force_site, force_wavelet, save_cells, save_writer):
    velocity = velocity_start
    stress = stress_start
    lame_first = material[0]
    shear = material[1]
    buoyancy = material[2]
    site = force_site[0]
    site_x = site // (NY * NZ)
    site_y = (site // NZ) % NY
    site_z = site % NZ
    lame_points = jnp.take_along_axis(blocks(lame_first), save_cells, axis=3)
    shear_points = jnp.take_along_axis(blocks(shear), save_cells, axis=3)
    saved = []
    for step_index in range(STEPS):
        velocity = velocity + TIME_STEP * buoyancy * velocity_rates(stress)
        velocity = velocity.at[:, site_x, site_y, site_z].add(TIME_STEP * buoyancy[site_x, site_y, site_z] * force_wavelet[step_index])
        stress = stress_update(stress, velocity_gradients(velocity), lame_first, shear)
        points = jnp.stack([jnp.take_along_axis(blocks(stress[component]), save_cells, axis=3) for component in range(6)])
        saved.append(strain_of(points, lame_points, shear_points))
    values = jnp.concatenate(saved, axis=0)
    width = N_GX * N_GY
    writers_flat = save_writer.reshape(-1, SLOT)
    targets = jax.vmap(lambda writers: bucket_slots(writers, width, CAP))(writers_flat)
    values_flat = values.reshape(6 * STEPS, -1, SLOT).transpose(1, 0, 2)
    buffers = jax.vmap(lambda rows, target: jnp.zeros((6 * STEPS, width * CAP), jnp.float32).at[:, target].set(rows))(values_flat, targets)
    arranged = buffers.reshape(N_GX, N_GY, N_GZ, 6 * STEPS, width, CAP).transpose(2, 3, 4, 0, 1, 5).reshape(N_GZ, 6 * STEPS, width * width * CAP)
    return velocity, arranged
```

```python
import jax
import jax.numpy as jnp
from jax import lax
from jax.experimental import pallas as pl
from jax.experimental.pallas import tpu as pltpu
from jax.sharding import PartitionSpec as P

STEPS = 2
TIME_STEP = 0.12

SXX, SYY, SZZ, SXY, SXZ, SYZ, VX, VY, VZ, LAM, MU, BUOY = range(12)
FIELDS = 12
DEPTHS = (6, 5, 5, 6, 6, 5, 5, 5, 5, 3, 3, 5)
OFFSETS = tuple(sum(DEPTHS[:f]) for f in range(FIELDS + 1))
HALO = 6
LAYERS = OFFSETS[-1]
ROWS = 8
STRIP = 8
LANES = 128
CORNER_WHOLE = tuple((f, d) for f in (SXX, SYY, SXY, SXZ, SYZ) for d in (1, 2))
CORNER_HALF = (
    tuple((f, d) for f in (SXX, SYY, SXY, SXZ, SYZ) for d in (3, 4, 5))
    + tuple((f, d) for f in (SZZ, VX, VY, VZ, BUOY) for d in (1, 2, 3))
    + tuple((f, d) for f in (LAM, MU) for d in (1, 2))
)
CORNERS = len(CORNER_WHOLE) + (len(CORNER_HALF) + 1) // 2
VMEM_LIMIT = 40 * 1024 * 1024
VMEM = pl.BlockSpec(memory_space=pltpu.VMEM)
SMEM = pl.BlockSpec(memory_space=pltpu.SMEM)


def f32(*shape):
    return jax.ShapeDtypeStruct(shape, jnp.float32)


def groups(count):
    return -(-count // (LANES // STRIP))


def iota(dimension, shape=(ROWS, LANES)):
    return lax.broadcasted_iota(jnp.int32, shape, dimension)


def pack_strips(tiles, head):
    slot = iota(1) // STRIP
    packed = None
    for at, tile in enumerate(tiles):
        turned = pltpu.roll(tile, (STRIP * at + head) & (LANES - 1), 1)
        packed = turned if packed is None else jnp.where(slot == at, turned, packed)
    return packed


def source(refs, field):
    stress, velocity, material = refs
    if field < VX:
        return stress, field
    if field < LAM:
        return velocity, field - VX
    return material, field - LAM


class Grid:
    def __init__(self, block, counts):
        self.cx, self.cy, self.cz = block
        self.gx, self.gy, self.gz = counts
        self.x_pairs = ("even", "odd") if self.gx > 2 else ("even",)
        self.y_pairs = ("even", "odd") if self.gy > 2 else ("even",)
        self.rows = self.cy + ROWS * len(self.y_pairs)
        self.layers = self.cx + 2 * HALO
        self.tiles_y = self.cy // ROWS

    def pairs(self, count, kind):
        start = 0 if kind == "even" else 1
        out = []
        for i in range(start, count - 1, 2):
            out += [(i, i + 1), (i + 1, i)]
        return out

    def pieces(self):
        out = [(("x", a), LAYERS * self.tiles_y) for a in self.x_pairs]
        out += [(("y", b), FIELDS * self.cx) for b in self.y_pairs]
        out += [(("d", a, b), CORNERS) for b in self.y_pairs for a in self.x_pairs]
        return out

    def shape(self, name):
        if name[0] == "x":
            return (LAYERS, self.cy, self.cz)
        if name[0] == "y":
            return (FIELDS, self.cx, ROWS, self.cz)
        return (CORNERS, ROWS, self.cz)


def above(axis, kind):
    parity = lax.rem(lax.axis_index(axis), 2)
    return parity == (0 if kind == "even" else 1)


def pack_kernel(grid, *refs):
    sources = refs[:3]
    outs = refs[3:]
    own = outs[-1]
    sub = iota(0)
    for (name, _), out in zip(grid.pieces(), outs):
        if name[0] == "x":
            high = above("gx", name[1])
            for f in range(FIELDS):
                ref, at = source(sources, f)
                n = DEPTHS[f]
                start = jnp.where(high, grid.cx - n, 0)
                out[OFFSETS[f] : OFFSETS[f + 1]] = ref[at, pl.ds(start, n)]
        elif name[0] == "y":
            row = pl.multiple_of(jnp.where(above("gy", name[1]), grid.cy - ROWS, 0), ROWS)
            for f in range(FIELDS):
                ref, at = source(sources, f)
                out[f] = ref[at, :, pl.ds(row, ROWS), :]
        else:
            high = above("gx", name[1])
            up = above("gy", name[2])
            row = pl.multiple_of(jnp.where(up, grid.cy - ROWS, 0), ROWS)

            def tile(field, distance):
                ref, at = source(sources, field)
                layer = jnp.where(high, grid.cx - distance, distance - 1)
                return ref[at, layer, pl.ds(row, ROWS), :]

            for i, (f, d) in enumerate(CORNER_WHOLE):
                out[i] = tile(f, d)
            for i in range(0, len(CORNER_HALF), 2):
                first = tile(*CORNER_HALF[i])
                second = tile(*CORNER_HALF[min(i + 1, len(CORNER_HALF) - 1)])
                turned = pltpu.roll(jnp.where(up, first, second), 4, 0)
                lower = jnp.where(up, turned, first)
                upper = jnp.where(up, second, turned)
                out[len(CORNER_WHOLE) + i // 2] = jnp.where(sub < 4, lower, upper)
    head = jnp.where(lax.axis_index("gz") == 0, STRIP, 0)
    tiles = [(f, x, r) for f in range(FIELDS) for x in range(grid.cx) for r in range(grid.tiles_y)]
    for g in range(groups(len(tiles))):
        part = []
        for f, x, r in tiles[16 * g : 16 * g + 16]:
            ref, at = source(sources, f)
            part.append(ref[at, x, ROWS * r : ROWS * r + ROWS, :])
        own[g] = pack_strips(part, head)


def piece_tile(name, ref, at, grid):
    if name[0] == "x":
        r = at % grid.tiles_y
        return ref[at // grid.tiles_y, ROWS * r : ROWS * r + ROWS, :]
    if name[0] == "y":
        return ref[at // grid.cx, at % grid.cx]
    return ref[at]


def strip_kernel(grid, *refs):
    out = refs[-1]
    head = jnp.where(lax.axis_index("gz") == 0, STRIP, 0)
    base = 0
    for (name, count), ref in zip(grid.pieces(), refs[:-1]):
        for g in range(groups(count)):
            tiles = [
                piece_tile(name, ref, at, grid) for at in range(16 * g, min(16 * g + 16, count))
            ]
            out[base + g] = pack_strips(tiles, head)
        base += groups(count)


def slot_kernel(width, capacity, cz, cells_ref, writers_ref, lanes_ref, rows_ref):
    count = cells_ref.shape[1]
    cells = cells_ref[...]
    writers = writers_ref[...]
    padded = max(16, width)
    named = (iota(0, (padded, count)) == writers).astype(jnp.float32)
    earlier = (iota(0, (count, count)) < iota(1, (count, count))).astype(jnp.float32)
    before = jnp.dot(
        named.astype(jnp.bfloat16), earlier.astype(jnp.bfloat16), preferred_element_type=jnp.float32
    )
    position = jnp.sum(before * named, axis=0, keepdims=True).astype(jnp.int32)
    target = writers * capacity + position
    which = iota(0, (16, count))
    lane = lax.rem(cells, cz)
    row = lax.div(cells, cz)
    values = jnp.where(which == 0, lane, jnp.where(which == 1, row, jnp.where(which == 2, 1, 0)))
    values = values.astype(jnp.float32).astype(jnp.bfloat16)
    step = 256
    for n in range(width * capacity // step):
        hit = (iota(0, (step, count)) + n * step == target).astype(jnp.float32)
        table = lax.dot_general(
            values,
            hit.astype(jnp.bfloat16),
            (((1,), (1,)), ((), ())),
            preferred_element_type=jnp.float32,
        )
        lane_of = jnp.where(table[2:3] > 0.5, table[0:1], -1.0).astype(jnp.int32)
        marks = (iota(0, (cz, step)) == lane_of).astype(jnp.float32).astype(jnp.bfloat16)
        lanes_ref[0:cz, n * step : (n + 1) * step] = marks
        lanes_ref[cz : 2 * cz, n * step : (n + 1) * step] = marks
        rows_ref[:, n * step : (n + 1) * step] = jnp.broadcast_to(
            table[1:2].astype(jnp.int32), (ROWS, step)
        )


def main_kernel(grid, *refs):
    pieces = grid.pieces()
    n = len(pieces)
    sources = refs[:3]
    own_strips = refs[3]
    arrived = refs[4 : 4 + n]
    strips, lanes_ref, rows_ref, site_ref, wavelet_ref = refs[4 + n : 9 + n]
    velocity_out, table_out = refs[9 + n : 11 + n]
    ext, sampled = refs[11 + n :]
    rows = grid.rows
    cx, cy, cz = grid.cx, grid.cy, grid.cz
    half = lax.axis_index("gz")
    other = 1 - half
    sub = iota(0)
    lead = jnp.where(half == 0, 0, LANES - STRIP)

    def edge(up):
        if len(grid.y_pairs) > 1:
            return lambda tile: tile
        low, top = jnp.where(up, 6, 0), jnp.where(up, 8, 2)
        keep = jnp.logical_or(sub < low, sub >= top)
        return lambda tile: jnp.where(keep, tile, 0.0)

    def row_of(up):
        if len(grid.y_pairs) == 1:
            return cy
        return pl.multiple_of(jnp.where(up, cy, cy + ROWS), ROWS)

    for f in range(FIELDS):
        for x in list(range(HALO)) + list(range(HALO + cx, grid.layers)):
            for h in range(2):
                ext[f, h, x, cy:rows, :] = jnp.zeros((rows - cy, cz), jnp.float32)

    def unpack(ref, base, at):
        return pltpu.roll(ref[base + at // 16], (lead - STRIP * (at % 16)) & (LANES - 1), 1)

    at = 0
    for f in range(FIELDS):
        ref, k = source(sources, f)
        for x in range(cx):
            ext[f, half, HALO + x, 0:cy, :] = ref[k, x]
            for r in range(grid.tiles_y):
                ext[f, other, HALO + x, ROWS * r : ROWS * r + ROWS, :] = unpack(own_strips, 0, at)
                at += 1
    base = 0
    for (name, count), ref in zip(pieces, arrived):
        if name[0] == "x":
            high = above("gx", name[1])
            at = 0
            for f in range(FIELDS):
                start = jnp.where(high, HALO + cx, HALO - DEPTHS[f])
                for d in range(DEPTHS[f]):
                    ext[f, half, start + d, 0:cy, :] = ref[OFFSETS[f] + d]
                    for r in range(grid.tiles_y):
                        ext[f, other, start + d, ROWS * r : ROWS * r + ROWS, :] = unpack(
                            strips, base, at
                        )
                        at += 1
        elif name[0] == "y":
            up = above("gy", name[1])
            clear = edge(up)
            place = row_of(up)
            for f in range(FIELDS):
                for x in range(cx):
                    ext[f, half, HALO + x, pl.ds(place, ROWS), :] = clear(ref[f, x])
                    ext[f, other, HALO + x, pl.ds(place, ROWS), :] = clear(
                        unpack(strips, base, f * cx + x)
                    )
        else:
            high = above("gx", name[1])
            up = above("gy", name[2])
            clear = edge(up)
            place = row_of(up)

            def put(h, field, distance, tile):
                layer = jnp.where(high, HALO + cx - 1 + distance, HALO - distance)
                ext[field, h, layer, pl.ds(place, ROWS), :] = clear(tile)

            for h, tile_of in ((half, lambda i: ref[i]), (other, lambda i: unpack(strips, base, i))):
                for i, (f, d) in enumerate(CORNER_WHOLE):
                    put(h, f, d, tile_of(i))
                for i in range(0, len(CORNER_HALF), 2):
                    tile = tile_of(len(CORNER_WHOLE) + i // 2)
                    turned = pltpu.roll(tile, 4, 0)
                    put(h, *CORNER_HALF[i], jnp.where(up, tile, turned))
                    if i + 1 < len(CORNER_HALF):
                        put(h, *CORNER_HALF[i + 1], jnp.where(up, turned, tile))
        base += groups(count)

    lane_all = iota(1, (rows, cz))
    lane = iota(1)

    def pair(field, x):
        return ext[field, 0, x], ext[field, 1, x]

    def add(a, b):
        return a[0] + b[0], a[1] + b[1]

    def sub_(a, b):
        return a[0] - b[0], a[1] - b[1]

    def along_x(field, x):
        return (
            sub_(pair(field, x + 1), pair(field, x)),
            sub_(pair(field, x + 2), pair(field, x - 1)),
        )

    def moved_y(a, offset):
        return tuple(pltpu.roll(v, -offset % rows, 0) for v in a)

    def moved_z(a, offset):
        low = pltpu.roll(a[0], -offset % cz, 1)
        high = pltpu.roll(a[1], -offset % cz, 1)
        if offset > 0:
            inside = lane_all < cz - offset
            return jnp.where(inside, low, high), jnp.where(inside, high, 0.0)
        inside = lane_all >= -offset
        return jnp.where(inside, low, 0.0), jnp.where(inside, high, low)

    def forward(a, move):
        return sub_(move(a, 1), a), sub_(move(a, 2), move(a, -1))

    def backward(a, move):
        return sub_(a, move(a, -1)), sub_(move(a, 1), move(a, -2))

    def total(*terms):
        near, far = terms[0]
        for other_near, other_far in terms[1:]:
            near, far = add(near, other_near), add(far, other_far)
        return tuple(27.0 * p - q for p, q in zip(near, far))

    scale = TIME_STEP / 24.0

    def velocity_layer(x):
        y = x + 1
        sxy_x, sxz_x = pair(SXY, x), pair(SXZ, x)
        rate_x = total(along_x(SXX, x), backward(sxy_x, moved_y), backward(sxz_x, moved_z))
        syz = pair(SYZ, y)
        rate_y = total(
            along_x(SXY, y - 1), forward(pair(SYY, y), moved_y), backward(syz, moved_z)
        )
        rate_z = total(
            along_x(SXZ, y - 1), backward(syz, moved_y), forward(pair(SZZ, y), moved_z)
        )
        for h in range(2):
            b = scale * ext[BUOY, h, x]
            ext[VX, h, x] = ext[VX, h, x] + b * rate_x[h]
            b = scale * ext[BUOY, h, y]
            ext[VY, h, y] = ext[VY, h, y] + b * rate_y[h]
            ext[VZ, h, y] = ext[VZ, h, y] + b * rate_z[h]

    def stress_layer(x):
        vx, vy, vz = pair(VX, x), pair(VY, x), pair(VZ, x)
        gxx = total(along_x(VX, x - 1))
        gyy = total(backward(vy, moved_y))
        gzz = total(backward(vz, moved_z))
        gxy = total(forward(vx, moved_y), along_x(VY, x))
        gxz = total(forward(vx, moved_z), along_x(VZ, x))
        gyz = total(forward(vy, moved_z), forward(vz, moved_y))
        for h in range(2):
            shear = scale * ext[MU, h, x]
            volume = scale * ext[LAM, h, x] * (gxx[h] + gyy[h] + gzz[h])
            twice = 2.0 * shear
            ext[SXX, h, x] = ext[SXX, h, x] + (twice * gxx[h] + volume)
            ext[SYY, h, x] = ext[SYY, h, x] + (twice * gyy[h] + volume)
            ext[SZZ, h, x] = ext[SZZ, h, x] + (twice * gzz[h] + volume)
            ext[SXY, h, x] = ext[SXY, h, x] + shear * gxy[h]
            ext[SXZ, h, x] = ext[SXZ, h, x] + shear * gxz[h]
            ext[SYZ, h, x] = ext[SYZ, h, x] + shear * gyz[h]

    def loop(first, last, body):
        def step(x, carry):
            body(x)
            return carry

        lax.fori_loop(HALO + first, HALO + last + 1, step, 0)

    site = site_ref[0]
    total_y, total_z = cy * grid.gy, cz * grid.gz
    site_x = lax.div(site, total_y * total_z) - lax.axis_index("gx") * cx
    site_y = lax.rem(lax.div(site, total_z), total_y) - lax.axis_index("gy") * cy
    site_z = lax.rem(site, total_z)
    near = jnp.logical_and(site_x >= -HALO, site_x < cx + HALO)
    near = jnp.logical_and(near, jnp.logical_and(site_y >= -ROWS, site_y < cy + ROWS))
    site_row = jnp.where(site_y < 0, site_y + rows, site_y)

    def inject(step):
        @pl.when(near)
        def _():
            h = lax.div(site_z, cz)
            x = site_x + HALO
            row = pl.multiple_of(lax.div(site_row, ROWS) * ROWS, ROWS)
            here = jnp.logical_and(sub == lax.rem(site_row, ROWS), lane == lax.rem(site_z, cz))
            amount = jnp.where(here, TIME_STEP * ext[BUOY, h, x, pl.ds(row, ROWS), :], 0.0)
            for c in range(3):
                ext[VX + c, h, x, pl.ds(row, ROWS), :] = (
                    ext[VX + c, h, x, pl.ds(row, ROWS), :] + amount * wavelet_ref[step, c]
                )

    def strain_layer(x):
        lam = ext[LAM, half, x, 0:cy, :]
        shear = ext[MU, half, x, 0:cy, :]
        parts = [ext[f, half, x, 0:cy, :] for f in range(6)]
        shrink = lam / (3.0 * lam + 2.0 * shear) * (parts[0] + parts[1] + parts[2])
        inverse = 0.5 / shear
        for f in range(6):
            value = (parts[f] - shrink if f < 3 else parts[f]) * inverse
            head = value.astype(jnp.bfloat16)
            tail = (value - head.astype(jnp.float32)).astype(jnp.bfloat16)
            row = pl.multiple_of(f * cx * cy + (x - HALO) * cy, cy)
            sampled[pl.ds(row, cy), 0:cz] = head
            sampled[pl.ds(row, cy), cz : 2 * cz] = tail

    step_slots = 256
    block = cx * cy

    def sample(step):
        def body(k, carry):
            where = pl.ds(pl.multiple_of(k * step_slots, step_slots), step_slots)
            found = jnp.dot(
                sampled[...], lanes_ref[:, where], preferred_element_type=jnp.float32
            )
            row = rows_ref[:, where]
            for f in range(6):
                acc = jnp.zeros((ROWS, step_slots), jnp.float32)
                for r in range(block // ROWS):
                    tile = found[f * block + r * ROWS : f * block + r * ROWS + ROWS]
                    acc = acc + jnp.where(row == r * ROWS + iota(0, (ROWS, step_slots)), tile, 0.0)
                table_out[k, step * 6 + f : step * 6 + f + 1, :] = jnp.sum(
                    acc, axis=0, keepdims=True
                )
            return carry

        lax.fori_loop(0, lanes_ref.shape[1] // step_slots, body, 0)

    velocity_ranges = ((-5, cx + 3), (-2, cx))
    stress_ranges = ((-3, cx + 2), (0, cx - 1))
    for step in range(STEPS):
        loop(*velocity_ranges[step], velocity_layer)
        inject(step)
        loop(*stress_ranges[step], stress_layer)
        loop(0, cx - 1, strain_layer)
        sample(step)
    for c in range(3):
        for x in range(cx):
            velocity_out[c, x] = ext[VX + c, half, HALO + x, 0:cy, :]


def per_device(
    velocity_start, stress_start, material, force_site, force_wavelet, save_cells, save_writer
):
    counts = tuple(lax.axis_size(axis) for axis in ("gx", "gy", "gz"))
    grid = Grid(velocity_start.shape[1:], counts)
    pieces = grid.pieces()
    params = pltpu.CompilerParams(vmem_limit_bytes=VMEM_LIMIT)
    own_tiles = FIELDS * grid.cx * grid.tiles_y
    sources = (stress_start, velocity_start, material)
    packed = pl.pallas_call(
        lambda *refs: pack_kernel(grid, *refs),
        out_shape=[f32(*grid.shape(name)) for name, _ in pieces]
        + [f32(groups(own_tiles), ROWS, LANES)],
        in_specs=[VMEM] * 3,
        out_specs=[VMEM] * (len(pieces) + 1),
        compiler_params=params,
        name="pack_halos",
    )(*sources)
    swap = [(0, 1), (1, 0)]
    arrived = []
    for (name, _), piece in zip(pieces, packed):
        if name[0] == "x":
            arrived.append(lax.ppermute(piece, "gx", grid.pairs(grid.gx, name[1])))
        elif name[0] == "y":
            arrived.append(lax.ppermute(piece, "gy", grid.pairs(grid.gy, name[1])))
        else:
            pairs = [
                (a * grid.gy + b, c * grid.gy + d)
                for a, c in grid.pairs(grid.gx, name[1])
                for b, d in grid.pairs(grid.gy, name[2])
            ]
            arrived.append(lax.ppermute(piece, ("gx", "gy"), pairs))
    own_strips = lax.ppermute(packed[-1], "gz", swap)

    count = save_cells.size
    width = grid.gx * grid.gy
    capacity = max(2, 2 * count // width)
    slots = width * capacity
    lanes, rows = pl.pallas_call(
        lambda *refs: slot_kernel(width, capacity, grid.cz, *refs),
        out_shape=[
            jax.ShapeDtypeStruct((2 * grid.cz, slots), jnp.bfloat16),
            jax.ShapeDtypeStruct((ROWS, slots), jnp.int32),
        ],
        in_specs=[VMEM] * 2,
        out_specs=[VMEM] * 2,
        compiler_params=params,
        name="slot_tables",
    )(save_cells.reshape(1, count), save_writer.reshape(1, count))

    strips = pl.pallas_call(
        lambda *refs: strip_kernel(grid, *refs),
        out_shape=f32(sum(groups(c) for _, c in pieces), ROWS, LANES),
        in_specs=[VMEM] * len(pieces),
        out_specs=VMEM,
        compiler_params=params,
        name="pack_strips",
    )(*arrived)
    strips = lax.ppermute(strips, "gz", swap)

    velocity, table = pl.pallas_call(
        lambda *refs: main_kernel(grid, *refs),
        out_shape=[f32(*velocity_start.shape), f32(slots // 256, 6 * STEPS, 256)],
        in_specs=[VMEM] * (4 + len(pieces) + 3) + [SMEM] * 2,
        out_specs=[VMEM] * 2,
        scratch_shapes=[
            pltpu.VMEM((FIELDS, 2, grid.layers, grid.rows, grid.cz), jnp.float32),
            pltpu.VMEM((6 * grid.cx * grid.cy, 2 * grid.cz), jnp.bfloat16),
        ],
        compiler_params=params,
        name="two_steps",
    )(*sources, own_strips, *arrived, strips, lanes, rows, force_site, force_wavelet)

    values = 6 * STEPS
    if capacity != 256:
        table = table.transpose(1, 0, 2).reshape(values, width, capacity).transpose(1, 0, 2)
    sent = lax.all_to_all(table, ("gx", "gy"), split_axis=0, concat_axis=0, tiled=True)
    return velocity, sent.transpose(1, 0, 2).reshape(1, values, slots)


def solution(mesh):
    in_specs = (
        P(None, ("runs", "gx"), "gy", "gz"),
        P(None, ("runs", "gx"), "gy", "gz"),
        P(None, ("runs", "gx"), "gy", "gz"),
        P("runs"),
        P("runs", None),
        P(("runs", "gx"), "gy", "gz", None),
        P(("runs", "gx"), "gy", "gz", None, None),
    )
    out_specs = (P(None, ("runs", "gx"), "gy", "gz"), P(("runs", "gz"), None, ("gx", "gy")))
    return jax.shard_map(
        per_device, mesh=mesh, in_specs=in_specs, out_specs=out_specs, check_vma=False
    )
```

```python
import functools

import jax
import jax.numpy as jnp
from jax import lax
from jax.experimental import pallas as pl
from jax.experimental.pallas import tpu as pltpu
from jax.sharding import PartitionSpec as P

STEPS = 2
TIME_STEP = 0.12

SXX, SYY, SZZ, SXY, SXZ, SYZ, VX, VY, VZ, LAM, MU, BUOY = range(12)
FIELDS = 12
DEPTHS = (6, 5, 5, 6, 6, 5, 5, 5, 5, 3, 3, 5)
OFFSETS = tuple(sum(DEPTHS[:f]) for f in range(FIELDS + 1))
HALO = 6
LAYERS = OFFSETS[-1]
ROWS = 8
STRIP = 8
LANES = 128
CORNER_WHOLE = tuple((f, d) for f in (SXX, SYY, SXY, SXZ, SYZ) for d in (1, 2))
CORNER_HALF = (
    tuple((f, d) for f in (SXX, SYY, SXY, SXZ, SYZ) for d in (3, 4, 5))
    + tuple((f, d) for f in (SZZ, VX, VY, VZ, BUOY) for d in (1, 2, 3))
    + tuple((f, d) for f in (LAM, MU) for d in (1, 2))
)
CORNERS = len(CORNER_WHOLE) + (len(CORNER_HALF) + 1) // 2
VMEM_LIMIT = 40 * 1024 * 1024
UNROLL = 8
SAMPLE_UNROLL = 4
PART = 4
VMEM = pl.BlockSpec(memory_space=pltpu.VMEM)
HBM = pl.BlockSpec(memory_space=pltpu.HBM)


def f32(*shape):
    return jax.ShapeDtypeStruct(shape, jnp.float32)


def groups(count):
    return -(-count // (LANES // STRIP))


def iota(dimension, shape=(ROWS, LANES)):
    return lax.broadcasted_iota(jnp.int32, shape, dimension)


def pack_strips(tiles, head):
    slot = iota(1) // STRIP
    packed = None
    for at, tile in enumerate(tiles):
        turned = pltpu.roll(tile, (STRIP * at + head) & (LANES - 1), 1)
        packed = turned if packed is None else jnp.where(slot == at, turned, packed)
    return packed


class Grid:
    def __init__(self, block, counts):
        self.cx, self.cy, self.cz = block
        self.gx, self.gy, self.gz = counts
        self.x_pairs = ("even", "odd") if self.gx > 2 else ("even",)
        self.y_pairs = ("even", "odd") if self.gy > 2 else ("even",)
        self.rows = self.cy + ROWS * len(self.y_pairs)
        self.layers = self.cx + 2 * HALO
        self.tiles_y = self.cy // ROWS

    def pairs(self, count, kind):
        start = 0 if kind == "even" else 1
        out = []
        for i in range(start, count - 1, 2):
            out += [(i, i + 1), (i + 1, i)]
        return out

    def pieces(self):
        out = [(("x", a), LAYERS * self.tiles_y) for a in self.x_pairs]
        out += [(("y", b), FIELDS * self.cx) for b in self.y_pairs]
        out += [(("d", a, b), CORNERS) for b in self.y_pairs for a in self.x_pairs]
        return out

    def shape(self, name):
        if name[0] == "x":
            return (LAYERS, self.cy, self.cz)
        if name[0] == "y":
            return (FIELDS, self.cx, ROWS, self.cz)
        return (CORNERS, ROWS, self.cz)


def above(axis, kind):
    parity = lax.rem(lax.axis_index(axis), 2)
    return parity == (0 if kind == "even" else 1)


def pack_kernel(grid, *refs):
    fields = refs[0]
    outs = refs[1:]
    own = outs[-1]
    sub = iota(0)
    for (name, _), out in zip(grid.pieces(), outs):
        if name[0] == "x":
            high = above("gx", name[1])
            for f in range(FIELDS):
                n = DEPTHS[f]
                start = jnp.where(high, grid.cx - n, 0)
                out[OFFSETS[f] : OFFSETS[f + 1]] = fields[f, pl.ds(start, n)]
        elif name[0] == "y":
            row = pl.multiple_of(jnp.where(above("gy", name[1]), grid.cy - ROWS, 0), ROWS)
            for f in range(FIELDS):
                out[f] = fields[f, :, pl.ds(row, ROWS), :]
        else:
            high = above("gx", name[1])
            up = above("gy", name[2])
            row = pl.multiple_of(jnp.where(up, grid.cy - ROWS, 0), ROWS)

            def tile(field, distance):
                layer = jnp.where(high, grid.cx - distance, distance - 1)
                return fields[field, layer, pl.ds(row, ROWS), :]

            for i, (f, d) in enumerate(CORNER_WHOLE):
                out[i] = tile(f, d)
            for i in range(0, len(CORNER_HALF), 2):
                first = tile(*CORNER_HALF[i])
                second = tile(*CORNER_HALF[min(i + 1, len(CORNER_HALF) - 1)])
                turned = pltpu.roll(jnp.where(up, first, second), 4, 0)
                lower = jnp.where(up, turned, first)
                upper = jnp.where(up, second, turned)
                out[len(CORNER_WHOLE) + i // 2] = jnp.where(sub < 4, lower, upper)
    head = jnp.where(lax.axis_index("gz") == 0, STRIP, 0)
    tiles = [(f, x, r) for f in range(FIELDS) for x in range(grid.cx) for r in range(grid.tiles_y)]
    for g in range(groups(len(tiles))):
        part = []
        for f, x, r in tiles[16 * g : 16 * g + 16]:
            part.append(fields[f, x, ROWS * r : ROWS * r + ROWS, :])
        own[g] = pack_strips(part, head)


def piece_tile(name, ref, at, grid):
    if name[0] == "x":
        r = at % grid.tiles_y
        return ref[at // grid.tiles_y, ROWS * r : ROWS * r + ROWS, :]
    if name[0] == "y":
        return ref[at // grid.cx, at % grid.cx]
    return ref[at]


def strip_kernel(grid, *refs):
    out = refs[-1]
    head = jnp.where(lax.axis_index("gz") == 0, STRIP, 0)
    base = 0
    for (name, count), ref in zip(grid.pieces(), refs[:-1]):
        for g in range(groups(count)):
            tiles = [
                piece_tile(name, ref, at, grid) for at in range(16 * g, min(16 * g + 16, count))
            ]
            out[base + g] = pack_strips(tiles, head)
        base += groups(count)


def slot_kernel(width, capacity, cz, cells_ref, writers_ref, lanes_ref, rows_ref):
    count = cells_ref.shape[1]
    cells = cells_ref[...]
    writers = writers_ref[...]
    padded = max(16, width)
    named = (iota(0, (padded, count)) == writers).astype(jnp.float32)
    earlier = (iota(0, (count, count)) < iota(1, (count, count))).astype(jnp.float32)
    before = jnp.dot(
        named.astype(jnp.bfloat16), earlier.astype(jnp.bfloat16), preferred_element_type=jnp.float32
    )
    position = jnp.sum(before * named, axis=0, keepdims=True).astype(jnp.int32)
    target = writers * capacity + position
    which = iota(0, (16, count))
    lane = lax.rem(cells, cz)
    row = lax.div(cells, cz)
    values = jnp.where(which == 0, lane, jnp.where(which == 1, row, jnp.where(which == 2, 1, 0)))
    values = values.astype(jnp.float32).astype(jnp.bfloat16)
    step = 256
    for n in range(width * capacity // step):
        hit = (iota(0, (step, count)) + n * step == target).astype(jnp.float32)
        table = lax.dot_general(
            values,
            hit.astype(jnp.bfloat16),
            (((1,), (1,)), ((), ())),
            preferred_element_type=jnp.float32,
        )
        lane_of = jnp.where(table[2:3] > 0.5, table[0:1], -1.0).astype(jnp.int32)
        marks = (iota(0, (cz, step)) == lane_of).astype(jnp.float32).astype(jnp.bfloat16)
        lanes_ref[0:cz, n * step : (n + 1) * step] = marks
        lanes_ref[cz : 2 * cz, n * step : (n + 1) * step] = marks
        rows_ref[:, n * step : (n + 1) * step] = jnp.broadcast_to(
            table[1:2].astype(jnp.int32), (ROWS, step)
        )


def edge(grid, up):
    if len(grid.y_pairs) > 1:
        return lambda tile: tile
    sub = iota(0)
    keep = jnp.logical_or(sub < jnp.where(up, 6, 0), sub >= jnp.where(up, 8, 2))
    return lambda tile: jnp.where(keep, tile, 0.0)


def halo_row(grid, up):
    if len(grid.y_pairs) == 1:
        return grid.cy
    return pl.multiple_of(jnp.where(up, grid.cy, grid.cy + ROWS), ROWS)


def lay_own(grid, ext, own):
    cx, cy = grid.cx, grid.cy
    for f in range(FIELDS):
        for x in list(range(HALO)) + list(range(HALO + cx, grid.layers)):
            for row in range(cy, grid.rows, ROWS):
                ext[f, x, row : row + ROWS, :] = jnp.zeros((ROWS, grid.cz), jnp.float32)
    at = 0
    for f in range(FIELDS):
        for x in range(cx):
            for r in range(grid.tiles_y):
                ext[f, HALO + x, ROWS * r : ROWS * r + ROWS, :] = own(at)
                at += 1


def lay_halos(grid, ext, arrived):
    cx, cy = grid.cx, grid.cy
    for (name, count), tile_of in zip(grid.pieces(), arrived):
        if name[0] == "x":
            high = above("gx", name[1])
            at = 0
            for f in range(FIELDS):
                start = jnp.where(high, HALO + cx, HALO - DEPTHS[f])
                for d in range(DEPTHS[f]):
                    for r in range(grid.tiles_y):
                        ext[f, start + d, ROWS * r : ROWS * r + ROWS, :] = tile_of(at)
                        at += 1
            continue
        up = above("gy", name[-1])
        clear = edge(grid, up)
        place = halo_row(grid, up)
        if name[0] == "y":
            for f in range(FIELDS):
                for x in range(cx):
                    ext[f, HALO + x, pl.ds(place, ROWS), :] = clear(tile_of(f * cx + x))
            continue
        high = above("gx", name[1])

        def put(field, distance, tile):
            layer = jnp.where(high, HALO + cx - 1 + distance, HALO - distance)
            ext[field, layer, pl.ds(place, ROWS), :] = clear(tile)

        for i, (f, d) in enumerate(CORNER_WHOLE):
            put(f, d, tile_of(i))
        for i in range(0, len(CORNER_HALF), 2):
            tile = tile_of(len(CORNER_WHOLE) + i // 2)
            turned = pltpu.roll(tile, 4, 0)
            put(*CORNER_HALF[i], jnp.where(up, tile, turned))
            if i + 1 < len(CORNER_HALF):
                put(*CORNER_HALF[i + 1], jnp.where(up, turned, tile))


def known_lanes():
    lead = jnp.where(lax.axis_index("gz") == 0, 0, LANES - STRIP)
    lane = iota(1)
    return lead, jnp.logical_and(lane >= lead, lane < lead + STRIP)


def unpack(ref, base, at):
    lead, known = known_lanes()
    turned = pltpu.roll(ref[base + at // 16], (lead - STRIP * (at % 16)) & (LANES - 1), 1)
    return jnp.where(known, turned, 0.0)


def begin_kernel(grid, *refs):
    fields, own_strips, ext, beside = refs

    def own(at):
        x, r = at // grid.tiles_y % grid.cx, at % grid.tiles_y
        return fields[at // (grid.tiles_y * grid.cx), x, ROWS * r : ROWS * r + ROWS, :]

    lay_own(grid, ext, own)
    lay_own(grid, beside, functools.partial(unpack, own_strips, 0))


def assemble_kernel(grid, *refs):
    arrived, ext = refs[1:-1], refs[-1]
    tiles = [
        functools.partial(piece_tile, name, ref, grid=grid)
        for (name, _), ref in zip(grid.pieces(), arrived)
    ]
    lay_halos(grid, ext, tiles)


def main_kernel(grid, *refs):
    strips, lanes_ref, rows_ref, site_hbm, wavelet_hbm = refs[2:7]
    ext, beside, velocity_out, table_out = refs[7:11]
    sampled, site_ref, wavelet_ref, sems = refs[11:]
    copies = (
        pltpu.make_async_copy(site_hbm, site_ref, sems.at[0]),
        pltpu.make_async_copy(wavelet_hbm, wavelet_ref, sems.at[1]),
    )
    for copy in copies:
        copy.start()
    rows = grid.rows
    cx, cy, cz = grid.cx, grid.cy, grid.cz
    half = lax.axis_index("gz")
    sub = iota(0)
    lane = iota(1)
    bases = [0]
    for _, count in grid.pieces():
        bases.append(bases[-1] + groups(count))
    lay_halos(grid, beside, [functools.partial(unpack, strips, base) for base in bases[:-1]])
    lane_all = iota(1, (rows, cz))

    def pair(field, x):
        return ext[field, x], beside[field, x]

    def add(a, b):
        return a[0] + b[0], a[1] + b[1]

    def sub_(a, b):
        return a[0] - b[0], a[1] - b[1]

    def along_x(field, x):
        return (
            sub_(pair(field, x + 1), pair(field, x)),
            sub_(pair(field, x + 2), pair(field, x - 1)),
        )

    def moved_y(a, offset):
        return tuple(pltpu.roll(v, -offset % rows, 0) for v in a)

    def moved_z(a, offset):
        own = pltpu.roll(a[0], -offset % cz, 1)
        far = pltpu.roll(a[1], -offset % cz, 1)
        inside = lane_all < cz - offset if offset > 0 else lane_all >= -offset
        return jnp.where(inside, own, far), jnp.where(inside, far, own)

    def forward(a, move):
        return sub_(move(a, 1), a), sub_(move(a, 2), move(a, -1))

    def backward(a, move):
        return sub_(a, move(a, -1)), sub_(move(a, 1), move(a, -2))

    def total(*terms):
        near, far = terms[0]
        for other_near, other_far in terms[1:]:
            near, far = add(near, other_near), add(far, other_far)
        return tuple(27.0 * p - q for p, q in zip(near, far))

    scale = TIME_STEP / 24.0

    def velocity_layer(x):
        y = x + 1
        sxy_x, sxz_x = pair(SXY, x), pair(SXZ, x)
        rate_x = total(along_x(SXX, x), backward(sxy_x, moved_y), backward(sxz_x, moved_z))
        syz = pair(SYZ, y)
        rate_y = total(
            along_x(SXY, y - 1), forward(pair(SYY, y), moved_y), backward(syz, moved_z)
        )
        rate_z = total(
            along_x(SXZ, y - 1), backward(syz, moved_y), forward(pair(SZZ, y), moved_z)
        )
        for h, block in enumerate((ext, beside)):
            b = scale * block[BUOY, x]
            block[VX, x] = block[VX, x] + b * rate_x[h]
            b = scale * block[BUOY, y]
            block[VY, y] = block[VY, y] + b * rate_y[h]
            block[VZ, y] = block[VZ, y] + b * rate_z[h]

    def stress_layer(x):
        vx, vy, vz = pair(VX, x), pair(VY, x), pair(VZ, x)
        gxx = total(along_x(VX, x - 1))
        gyy = total(backward(vy, moved_y))
        gzz = total(backward(vz, moved_z))
        gxy = total(forward(vx, moved_y), along_x(VY, x))
        gxz = total(forward(vx, moved_z), along_x(VZ, x))
        gyz = total(forward(vy, moved_z), forward(vz, moved_y))
        for h, block in enumerate((ext, beside)):
            shear = scale * block[MU, x]
            volume = scale * block[LAM, x] * (gxx[h] + gyy[h] + gzz[h])
            twice = 2.0 * shear
            block[SXX, x] = block[SXX, x] + (twice * gxx[h] + volume)
            block[SYY, x] = block[SYY, x] + (twice * gyy[h] + volume)
            block[SZZ, x] = block[SZZ, x] + (twice * gzz[h] + volume)
            block[SXY, x] = block[SXY, x] + shear * gxy[h]
            block[SXZ, x] = block[SXZ, x] + shear * gxz[h]
            block[SYZ, x] = block[SYZ, x] + shear * gyz[h]

    def loop(first, last, body, unroll=UNROLL):
        def step(x, carry):
            body(x)
            return carry

        lax.fori_loop(HALO + first, HALO + last + 1, step, 0, unroll=unroll)

    loop(-5, cx + 3, velocity_layer)
    for copy in copies:
        copy.wait()
    site = site_ref[0]
    total_y, total_z = cy * grid.gy, cz * grid.gz
    site_x = lax.div(site, total_y * total_z) - lax.axis_index("gx") * cx
    site_y = lax.rem(lax.div(site, total_z), total_y) - lax.axis_index("gy") * cy
    site_z = lax.rem(site, total_z)
    near = jnp.logical_and(site_x >= -HALO, site_x < cx + HALO)
    near = jnp.logical_and(near, jnp.logical_and(site_y >= -ROWS, site_y < cy + ROWS))
    site_row = jnp.where(site_y < 0, site_y + rows, site_y)

    def inject(step):
        x = site_x + HALO
        row = pl.multiple_of(lax.div(site_row, ROWS) * ROWS, ROWS)
        here = jnp.logical_and(sub == lax.rem(site_row, ROWS), lane == lax.rem(site_z, cz))
        own = lax.div(site_z, cz) == half
        for mine, block in ((True, ext), (False, beside)):

            @pl.when(jnp.logical_and(near, own if mine else jnp.logical_not(own)))
            def _():
                amount = jnp.where(here, TIME_STEP * block[BUOY, x, pl.ds(row, ROWS), :], 0.0)
                for c in range(3):
                    block[VX + c, x, pl.ds(row, ROWS), :] = (
                        block[VX + c, x, pl.ds(row, ROWS), :] + amount * wavelet_ref[step, c]
                    )

    def strain_layer(step, x):
        lam = ext[LAM, x, 0:cy, :]
        shear = ext[MU, x, 0:cy, :]
        parts = [ext[f, x, 0:cy, :] for f in range(6)]
        shrink = lam / (3.0 * lam + 2.0 * shear) * (parts[0] + parts[1] + parts[2])
        inverse = 0.5 / shear
        for f in range(6):
            value = (parts[f] - shrink if f < 3 else parts[f]) * inverse
            head = value.astype(jnp.bfloat16)
            tail = (value - head.astype(jnp.float32)).astype(jnp.bfloat16)
            row = pl.multiple_of((6 * step + f) * cx * cy + (x - HALO) * cy, cy)
            sampled[pl.ds(row, cy), 0:cz] = head
            sampled[pl.ds(row, cy), cz : 2 * cz] = tail

    step_slots = 256
    block = cx * cy

    def sample(k, carry):
        where = pl.ds(pl.multiple_of(k * step_slots, step_slots), step_slots)
        row = rows_ref[:, where]
        marks = [row == r * ROWS + iota(0, (ROWS, step_slots)) for r in range(block // ROWS)]
        for part in range(6 * STEPS // PART):
            found = jnp.dot(
                sampled[part * PART * block : (part + 1) * PART * block, :],
                lanes_ref[:, where],
                preferred_element_type=jnp.float32,
            )
            for f in range(PART):
                acc = jnp.zeros((ROWS, step_slots), jnp.float32)
                for r in range(block // ROWS):
                    tile = found[f * block + r * ROWS : f * block + r * ROWS + ROWS]
                    acc = acc + jnp.where(marks[r], tile, 0.0)
                to = part * PART + f
                table_out[k, to : to + 1, :] = jnp.sum(acc, axis=0, keepdims=True)
        return carry

    inject(0)
    loop(-3, cx + 2, stress_layer)
    loop(0, cx - 1, functools.partial(strain_layer, 0))
    loop(-2, cx, velocity_layer)
    inject(1)
    leaving = pltpu.make_async_copy(
        ext.at[VX : VX + 3, HALO : HALO + cx, 0:cy, :], velocity_out, sems.at[2]
    )
    leaving.start()
    loop(0, cx - 1, stress_layer)
    loop(0, cx - 1, functools.partial(strain_layer, 1))
    lax.fori_loop(0, lanes_ref.shape[1] // step_slots, sample, 0, unroll=SAMPLE_UNROLL)
    leaving.wait()


def per_device(
    velocity_start, stress_start, material, force_site, force_wavelet, save_cells, save_writer
):
    counts = tuple(lax.axis_size(axis) for axis in ("gx", "gy", "gz"))
    grid = Grid(velocity_start.shape[1:], counts)
    pieces = grid.pieces()
    params = pltpu.CompilerParams(vmem_limit_bytes=VMEM_LIMIT)
    own_tiles = FIELDS * grid.cx * grid.tiles_y
    fields = sum(
        lax.pad(part, jnp.float32(0.0), [(first, FIELDS - first - part.shape[0], 0)] + [(0, 0, 0)] * 3)
        for first, part in ((SXX, stress_start), (VX, velocity_start), (LAM, material))
    )
    packed = pl.pallas_call(
        lambda *refs: pack_kernel(grid, *refs),
        out_shape=[f32(*grid.shape(name)) for name, _ in pieces]
        + [f32(groups(own_tiles), ROWS, LANES)],
        in_specs=[VMEM],
        out_specs=[VMEM] * (len(pieces) + 1),
        compiler_params=params,
        name="pack_halos",
    )(fields)
    swap = [(0, 1), (1, 0)]
    arrived = []
    for (name, _), piece in zip(pieces, packed):
        if name[0] == "x":
            arrived.append(lax.ppermute(piece, "gx", grid.pairs(grid.gx, name[1])))
        elif name[0] == "y":
            arrived.append(lax.ppermute(piece, "gy", grid.pairs(grid.gy, name[1])))
        else:
            pairs = [
                (a * grid.gy + b, c * grid.gy + d)
                for a, c in grid.pairs(grid.gx, name[1])
                for b, d in grid.pairs(grid.gy, name[2])
            ]
            arrived.append(lax.ppermute(piece, ("gx", "gy"), pairs))
    own_strips = lax.ppermute(packed[-1], "gz", swap)

    count = save_cells.size
    width = grid.gx * grid.gy
    capacity = max(2, 2 * count // width)
    slots = width * capacity
    lanes, rows = pl.pallas_call(
        lambda *refs: slot_kernel(width, capacity, grid.cz, *refs),
        out_shape=[
            jax.ShapeDtypeStruct((2 * grid.cz, slots), jnp.bfloat16),
            jax.ShapeDtypeStruct((ROWS, slots), jnp.int32),
        ],
        in_specs=[VMEM] * 2,
        out_specs=[VMEM] * 2,
        compiler_params=params,
        name="slot_tables",
    )(save_cells.reshape(1, count), save_writer.reshape(1, count))

    extended = f32(FIELDS, grid.layers, grid.rows, grid.cz)
    block, beside = pl.pallas_call(
        lambda *refs: begin_kernel(grid, *refs),
        out_shape=[extended] * 2,
        in_specs=[VMEM] * 2,
        out_specs=[VMEM] * 2,
        compiler_params=params,
        name="begin_block",
    )(fields, own_strips)

    strips = pl.pallas_call(
        lambda *refs: strip_kernel(grid, *refs[3:]),
        out_shape=f32(sum(groups(c) for _, c in pieces), ROWS, LANES),
        in_specs=[VMEM] * (len(pieces) + 3),
        out_specs=VMEM,
        compiler_params=params,
        name="pack_strips",
    )(rows, block, beside, *arrived)
    strips = lax.ppermute(strips, "gz", swap)

    block = pl.pallas_call(
        lambda *refs: assemble_kernel(grid, *refs),
        out_shape=extended,
        in_specs=[VMEM] * (1 + len(pieces)),
        out_specs=VMEM,
        input_output_aliases={0: 0},
        compiler_params=params,
        name="assemble",
    )(block, *arrived)

    _, _, velocity, table = pl.pallas_call(
        lambda *refs: main_kernel(grid, *refs),
        out_shape=[
            extended,
            extended,
            f32(*velocity_start.shape),
            f32(slots // 256, 6 * STEPS, 256),
        ],
        in_specs=[VMEM] * 5 + [HBM] * 2,
        out_specs=[VMEM, VMEM, HBM, VMEM],
        scratch_shapes=[
            pltpu.VMEM((STEPS * 6 * grid.cx * grid.cy, 2 * grid.cz), jnp.bfloat16),
            pltpu.SMEM(force_site.shape, jnp.int32),
            pltpu.SMEM(force_wavelet.shape, jnp.float32),
            pltpu.SemaphoreType.DMA((3,)),
        ],
        input_output_aliases={0: 0, 1: 1},
        compiler_params=params,
        name="two_steps",
    )(block, beside, strips, lanes, rows, force_site, force_wavelet)

    values = 6 * STEPS
    if capacity != 256:
        table = table.transpose(1, 0, 2).reshape(values, width, capacity).transpose(1, 0, 2)
    sent = lax.all_to_all(table, ("gx", "gy"), split_axis=0, concat_axis=0, tiled=True)
    return velocity, sent.transpose(1, 0, 2).reshape(1, values, slots)


def solution(mesh):
    in_specs = (
        P(None, ("runs", "gx"), "gy", "gz"),
        P(None, ("runs", "gx"), "gy", "gz"),
        P(None, ("runs", "gx"), "gy", "gz"),
        P("runs"),
        P("runs", None),
        P(("runs", "gx"), "gy", "gz", None),
        P(("runs", "gx"), "gy", "gz", None, None),
    )
    out_specs = (P(None, ("runs", "gx"), "gy", "gz"), P(("runs", "gz"), None, ("gx", "gy")))
    return jax.shard_map(
        per_device, mesh=mesh, in_specs=in_specs, out_specs=out_specs, check_vma=False
    )
```

```python
import functools

import jax
import jax.numpy as jnp
from jax import lax
from jax.experimental import pallas as pl
from jax.experimental.pallas import tpu as pltpu
from jax.sharding import PartitionSpec as P

STEPS = 2
TIME_STEP = 0.12

SXX, SYY, SZZ, SXY, SXZ, SYZ, VX, VY, VZ, LAM, MU, BUOY = range(12)
FIELDS = 12
DEPTHS = (6, 5, 5, 6, 6, 5, 5, 5, 5, 3, 3, 5)
OFFSETS = tuple(sum(DEPTHS[:f]) for f in range(FIELDS + 1))
HALO = 6
LAYERS = OFFSETS[-1]
ROWS = 8
STRIP = 8
LANES = 128
CORNER_ROWS = {f: (5, 5, 3, 2, 2) for f in (SXX, SYY, SXY, SXZ, SYZ)}
CORNER_ROWS.update({f: (3, 3, 2) for f in (SZZ, VX, VY, VZ, BUOY)})
CORNER_ROWS.update({f: (2, 2) for f in (LAM, MU)})


def corner_tiles():
    parts = [(n, f, d + 1) for f, counts in CORNER_ROWS.items() for d, n in enumerate(counts)]
    tiles = []
    for n, f, d in sorted(parts, reverse=True):
        for tile in tiles:
            used = sum(part[2] for part in tile)
            if used + n <= ROWS:
                tile.append((f, d, n, used))
                break
        else:
            tiles.append([(f, d, n, 0)])
    return tiles


CORNER_TILES = corner_tiles()
CORNERS = len(CORNER_TILES)
SLOT_STEP = 256
VMEM_LIMIT = 40 * 1024 * 1024
UNROLL = 8
SAMPLE_UNROLL = 4
PART = 6
VMEM = pl.BlockSpec(memory_space=pltpu.VMEM)
HBM = pl.BlockSpec(memory_space=pltpu.HBM)
IDLE = pl.CostEstimate(flops=0, bytes_accessed=0, transcendentals=0)


def f32(*shape):
    return jax.ShapeDtypeStruct(shape, jnp.float32)


def groups(count):
    return -(-count // (LANES // STRIP))


def iota(dimension, shape=(ROWS, LANES)):
    return lax.broadcasted_iota(jnp.int32, shape, dimension)


def pack_strips(tiles, head):
    slot = iota(1) // STRIP
    packed = None
    for at, tile in enumerate(tiles):
        turned = pltpu.roll(tile, (STRIP * at + head) & (LANES - 1), 1)
        packed = turned if packed is None else jnp.where(slot == at, turned, packed)
    return packed


class Grid:
    def __init__(self, block, counts):
        self.cx, self.cy, self.cz = block
        self.gx, self.gy, self.gz = counts
        self.x_pairs = ("odd", "even") if self.gx > 2 else ("even",)
        self.y_pairs = ("even", "odd") if self.gy > 2 else ("even",)
        self.rows = self.cy + ROWS * len(self.y_pairs)
        self.layers = self.cx + 2 * HALO
        self.tiles_y = self.cy // ROWS

    def pairs(self, count, kind):
        start = 0 if kind == "even" else 1
        out = []
        for i in range(start, count - 1, 2):
            out += [(i, i + 1), (i + 1, i)]
        return out

    def pieces(self):
        out = [(("y", b), FIELDS * self.cx) for b in self.y_pairs]
        out += [(("x", a), LAYERS * self.tiles_y) for a in self.x_pairs]
        out += [(("d", a, b), CORNERS) for b in self.y_pairs for a in self.x_pairs]
        return out

    def shape(self, name):
        if name[0] == "x":
            return (LAYERS, self.cy, self.cz)
        if name[0] == "y":
            return (FIELDS, self.cx, ROWS, self.cz)
        return (CORNERS, ROWS, self.cz)


def above(axis, kind):
    parity = lax.rem(lax.axis_index(axis), 2)
    return parity == (0 if kind == "even" else 1)


def pack_kernel(grid, *refs):
    fields = refs[0]
    outs = refs[1:]
    sub = iota(0)
    for (name, _), out in zip(grid.pieces(), outs):
        if name[0] == "x":
            high = above("gx", name[1])
            for f in range(FIELDS):
                n = DEPTHS[f]
                start = jnp.where(high, grid.cx - n, 0)
                out[OFFSETS[f] : OFFSETS[f + 1]] = fields[f, pl.ds(start, n)]
        elif name[0] == "y":
            row = pl.multiple_of(jnp.where(above("gy", name[1]), grid.cy - ROWS, 0), ROWS)
            for f in range(FIELDS):
                out[f] = fields[f, :, pl.ds(row, ROWS), :]
        else:
            high = above("gx", name[1])
            up = above("gy", name[2])
            row = pl.multiple_of(jnp.where(up, grid.cy - ROWS, 0), ROWS)

            def tile(field, distance):
                layer = jnp.where(high, grid.cx - distance, distance - 1)
                return fields[field, layer, pl.ds(row, ROWS), :]

            for i, parts in enumerate(CORNER_TILES):
                packed = None
                for f, d, n, first in parts:
                    whole = tile(f, d)
                    turned = jnp.where(
                        up,
                        pltpu.roll(whole, (first + n) % ROWS, 0),
                        pltpu.roll(whole, first, 0) if first else whole,
                    )
                    packed = turned if packed is None else jnp.where(sub < first, packed, turned)
                out[i] = packed


def own_strip_kernel(grid, after, fields, own):
    head = jnp.where(lax.axis_index("gz") == 0, STRIP, 0)
    tiles = [(f, x, r) for f in range(FIELDS) for x in range(grid.cx) for r in range(grid.tiles_y)]
    for g in range(groups(len(tiles))):
        part = []
        for f, x, r in tiles[16 * g : 16 * g + 16]:
            part.append(fields[f, x, ROWS * r : ROWS * r + ROWS, :])
        own[g] = pack_strips(part, head)


def piece_tile(name, ref, at, grid):
    if name[0] == "x":
        r = at % grid.tiles_y
        return ref[at // grid.tiles_y, ROWS * r : ROWS * r + ROWS, :]
    if name[0] == "y":
        return ref[at // grid.cx, at % grid.cx]
    return ref[at]


def strip_kernel(grid, *refs):
    out = refs[-1]
    head = jnp.where(lax.axis_index("gz") == 0, STRIP, 0)
    base = 0
    for (name, count), ref in zip(grid.pieces(), refs[:-1]):
        for g in range(groups(count)):
            tiles = [
                piece_tile(name, ref, at, grid) for at in range(16 * g, min(16 * g + 16, count))
            ]
            out[base + g] = pack_strips(tiles, head)
        base += groups(count)


def slot_kernel(width, cz, cells_ref, writers_ref, lanes_ref, rows_ref, spans_ref):
    count = cells_ref.shape[1]
    cells = cells_ref[...]
    writers = writers_ref[...]
    padded = max(LANES, width)
    writer = iota(0, (padded, count))
    named = (writer == writers).astype(jnp.float32)
    fewer = (writers < writer).astype(jnp.float32)
    earlier = (iota(0, (count, count)) < iota(1, (count, count))).astype(jnp.float32)
    before = jnp.dot(
        named.astype(jnp.bfloat16), earlier.astype(jnp.bfloat16), preferred_element_type=jnp.float32
    )
    start = jnp.sum(fewer, axis=1, keepdims=True)
    rank = jnp.sum((before + start) * named, axis=0, keepdims=True).astype(jnp.int32)
    ones = jnp.ones((16, count), jnp.bfloat16)

    def across(marks):
        return lax.dot_general(
            ones,
            marks.astype(jnp.bfloat16),
            (((1,), (1,)), ((), ())),
            preferred_element_type=jnp.float32,
        ).astype(jnp.int32)

    spans_ref[0:ROWS, :] = across(fewer)[0:ROWS]
    spans_ref[ROWS : 2 * ROWS, :] = across(named)[0:ROWS]
    which = iota(0, (16, count))
    values = jnp.where(which == 0, lax.rem(cells, cz), jnp.where(which == 1, lax.div(cells, cz), 0))
    values = values.astype(jnp.float32).astype(jnp.bfloat16)
    for n in range(0, count, SLOT_STEP):
        hit = (iota(0, (SLOT_STEP, count)) + n == rank).astype(jnp.float32)
        table = lax.dot_general(
            values,
            hit.astype(jnp.bfloat16),
            (((1,), (1,)), ((), ())),
            preferred_element_type=jnp.float32,
        ).astype(jnp.int32)
        marks = (iota(0, (cz, SLOT_STEP)) == table[0:1]).astype(jnp.float32).astype(jnp.bfloat16)
        lanes_ref[0:cz, n : n + SLOT_STEP] = marks
        lanes_ref[cz : 2 * cz, n : n + SLOT_STEP] = marks
        rows_ref[:, n : n + SLOT_STEP] = jnp.broadcast_to(table[1:2], (ROWS, SLOT_STEP))


def edge(grid, up):
    if len(grid.y_pairs) > 1:
        return lambda tile: tile
    sub = iota(0)
    keep = jnp.logical_or(sub < jnp.where(up, 6, 0), sub >= jnp.where(up, 8, 2))
    return lambda tile: jnp.where(keep, tile, 0.0)


def halo_row(grid, up):
    if len(grid.y_pairs) == 1:
        return grid.cy
    return pl.multiple_of(jnp.where(up, grid.cy, grid.cy + ROWS), ROWS)


def lay_own(grid, ext, own):
    cx, cy = grid.cx, grid.cy
    for f in range(FIELDS):
        for x in list(range(HALO)) + list(range(HALO + cx, grid.layers)):
            for row in range(cy, grid.rows, ROWS):
                ext[f, x, row : row + ROWS, :] = jnp.zeros((ROWS, grid.cz), jnp.float32)
    at = 0
    for f in range(FIELDS):
        for x in range(cx):
            for r in range(grid.tiles_y):
                ext[f, HALO + x, ROWS * r : ROWS * r + ROWS, :] = own(at)
                at += 1


def lay_halos(grid, ext, arrived):
    cx, cy = grid.cx, grid.cy
    for (name, count), tile_of in zip(grid.pieces(), arrived):
        if name[0] == "x":
            high = above("gx", name[1])
            at = 0
            for f in range(FIELDS):
                start = jnp.where(high, HALO + cx, HALO - DEPTHS[f])
                for d in range(DEPTHS[f]):
                    for r in range(grid.tiles_y):
                        ext[f, start + d, ROWS * r : ROWS * r + ROWS, :] = tile_of(at)
                        at += 1
            continue
        up = above("gy", name[-1])
        clear = edge(grid, up)
        place = halo_row(grid, up)
        if name[0] == "y":
            for f in range(FIELDS):
                for x in range(cx):
                    ext[f, HALO + x, pl.ds(place, ROWS), :] = clear(tile_of(f * cx + x))
            continue
        high = above("gx", name[1])

        def put(field, distance, tile):
            layer = jnp.where(high, HALO + cx - 1 + distance, HALO - distance)
            ext[field, layer, pl.ds(place, ROWS), :] = clear(tile)

        for i, parts in enumerate(CORNER_TILES):
            tile = tile_of(i)
            for f, d, n, first in parts:
                turned = jnp.where(
                    up,
                    pltpu.roll(tile, ROWS - first, 0) if first else tile,
                    pltpu.roll(tile, (-first - n) % ROWS, 0),
                )
                put(f, d, turned)


def known_lanes():
    lead = jnp.where(lax.axis_index("gz") == 0, 0, LANES - STRIP)
    lane = iota(1)
    return lead, jnp.logical_and(lane >= lead, lane < lead + STRIP)


def unpack(ref, base, at):
    lead, known = known_lanes()
    turned = pltpu.roll(ref[base + at // 16], (lead - STRIP * (at % 16)) & (LANES - 1), 1)
    return jnp.where(known, turned, 0.0)


def begin_kernel(grid, *refs):
    fields, own_strips, ext, beside = refs

    def own(at):
        x, r = at // grid.tiles_y % grid.cx, at % grid.tiles_y
        return fields[at // (grid.tiles_y * grid.cx), x, ROWS * r : ROWS * r + ROWS, :]

    lay_own(grid, ext, own)
    lay_own(grid, beside, functools.partial(unpack, own_strips, 0))


def assemble_kernel(grid, *refs):
    arrived, ext = refs[1:-1], refs[-1]
    tiles = [
        functools.partial(piece_tile, name, ref, grid=grid)
        for (name, _), ref in zip(grid.pieces(), arrived)
    ]
    lay_halos(grid, ext, tiles)


def main_kernel(grid, width, capacity, *refs):
    strips, lanes_ref, rows_ref, spans_vmem, site_hbm, wavelet_hbm = refs[2:8]
    ext, beside, velocity_out, table_out = refs[8:12]
    sampled, compact, site_ref, wavelet_ref, spans_ref, sems = refs[12:]
    copies = (
        pltpu.make_async_copy(site_hbm, site_ref, sems.at[0]),
        pltpu.make_async_copy(wavelet_hbm, wavelet_ref, sems.at[1]),
        pltpu.make_async_copy(spans_vmem, spans_ref, sems.at[2]),
    )
    for copy in copies:
        copy.start()
    rows = grid.rows
    cx, cy, cz = grid.cx, grid.cy, grid.cz
    half = lax.axis_index("gz")
    sub = iota(0)
    lane = iota(1)
    bases = [0]
    for _, count in grid.pieces():
        bases.append(bases[-1] + groups(count))
    lay_halos(grid, beside, [functools.partial(unpack, strips, base) for base in bases[:-1]])
    lane_all = iota(1, (rows, cz))

    def pair(field, x):
        return ext[field, x], beside[field, x]

    def add(a, b):
        return a[0] + b[0], a[1] + b[1]

    def sub_(a, b):
        return a[0] - b[0], a[1] - b[1]

    def along_x(field, x):
        return (
            sub_(pair(field, x + 1), pair(field, x)),
            sub_(pair(field, x + 2), pair(field, x - 1)),
        )

    def moved_y(a, offset):
        return tuple(pltpu.roll(v, -offset % rows, 0) for v in a)

    def moved_z(a, offset):
        own = pltpu.roll(a[0], -offset % cz, 1)
        far = pltpu.roll(a[1], -offset % cz, 1)
        inside = lane_all[: own.shape[0]]
        inside = inside < cz - offset if offset > 0 else inside >= -offset
        return jnp.where(inside, own, far), jnp.where(inside, far, own)

    def forward(a, move):
        return sub_(move(a, 1), a), sub_(move(a, 2), move(a, -1))

    def backward(a, move):
        return sub_(a, move(a, -1)), sub_(move(a, 1), move(a, -2))

    def total(*terms):
        near, far = terms[0]
        for other_near, other_far in terms[1:]:
            near, far = add(near, other_near), add(far, other_far)
        return tuple(27.0 * p - q for p, q in zip(near, far))

    scale = TIME_STEP / 24.0

    def velocity_layer(x):
        y = x + 1
        sxy_x, sxz_x = pair(SXY, x), pair(SXZ, x)
        rate_x = total(along_x(SXX, x), backward(sxy_x, moved_y), backward(sxz_x, moved_z))
        syz = pair(SYZ, y)
        rate_y = total(
            along_x(SXY, y - 1), forward(pair(SYY, y), moved_y), backward(syz, moved_z)
        )
        rate_z = total(
            along_x(SXZ, y - 1), backward(syz, moved_y), forward(pair(SZZ, y), moved_z)
        )
        for h, block in enumerate((ext, beside)):
            b = scale * block[BUOY, x]
            block[VX, x] = block[VX, x] + b * rate_x[h]
            b = scale * block[BUOY, y]
            block[VY, y] = block[VY, y] + b * rate_y[h]
            block[VZ, y] = block[VZ, y] + b * rate_z[h]

    def stress_layer(x, last=False):
        kept = cy if last else rows

        def cut(a):
            return tuple(v[:kept] for v in a)

        def across_y(move, a):
            return tuple(cut(v) for v in move(a, moved_y))

        def along(move, a):
            return move(cut(a), moved_z)

        def beyond(field, at):
            return tuple(cut(v) for v in along_x(field, at))

        vx, vy, vz = pair(VX, x), pair(VY, x), pair(VZ, x)
        gxx = total(beyond(VX, x - 1))
        gyy = total(across_y(backward, vy))
        gzz = total(along(backward, vz))
        gxy = total(across_y(forward, vx), beyond(VY, x))
        gxz = total(along(forward, vx), beyond(VZ, x))
        gyz = total(along(forward, vy), across_y(forward, vz))
        for h, block in enumerate((ext,) if last else (ext, beside)):
            shear = scale * block[MU, x, 0:kept]
            volume = scale * block[LAM, x, 0:kept] * (gxx[h] + gyy[h] + gzz[h])
            twice = 2.0 * shear
            for f, change in (
                (SXX, twice * gxx[h] + volume),
                (SYY, twice * gyy[h] + volume),
                (SZZ, twice * gzz[h] + volume),
                (SXY, shear * gxy[h]),
                (SXZ, shear * gxz[h]),
                (SYZ, shear * gyz[h]),
            ):
                block[f, x, 0:kept] = block[f, x, 0:kept] + change

    def loop(first, last, body, unroll=UNROLL):
        def step(x, carry):
            body(x)
            return carry

        lax.fori_loop(HALO + first, HALO + last + 1, step, 0, unroll=unroll)

    loop(-5, cx + 3, velocity_layer)
    for copy in copies:
        copy.wait()
    site = site_ref[0]
    total_y, total_z = cy * grid.gy, cz * grid.gz
    site_x = lax.div(site, total_y * total_z) - lax.axis_index("gx") * cx
    site_y = lax.rem(lax.div(site, total_z), total_y) - lax.axis_index("gy") * cy
    site_z = lax.rem(site, total_z)
    near = jnp.logical_and(site_x >= -HALO, site_x < cx + HALO)
    near = jnp.logical_and(near, jnp.logical_and(site_y >= -ROWS, site_y < cy + ROWS))
    site_row = jnp.where(site_y < 0, site_y + rows, site_y)

    def inject(step):
        x = site_x + HALO
        row = pl.multiple_of(lax.div(site_row, ROWS) * ROWS, ROWS)
        here = jnp.logical_and(sub == lax.rem(site_row, ROWS), lane == lax.rem(site_z, cz))
        own = lax.div(site_z, cz) == half
        for mine, block in ((True, ext), (False, beside)):

            @pl.when(jnp.logical_and(near, own if mine else jnp.logical_not(own)))
            def _():
                amount = jnp.where(here, TIME_STEP * block[BUOY, x, pl.ds(row, ROWS), :], 0.0)
                for c in range(3):
                    block[VX + c, x, pl.ds(row, ROWS), :] = (
                        block[VX + c, x, pl.ds(row, ROWS), :] + amount * wavelet_ref[step, c]
                    )

    def strain_layer(step, x):
        lam = ext[LAM, x, 0:cy, :]
        shear = ext[MU, x, 0:cy, :]
        parts = [ext[f, x, 0:cy, :] for f in range(6)]
        shrink = lam / (3.0 * lam + 2.0 * shear) * (parts[0] + parts[1] + parts[2])
        inverse = 0.5 / shear
        for f in range(6):
            value = (parts[f] - shrink if f < 3 else parts[f]) * inverse
            head = value.astype(jnp.bfloat16)
            tail = (value - head.astype(jnp.float32)).astype(jnp.bfloat16)
            row = pl.multiple_of((6 * step + f) * cx * cy + (x - HALO) * cy, cy)
            sampled[pl.ds(row, cy), 0:cz] = head
            sampled[pl.ds(row, cy), cz : 2 * cz] = tail

    block = cx * cy

    def sample(k, carry):
        where = pl.ds(pl.multiple_of(k * SLOT_STEP, SLOT_STEP), SLOT_STEP)
        to_lanes = pl.ds(pl.multiple_of(k * SLOT_STEP + LANES, LANES), SLOT_STEP)
        row = rows_ref[:, where]
        marks = [row == r * ROWS + iota(0, (ROWS, SLOT_STEP)) for r in range(block // ROWS)]
        for part in range(6 * STEPS // PART):
            found = jnp.dot(
                sampled[part * PART * block : (part + 1) * PART * block, :],
                lanes_ref[:, where],
                preferred_element_type=jnp.float32,
            )
            for f in range(PART):
                acc = jnp.zeros((ROWS, SLOT_STEP), jnp.float32)
                for r in range(block // ROWS):
                    tile = found[f * block + r * ROWS : f * block + r * ROWS + ROWS]
                    acc = acc + jnp.where(marks[r], tile, 0.0)
                to = part * PART + f
                compact[to : to + 1, to_lanes] = jnp.sum(acc, axis=0, keepdims=True)
        return carry

    def spread():
        values = 6 * STEPS
        lanes_at = iota(1, (values, LANES))
        for t in range(width * capacity // LANES):
            out = jnp.zeros((values, LANES), jnp.float32)
            for w in range(t * LANES // capacity, -(-(t + 1) * LANES // capacity)):
                skip = t * LANES - w * capacity
                start = spans_ref[0, w] + skip + LANES
                base = pl.multiple_of(lax.div(start, LANES) * LANES, LANES)
                shift = lax.rem(start, LANES)
                near = pltpu.roll(compact[0:values, pl.ds(base, LANES)], LANES - shift, 1)
                far = pltpu.roll(compact[0:values, pl.ds(base + LANES, LANES)], LANES - shift, 1)
                place = lanes_at + skip
                mine = jnp.logical_and(place >= 0, place < spans_ref[ROWS, w])
                out = jnp.where(mine, jnp.where(lanes_at < LANES - shift, near, far), out)
            per = 256 // LANES
            table_out[t // per, :, t % per * LANES : (t % per + 1) * LANES] = out

    inject(0)
    loop(-3, cx + 2, stress_layer)
    loop(0, cx - 1, functools.partial(strain_layer, 0))
    loop(-2, cx, velocity_layer)
    inject(1)
    leaving = pltpu.make_async_copy(
        ext.at[VX : VX + 3, HALO : HALO + cx, 0:cy, :], velocity_out, sems.at[3]
    )
    leaving.start()
    loop(0, cx - 1, functools.partial(stress_layer, last=True))
    loop(0, cx - 1, functools.partial(strain_layer, 1))
    lax.fori_loop(0, lanes_ref.shape[1] // SLOT_STEP, sample, 0, unroll=SAMPLE_UNROLL)
    spread()
    leaving.wait()


def per_device(
    velocity_start, stress_start, material, force_site, force_wavelet, save_cells, save_writer
):
    counts = tuple(lax.axis_size(axis) for axis in ("gx", "gy", "gz"))
    grid = Grid(velocity_start.shape[1:], counts)
    pieces = grid.pieces()
    params = pltpu.CompilerParams(vmem_limit_bytes=VMEM_LIMIT)
    own_tiles = FIELDS * grid.cx * grid.tiles_y
    fields = sum(
        lax.pad(part, jnp.float32(0.0), [(first, FIELDS - first - part.shape[0], 0)] + [(0, 0, 0)] * 3)
        for first, part in ((SXX, stress_start), (VX, velocity_start), (LAM, material))
    )
    packed = pl.pallas_call(
        lambda *refs: pack_kernel(grid, *refs),
        out_shape=[f32(*grid.shape(name)) for name, _ in pieces],
        in_specs=[VMEM],
        out_specs=[VMEM] * len(pieces),
        compiler_params=params,
        name="pack_halos",
    )(fields)
    swap = [(0, 1), (1, 0)]
    arrived = []
    for (name, _), piece in zip(pieces, packed):
        if name[0] == "x":
            arrived.append(lax.ppermute(piece, "gx", grid.pairs(grid.gx, name[1])))
        elif name[0] == "y":
            arrived.append(lax.ppermute(piece, "gy", grid.pairs(grid.gy, name[1])))
        else:
            pairs = [
                (a * grid.gy + b, c * grid.gy + d)
                for a, c in grid.pairs(grid.gx, name[1])
                for b, d in grid.pairs(grid.gy, name[2])
            ]
            arrived.append(lax.ppermute(piece, ("gx", "gy"), pairs))
    count = save_cells.size
    width = grid.gx * grid.gy
    capacity = max(2, 2 * count // width)
    slots = width * capacity
    lanes, rows, spans = pl.pallas_call(
        functools.partial(slot_kernel, width, grid.cz),
        out_shape=[
            jax.ShapeDtypeStruct((2 * grid.cz, count), jnp.bfloat16),
            jax.ShapeDtypeStruct((ROWS, count), jnp.int32),
            jax.ShapeDtypeStruct((2 * ROWS, max(LANES, width)), jnp.int32),
        ],
        in_specs=[VMEM] * 2,
        out_specs=[VMEM] * 3,
        compiler_params=params,
        cost_estimate=IDLE,
        name="slot_tables",
    )(save_cells.reshape(1, count), save_writer.reshape(1, count))

    own_strips = pl.pallas_call(
        functools.partial(own_strip_kernel, grid),
        out_shape=f32(groups(own_tiles), ROWS, LANES),
        in_specs=[VMEM] * 2,
        out_specs=VMEM,
        compiler_params=params,
        cost_estimate=IDLE,
        name="pack_own_strips",
    )(rows, fields)
    own_strips = lax.ppermute(own_strips, "gz", swap)

    extended = f32(FIELDS, grid.layers, grid.rows, grid.cz)
    block, beside = pl.pallas_call(
        lambda *refs: begin_kernel(grid, *refs),
        out_shape=[extended] * 2,
        in_specs=[VMEM] * 2,
        out_specs=[VMEM] * 2,
        compiler_params=params,
        cost_estimate=IDLE,
        name="begin_block",
    )(fields, own_strips)

    strips = pl.pallas_call(
        lambda *refs: strip_kernel(grid, *refs[3:]),
        out_shape=f32(sum(groups(c) for _, c in pieces), ROWS, LANES),
        in_specs=[VMEM] * (len(pieces) + 3),
        out_specs=VMEM,
        compiler_params=params,
        name="pack_strips",
    )(rows, block, beside, *arrived)
    strips = lax.ppermute(strips, "gz", swap)

    block = pl.pallas_call(
        lambda *refs: assemble_kernel(grid, *refs),
        out_shape=extended,
        in_specs=[VMEM] * (1 + len(pieces)),
        out_specs=VMEM,
        input_output_aliases={0: 0},
        compiler_params=params,
        name="assemble",
    )(block, *arrived)

    _, _, velocity, table = pl.pallas_call(
        functools.partial(main_kernel, grid, width, capacity),
        out_shape=[
            extended,
            extended,
            f32(*velocity_start.shape),
            f32(slots // 256, 6 * STEPS, 256),
        ],
        in_specs=[VMEM] * 6 + [HBM] * 2,
        out_specs=[VMEM, VMEM, HBM, VMEM],
        scratch_shapes=[
            pltpu.VMEM((STEPS * 6 * grid.cx * grid.cy, 2 * grid.cz), jnp.bfloat16),
            pltpu.VMEM((16, count + 4 * LANES), jnp.float32),
            pltpu.SMEM(force_site.shape, jnp.int32),
            pltpu.SMEM(force_wavelet.shape, jnp.float32),
            pltpu.SMEM(spans.shape, jnp.int32),
            pltpu.SemaphoreType.DMA((4,)),
        ],
        input_output_aliases={0: 0, 1: 1},
        compiler_params=params,
        name="two_steps",
    )(block, beside, strips, lanes, rows, spans, force_site, force_wavelet)

    values = 6 * STEPS
    if capacity != 256:
        table = table.transpose(1, 0, 2).reshape(values, width, capacity).transpose(1, 0, 2)
    sent = lax.all_to_all(table, ("gx", "gy"), split_axis=0, concat_axis=0, tiled=True)
    return velocity, sent.transpose(1, 0, 2).reshape(1, values, slots)


def solution(mesh):
    in_specs = (
        P(None, ("runs", "gx"), "gy", "gz"),
        P(None, ("runs", "gx"), "gy", "gz"),
        P(None, ("runs", "gx"), "gy", "gz"),
        P("runs"),
        P("runs", None),
        P(("runs", "gx"), "gy", "gz", None),
        P(("runs", "gx"), "gy", "gz", None, None),
    )
    out_specs = (P(None, ("runs", "gx"), "gy", "gz"), P(("runs", "gz"), None, ("gx", "gy")))
    return jax.shard_map(
        per_device, mesh=mesh, in_specs=in_specs, out_specs=out_specs, check_vma=False
    )
```

```python
import functools

import jax
import jax.numpy as jnp
from jax import lax
from jax.experimental import pallas as pl
from jax.experimental.pallas import tpu as pltpu
from jax.sharding import PartitionSpec as P

STEPS = 2
TIME_STEP = 0.12

SXX, SYY, SZZ, SXY, SXZ, SYZ, VX, VY, VZ, LAM, MU, BUOY = range(12)
FIELDS = 12
DEPTHS = (6, 5, 5, 6, 6, 5, 5, 5, 5, 3, 3, 5)
OFFSETS = tuple(sum(DEPTHS[:f]) for f in range(FIELDS + 1))
HALO = 6
LAYERS = OFFSETS[-1]
ROWS = 8
STRIP = 8
LANES = 128
CORNER_ROWS = {f: (5, 5, 3, 2, 2) for f in (SXX, SYY, SXY, SXZ, SYZ)}
CORNER_ROWS.update({f: (3, 3, 2) for f in (SZZ, VX, VY, VZ, BUOY)})
CORNER_ROWS.update({f: (2, 2) for f in (LAM, MU)})


def corner_tiles():
    parts = [(n, f, d + 1) for f, counts in CORNER_ROWS.items() for d, n in enumerate(counts)]
    tiles = []
    for n, f, d in sorted(parts, reverse=True):
        for tile in tiles:
            used = sum(part[2] for part in tile)
            if used + n <= ROWS:
                tile.append((f, d, n, used))
                break
        else:
            tiles.append([(f, d, n, 0)])
    return tiles


CORNER_TILES = corner_tiles()
CORNERS = len(CORNER_TILES)
SLOT_STEP = 256
VMEM_LIMIT = 40 * 1024 * 1024
PART = 6
VMEM = pl.BlockSpec(memory_space=pltpu.VMEM)
HBM = pl.BlockSpec(memory_space=pltpu.HBM)
IDLE = pl.CostEstimate(flops=0, bytes_accessed=0, transcendentals=0)


def f32(*shape):
    return jax.ShapeDtypeStruct(shape, jnp.float32)


def groups(count):
    return -(-count // (LANES // STRIP))


def iota(dimension, shape=(ROWS, LANES)):
    return lax.broadcasted_iota(jnp.int32, shape, dimension)


def pack_strips(tiles, head):
    slot = iota(1) // STRIP
    packed = None
    for at, tile in enumerate(tiles):
        turned = pltpu.roll(tile, (STRIP * at + head) & (LANES - 1), 1)
        packed = turned if packed is None else jnp.where(slot == at, turned, packed)
    return packed


class Grid:
    def __init__(self, block, counts):
        self.cx, self.cy, self.cz = block
        self.gx, self.gy, self.gz = counts
        self.x_pairs = ("odd", "even") if self.gx > 2 else ("even",)
        self.y_pairs = ("even", "odd") if self.gy > 2 else ("even",)
        self.rows = self.cy + ROWS * len(self.y_pairs)
        self.layers = self.cx + 2 * HALO
        self.tiles_y = self.cy // ROWS

    def pairs(self, count, kind):
        start = 0 if kind == "even" else 1
        out = []
        for i in range(start, count - 1, 2):
            out += [(i, i + 1), (i + 1, i)]
        return out

    def pieces(self):
        out = [(("y", b), FIELDS * self.cx) for b in self.y_pairs]
        out += [(("x", a), LAYERS * self.tiles_y) for a in self.x_pairs]
        out += [(("d", a, b), CORNERS) for b in self.y_pairs for a in self.x_pairs]
        return out

    def shape(self, name):
        if name[0] == "x":
            return (LAYERS, self.cy, self.cz)
        if name[0] == "y":
            return (FIELDS, self.cx, ROWS, self.cz)
        return (CORNERS, ROWS, self.cz)


def above(axis, kind):
    parity = lax.rem(lax.axis_index(axis), 2)
    return parity == (0 if kind == "even" else 1)


def pack_kernel(grid, *refs):
    fields = refs[0]
    outs = refs[1:]
    sub = iota(0)
    for (name, _), out in zip(grid.pieces(), outs):
        if name[0] == "x":
            high = above("gx", name[1])
            for f in range(FIELDS):
                n = DEPTHS[f]
                start = jnp.where(high, grid.cx - n, 0)
                out[OFFSETS[f] : OFFSETS[f + 1]] = fields[f, pl.ds(start, n)]
        elif name[0] == "y":
            row = pl.multiple_of(jnp.where(above("gy", name[1]), grid.cy - ROWS, 0), ROWS)
            for f in range(FIELDS):
                out[f] = fields[f, :, pl.ds(row, ROWS), :]
        else:
            high = above("gx", name[1])
            up = above("gy", name[2])
            row = pl.multiple_of(jnp.where(up, grid.cy - ROWS, 0), ROWS)

            def tile(field, distance):
                layer = jnp.where(high, grid.cx - distance, distance - 1)
                return fields[field, layer, pl.ds(row, ROWS), :]

            for i, parts in enumerate(CORNER_TILES):
                packed = None
                for f, d, n, first in parts:
                    whole = tile(f, d)
                    turned = jnp.where(
                        up,
                        pltpu.roll(whole, (first + n) % ROWS, 0),
                        pltpu.roll(whole, first, 0) if first else whole,
                    )
                    packed = turned if packed is None else jnp.where(sub < first, packed, turned)
                out[i] = packed


def own_strip_kernel(grid, after, fields, own):
    head = jnp.where(lax.axis_index("gz") == 0, STRIP, 0)
    tiles = [(f, x, r) for f in range(FIELDS) for x in range(grid.cx) for r in range(grid.tiles_y)]
    for g in range(groups(len(tiles))):
        part = []
        for f, x, r in tiles[16 * g : 16 * g + 16]:
            part.append(fields[f, x, ROWS * r : ROWS * r + ROWS, :])
        own[g] = pack_strips(part, head)


def piece_tile(name, ref, at, grid):
    if name[0] == "x":
        r = at % grid.tiles_y
        return ref[at // grid.tiles_y, ROWS * r : ROWS * r + ROWS, :]
    if name[0] == "y":
        return ref[at // grid.cx, at % grid.cx]
    return ref[at]


def strip_kernel(grid, own, *refs):
    out = refs[-1]
    head = jnp.where(lax.axis_index("gz") == 0, STRIP, 0)
    base = own.shape[0]
    out[0:base] = own[...]
    for (name, count), ref in zip(grid.pieces(), refs[:-1]):
        for g in range(groups(count)):
            tiles = [
                piece_tile(name, ref, at, grid) for at in range(16 * g, min(16 * g + 16, count))
            ]
            out[base + g] = pack_strips(tiles, head)
        base += groups(count)


def slot_kernel(width, cz, cells_ref, writers_ref, lanes_ref, rows_ref, spans_ref):
    count = cells_ref.shape[1]
    cells = cells_ref[...]
    writers = writers_ref[...]
    padded = max(LANES, width)
    writer = iota(0, (padded, count))
    named = (writer == writers).astype(jnp.float32)
    fewer = (writers < writer).astype(jnp.float32)
    earlier = (iota(0, (count, count)) < iota(1, (count, count))).astype(jnp.float32)
    before = jnp.dot(
        named.astype(jnp.bfloat16), earlier.astype(jnp.bfloat16), preferred_element_type=jnp.float32
    )
    start = jnp.sum(fewer, axis=1, keepdims=True)
    rank = jnp.sum((before + start) * named, axis=0, keepdims=True).astype(jnp.int32)
    ones = jnp.ones((16, count), jnp.bfloat16)

    def across(marks):
        return lax.dot_general(
            ones,
            marks.astype(jnp.bfloat16),
            (((1,), (1,)), ((), ())),
            preferred_element_type=jnp.float32,
        ).astype(jnp.int32)

    spans_ref[0:ROWS, :] = across(fewer)[0:ROWS]
    spans_ref[ROWS : 2 * ROWS, :] = across(named)[0:ROWS]
    which = iota(0, (16, count))
    values = jnp.where(which == 0, lax.rem(cells, cz), jnp.where(which == 1, lax.div(cells, cz), 0))
    values = values.astype(jnp.float32).astype(jnp.bfloat16)
    for n in range(0, count, SLOT_STEP):
        hit = (iota(0, (SLOT_STEP, count)) + n == rank).astype(jnp.float32)
        table = lax.dot_general(
            values,
            hit.astype(jnp.bfloat16),
            (((1,), (1,)), ((), ())),
            preferred_element_type=jnp.float32,
        ).astype(jnp.int32)
        marks = (iota(0, (cz, SLOT_STEP)) == table[0:1]).astype(jnp.float32).astype(jnp.bfloat16)
        lanes_ref[0:cz, n : n + SLOT_STEP] = marks
        lanes_ref[cz : 2 * cz, n : n + SLOT_STEP] = marks
        rows_ref[:, n : n + SLOT_STEP] = jnp.broadcast_to(table[1:2], (ROWS, SLOT_STEP))


def edge(grid, up):
    if len(grid.y_pairs) > 1:
        return lambda tile: tile
    sub = iota(0)
    keep = jnp.logical_or(sub < jnp.where(up, 6, 0), sub >= jnp.where(up, 8, 2))
    return lambda tile: jnp.where(keep, tile, 0.0)


def halo_row(grid, up):
    if len(grid.y_pairs) == 1:
        return grid.cy
    return pl.multiple_of(jnp.where(up, grid.cy, grid.cy + ROWS), ROWS)


def lay_own(grid, ext, own):
    cx, cy = grid.cx, grid.cy
    for f in range(FIELDS):
        for x in list(range(HALO)) + list(range(HALO + cx, grid.layers)):
            for row in range(cy, grid.rows, ROWS):
                ext[f, x, row : row + ROWS, :] = jnp.zeros((ROWS, grid.cz), jnp.float32)
    at = 0
    for f in range(FIELDS):
        for x in range(cx):
            for r in range(grid.tiles_y):
                ext[f, HALO + x, ROWS * r : ROWS * r + ROWS, :] = own(at)
                at += 1


def lay_halos(grid, ext, arrived):
    cx, cy = grid.cx, grid.cy
    for (name, count), tile_of in zip(grid.pieces(), arrived):
        if name[0] == "x":
            high = above("gx", name[1])
            at = 0
            for f in range(FIELDS):
                start = jnp.where(high, HALO + cx, HALO - DEPTHS[f])
                for d in range(DEPTHS[f]):
                    for r in range(grid.tiles_y):
                        ext[f, start + d, ROWS * r : ROWS * r + ROWS, :] = tile_of(at)
                        at += 1
            continue
        up = above("gy", name[-1])
        clear = edge(grid, up)
        place = halo_row(grid, up)
        if name[0] == "y":
            for f in range(FIELDS):
                for x in range(cx):
                    ext[f, HALO + x, pl.ds(place, ROWS), :] = clear(tile_of(f * cx + x))
            continue
        high = above("gx", name[1])

        def put(field, distance, tile):
            layer = jnp.where(high, HALO + cx - 1 + distance, HALO - distance)
            ext[field, layer, pl.ds(place, ROWS), :] = clear(tile)

        for i, parts in enumerate(CORNER_TILES):
            tile = tile_of(i)
            for f, d, n, first in parts:
                turned = jnp.where(
                    up,
                    pltpu.roll(tile, ROWS - first, 0) if first else tile,
                    pltpu.roll(tile, (-first - n) % ROWS, 0),
                )
                put(f, d, turned)


def known_lanes():
    lead = jnp.where(lax.axis_index("gz") == 0, 0, LANES - STRIP)
    lane = iota(1)
    return lead, jnp.logical_and(lane >= lead, lane < lead + STRIP)


def unpack(ref, base, at):
    lead, known = known_lanes()
    turned = pltpu.roll(ref[base + at // 16], (lead - STRIP * (at % 16)) & (LANES - 1), 1)
    return jnp.where(known, turned, 0.0)


def begin_kernel(grid, *refs):
    fields, ext = refs

    def own(at):
        x, r = at // grid.tiles_y % grid.cx, at % grid.tiles_y
        return fields[at // (grid.tiles_y * grid.cx), x, ROWS * r : ROWS * r + ROWS, :]

    lay_own(grid, ext, own)


def assemble_kernel(grid, *refs):
    arrived, ext = refs[1:-1], refs[-1]
    tiles = [
        functools.partial(piece_tile, name, ref, grid=grid)
        for (name, _), ref in zip(grid.pieces(), arrived)
    ]
    lay_halos(grid, ext, tiles)


def main_kernel(grid, width, capacity, *refs):
    strips, lanes_ref, rows_ref, spans_vmem, site_hbm, wavelet_hbm = refs[1:7]
    ext, velocity_out, table_out = refs[7:10]
    beside, sampled, compact, site_ref, wavelet_ref, spans_ref, sems = refs[10:]
    copies = (
        pltpu.make_async_copy(site_hbm, site_ref, sems.at[0]),
        pltpu.make_async_copy(wavelet_hbm, wavelet_ref, sems.at[1]),
        pltpu.make_async_copy(spans_vmem, spans_ref, sems.at[2]),
    )
    for copy in copies:
        copy.start()
    rows = grid.rows
    cx, cy, cz = grid.cx, grid.cy, grid.cz
    half = lax.axis_index("gz")
    sub = iota(0)
    lane = iota(1)
    lay_own(grid, beside, functools.partial(unpack, strips, 0))
    bases = [groups(FIELDS * cx * grid.tiles_y)]
    for _, count in grid.pieces():
        bases.append(bases[-1] + groups(count))
    lay_halos(grid, beside, [functools.partial(unpack, strips, base) for base in bases[:-1]])
    lane_all = iota(1, (rows, cz))

    def pair(field, x):
        return ext[field, x], beside[field, x]

    def add(a, b):
        return a[0] + b[0], a[1] + b[1]

    def sub_(a, b):
        return a[0] - b[0], a[1] - b[1]

    def along_x(field, x):
        return (
            sub_(pair(field, x + 1), pair(field, x)),
            sub_(pair(field, x + 2), pair(field, x - 1)),
        )

    def moved_y(a, offset):
        return tuple(pltpu.roll(v, -offset % rows, 0) for v in a)

    def moved_z(a, offset):
        own = pltpu.roll(a[0], -offset % cz, 1)
        far = pltpu.roll(a[1], -offset % cz, 1)
        inside = lane_all[: own.shape[0]]
        inside = inside < cz - offset if offset > 0 else inside >= -offset
        return jnp.where(inside, own, far), jnp.where(inside, far, own)

    def forward(a, move):
        return sub_(move(a, 1), a), sub_(move(a, 2), move(a, -1))

    def backward(a, move):
        return sub_(a, move(a, -1)), sub_(move(a, 1), move(a, -2))

    def total(*terms):
        near, far = terms[0]
        for other_near, other_far in terms[1:]:
            near, far = add(near, other_near), add(far, other_far)
        return tuple(27.0 * p - q for p, q in zip(near, far))

    scale = TIME_STEP / 24.0

    def velocity_layer(x):
        y = x + 1
        sxy_x, sxz_x = pair(SXY, x), pair(SXZ, x)
        rate_x = total(along_x(SXX, x), backward(sxy_x, moved_y), backward(sxz_x, moved_z))
        syz = pair(SYZ, y)
        rate_y = total(
            along_x(SXY, y - 1), forward(pair(SYY, y), moved_y), backward(syz, moved_z)
        )
        rate_z = total(
            along_x(SXZ, y - 1), backward(syz, moved_y), forward(pair(SZZ, y), moved_z)
        )
        for h, block in enumerate((ext, beside)):
            b = scale * block[BUOY, x]
            block[VX, x] = block[VX, x] + b * rate_x[h]
            b = scale * block[BUOY, y]
            block[VY, y] = block[VY, y] + b * rate_y[h]
            block[VZ, y] = block[VZ, y] + b * rate_z[h]

    def stress_layer(x, last=False):
        kept = cy if last else rows

        def cut(a):
            return tuple(v[:kept] for v in a)

        def across_y(move, a):
            return tuple(cut(v) for v in move(a, moved_y))

        def along(move, a):
            return move(cut(a), moved_z)

        def beyond(field, at):
            return tuple(cut(v) for v in along_x(field, at))

        vx, vy, vz = pair(VX, x), pair(VY, x), pair(VZ, x)
        gxx = total(beyond(VX, x - 1))
        gyy = total(across_y(backward, vy))
        gzz = total(along(backward, vz))
        gxy = total(across_y(forward, vx), beyond(VY, x))
        gxz = total(along(forward, vx), beyond(VZ, x))
        gyz = total(along(forward, vy), across_y(forward, vz))
        for h, block in enumerate((ext,) if last else (ext, beside)):
            shear = scale * block[MU, x, 0:kept]
            volume = scale * block[LAM, x, 0:kept] * (gxx[h] + gyy[h] + gzz[h])
            twice = 2.0 * shear
            for f, change in (
                (SXX, twice * gxx[h] + volume),
                (SYY, twice * gyy[h] + volume),
                (SZZ, twice * gzz[h] + volume),
                (SXY, shear * gxy[h]),
                (SXZ, shear * gxz[h]),
                (SYZ, shear * gyz[h]),
            ):
                block[f, x, 0:kept] = block[f, x, 0:kept] + change

    def loop(first, last, body):
        def step(x, carry):
            body(x)
            return carry

        lax.fori_loop(HALO + first, HALO + last + 1, step, 0, unroll=True)

    loop(-5, cx + 3, velocity_layer)
    for copy in copies:
        copy.wait()
    site = site_ref[0]
    total_y, total_z = cy * grid.gy, cz * grid.gz
    site_x = lax.div(site, total_y * total_z) - lax.axis_index("gx") * cx
    site_y = lax.rem(lax.div(site, total_z), total_y) - lax.axis_index("gy") * cy
    site_z = lax.rem(site, total_z)
    near = jnp.logical_and(site_x >= -HALO, site_x < cx + HALO)
    near = jnp.logical_and(near, jnp.logical_and(site_y >= -ROWS, site_y < cy + ROWS))
    site_row = jnp.where(site_y < 0, site_y + rows, site_y)

    def inject(step):
        x = site_x + HALO
        row = pl.multiple_of(lax.div(site_row, ROWS) * ROWS, ROWS)
        here = jnp.logical_and(sub == lax.rem(site_row, ROWS), lane == lax.rem(site_z, cz))
        own = lax.div(site_z, cz) == half
        for mine, block in ((True, ext), (False, beside)):

            @pl.when(jnp.logical_and(near, own if mine else jnp.logical_not(own)))
            def _():
                amount = jnp.where(here, TIME_STEP * block[BUOY, x, pl.ds(row, ROWS), :], 0.0)
                for c in range(3):
                    block[VX + c, x, pl.ds(row, ROWS), :] = (
                        block[VX + c, x, pl.ds(row, ROWS), :] + amount * wavelet_ref[step, c]
                    )

    def strain_layer(step, x):
        lam = ext[LAM, x, 0:cy, :]
        shear = ext[MU, x, 0:cy, :]
        parts = [ext[f, x, 0:cy, :] for f in range(6)]
        shrink = lam / (3.0 * lam + 2.0 * shear) * (parts[0] + parts[1] + parts[2])
        inverse = 0.5 / shear
        for f in range(6):
            value = (parts[f] - shrink if f < 3 else parts[f]) * inverse
            head = value.astype(jnp.bfloat16)
            tail = (value - head.astype(jnp.float32)).astype(jnp.bfloat16)
            row = pl.multiple_of((6 * step + f) * cx * cy + (x - HALO) * cy, cy)
            sampled[pl.ds(row, cy), 0:cz] = head
            sampled[pl.ds(row, cy), cz : 2 * cz] = tail

    block = cx * cy

    def sample(k, carry):
        where = pl.ds(pl.multiple_of(k * SLOT_STEP, SLOT_STEP), SLOT_STEP)
        to_lanes = pl.ds(pl.multiple_of(k * SLOT_STEP + LANES, LANES), SLOT_STEP)
        row = rows_ref[:, where]
        marks = [row == r * ROWS + iota(0, (ROWS, SLOT_STEP)) for r in range(block // ROWS)]
        for part in range(6 * STEPS // PART):
            found = jnp.dot(
                sampled[part * PART * block : (part + 1) * PART * block, :],
                lanes_ref[:, where],
                preferred_element_type=jnp.float32,
            )
            for f in range(PART):
                acc = jnp.zeros((ROWS, SLOT_STEP), jnp.float32)
                for r in range(block // ROWS):
                    tile = found[f * block + r * ROWS : f * block + r * ROWS + ROWS]
                    acc = acc + jnp.where(marks[r], tile, 0.0)
                to = part * PART + f
                compact[to : to + 1, to_lanes] = jnp.sum(acc, axis=0, keepdims=True)
        return carry

    def spread():
        values = 6 * STEPS
        lanes_at = iota(1, (values, LANES))
        for t in range(width * capacity // LANES):
            out = jnp.zeros((values, LANES), jnp.float32)
            for w in range(t * LANES // capacity, -(-(t + 1) * LANES // capacity)):
                skip = t * LANES - w * capacity
                start = spans_ref[0, w] + skip + LANES
                base = pl.multiple_of(lax.div(start, LANES) * LANES, LANES)
                shift = lax.rem(start, LANES)
                near = pltpu.roll(compact[0:values, pl.ds(base, LANES)], LANES - shift, 1)
                far = pltpu.roll(compact[0:values, pl.ds(base + LANES, LANES)], LANES - shift, 1)
                place = lanes_at + skip
                mine = jnp.logical_and(place >= 0, place < spans_ref[ROWS, w])
                out = jnp.where(mine, jnp.where(lanes_at < LANES - shift, near, far), out)
            per = 256 // LANES
            table_out[t // per, :, t % per * LANES : (t % per + 1) * LANES] = out

    inject(0)
    loop(-3, cx + 2, stress_layer)
    loop(0, cx - 1, functools.partial(strain_layer, 0))
    loop(-2, cx, velocity_layer)
    inject(1)
    leaving = pltpu.make_async_copy(
        ext.at[VX : VX + 3, HALO : HALO + cx, 0:cy, :], velocity_out, sems.at[3]
    )
    leaving.start()
    loop(0, cx - 1, functools.partial(stress_layer, last=True))
    loop(0, cx - 1, functools.partial(strain_layer, 1))
    lax.fori_loop(0, lanes_ref.shape[1] // SLOT_STEP, sample, 0, unroll=True)
    spread()
    leaving.wait()


def per_device(
    velocity_start, stress_start, material, force_site, force_wavelet, save_cells, save_writer
):
    counts = tuple(lax.axis_size(axis) for axis in ("gx", "gy", "gz"))
    grid = Grid(velocity_start.shape[1:], counts)
    pieces = grid.pieces()
    params = pltpu.CompilerParams(vmem_limit_bytes=VMEM_LIMIT)
    own_tiles = FIELDS * grid.cx * grid.tiles_y
    fields = sum(
        lax.pad(part, jnp.float32(0.0), [(first, FIELDS - first - part.shape[0], 0)] + [(0, 0, 0)] * 3)
        for first, part in ((SXX, stress_start), (VX, velocity_start), (LAM, material))
    )
    packed = pl.pallas_call(
        lambda *refs: pack_kernel(grid, *refs),
        out_shape=[f32(*grid.shape(name)) for name, _ in pieces],
        in_specs=[VMEM],
        out_specs=[VMEM] * len(pieces),
        compiler_params=params,
        name="pack_halos",
    )(fields)
    swap = [(0, 1), (1, 0)]
    arrived = []
    for (name, _), piece in zip(pieces, packed):
        if name[0] == "x":
            arrived.append(lax.ppermute(piece, "gx", grid.pairs(grid.gx, name[1])))
        elif name[0] == "y":
            arrived.append(lax.ppermute(piece, "gy", grid.pairs(grid.gy, name[1])))
        else:
            pairs = [
                (a * grid.gy + b, c * grid.gy + d)
                for a, c in grid.pairs(grid.gx, name[1])
                for b, d in grid.pairs(grid.gy, name[2])
            ]
            arrived.append(lax.ppermute(piece, ("gx", "gy"), pairs))
    count = save_cells.size
    width = grid.gx * grid.gy
    capacity = max(2, 2 * count // width)
    slots = width * capacity
    lanes, rows, spans = pl.pallas_call(
        functools.partial(slot_kernel, width, grid.cz),
        out_shape=[
            jax.ShapeDtypeStruct((2 * grid.cz, count), jnp.bfloat16),
            jax.ShapeDtypeStruct((ROWS, count), jnp.int32),
            jax.ShapeDtypeStruct((2 * ROWS, max(LANES, width)), jnp.int32),
        ],
        in_specs=[VMEM] * 2,
        out_specs=[VMEM] * 3,
        compiler_params=params,
        cost_estimate=IDLE,
        name="slot_tables",
    )(save_cells.reshape(1, count), save_writer.reshape(1, count))

    own_strips = pl.pallas_call(
        functools.partial(own_strip_kernel, grid),
        out_shape=f32(groups(own_tiles), ROWS, LANES),
        in_specs=[VMEM] * 2,
        out_specs=VMEM,
        compiler_params=params,
        cost_estimate=IDLE,
        name="pack_own_strips",
    )(rows, fields)

    extended = f32(FIELDS, grid.layers, grid.rows, grid.cz)
    block = pl.pallas_call(
        lambda *refs: begin_kernel(grid, *refs),
        out_shape=extended,
        in_specs=[VMEM],
        out_specs=VMEM,
        compiler_params=params,
        cost_estimate=IDLE,
        name="begin_block",
    )(fields)

    strips = pl.pallas_call(
        lambda *refs: strip_kernel(grid, *refs[2:]),
        out_shape=f32(groups(own_tiles) + sum(groups(c) for _, c in pieces), ROWS, LANES),
        in_specs=[VMEM] * (len(pieces) + 3),
        out_specs=VMEM,
        compiler_params=params,
        name="pack_strips",
    )(rows, block, own_strips, *arrived)
    strips = lax.ppermute(strips, "gz", swap)

    block = pl.pallas_call(
        lambda *refs: assemble_kernel(grid, *refs),
        out_shape=extended,
        in_specs=[VMEM] * (1 + len(pieces)),
        out_specs=VMEM,
        input_output_aliases={0: 0},
        compiler_params=params,
        name="assemble",
    )(block, *arrived)

    _, velocity, table = pl.pallas_call(
        functools.partial(main_kernel, grid, width, capacity),
        out_shape=[
            extended,
            f32(*velocity_start.shape),
            f32(slots // 256, 6 * STEPS, 256),
        ],
        in_specs=[VMEM] * 5 + [HBM] * 2,
        out_specs=[VMEM, HBM, VMEM],
        scratch_shapes=[
            pltpu.VMEM(extended.shape, jnp.float32),
            pltpu.VMEM((STEPS * 6 * grid.cx * grid.cy, 2 * grid.cz), jnp.bfloat16),
            pltpu.VMEM((16, count + 4 * LANES), jnp.float32),
            pltpu.SMEM(force_site.shape, jnp.int32),
            pltpu.SMEM(force_wavelet.shape, jnp.float32),
            pltpu.SMEM(spans.shape, jnp.int32),
            pltpu.SemaphoreType.DMA((4,)),
        ],
        input_output_aliases={0: 0},
        compiler_params=params,
        name="two_steps",
    )(block, strips, lanes, rows, spans, force_site, force_wavelet)

    values = 6 * STEPS
    if capacity != 256:
        table = table.transpose(1, 0, 2).reshape(values, width, capacity).transpose(1, 0, 2)
    sent = lax.all_to_all(table, ("gx", "gy"), split_axis=0, concat_axis=0, tiled=True)
    return velocity, sent.transpose(1, 0, 2).reshape(1, values, slots)


def solution(mesh):
    in_specs = (
        P(None, ("runs", "gx"), "gy", "gz"),
        P(None, ("runs", "gx"), "gy", "gz"),
        P(None, ("runs", "gx"), "gy", "gz"),
        P("runs"),
        P("runs", None),
        P(("runs", "gx"), "gy", "gz", None),
        P(("runs", "gx"), "gy", "gz", None, None),
    )
    out_specs = (P(None, ("runs", "gx"), "gy", "gz"), P(("runs", "gz"), None, ("gx", "gy")))
    return jax.shard_map(
        per_device, mesh=mesh, in_specs=in_specs, out_specs=out_specs, check_vma=False
    )
```

```python
import functools

import jax
import jax.numpy as jnp
from jax import lax
from jax.experimental import pallas as pl
from jax.experimental.pallas import tpu as pltpu
from jax.sharding import PartitionSpec as P

STEPS = 2
TIME_STEP = 0.12

SXX, SYY, SZZ, SXY, SXZ, SYZ, VX, VY, VZ, LAM, MU, BUOY = range(12)
FIELDS = 12
DEPTHS = (6, 5, 5, 6, 6, 5, 5, 5, 5, 3, 3, 5)
OFFSETS = tuple(sum(DEPTHS[:f]) for f in range(FIELDS + 1))
HALO = 6
LAYERS = OFFSETS[-1]
ROWS = 8
STRIP = 8
LANES = 128
CORNER_ROWS = {f: (5, 5, 3, 2, 2) for f in (SXX, SYY, SXY, SXZ, SYZ)}
CORNER_ROWS.update({f: (3, 3, 2) for f in (SZZ, VX, VY, VZ, BUOY)})
CORNER_ROWS.update({f: (2, 2) for f in (LAM, MU)})


def corner_tiles():
    parts = [(n, f, d + 1) for f, counts in CORNER_ROWS.items() for d, n in enumerate(counts)]
    tiles = []
    for n, f, d in sorted(parts, reverse=True):
        for tile in tiles:
            used = sum(part[2] for part in tile)
            if used + n <= ROWS:
                tile.append((f, d, n, used))
                break
        else:
            tiles.append([(f, d, n, 0)])
    return tiles


CORNER_TILES = corner_tiles()
CORNERS = len(CORNER_TILES)
SLOT_STEP = 256
VMEM_LIMIT = 40 * 1024 * 1024
PART = 6
VMEM = pl.BlockSpec(memory_space=pltpu.VMEM)
HBM = pl.BlockSpec(memory_space=pltpu.HBM)
SMEM = pl.BlockSpec(memory_space=pltpu.SMEM)
IDLE = pl.CostEstimate(flops=0, bytes_accessed=0, transcendentals=0)


def f32(*shape):
    return jax.ShapeDtypeStruct(shape, jnp.float32)


def groups(count):
    return -(-count // (LANES // STRIP))


def iota(dimension, shape=(ROWS, LANES)):
    return lax.broadcasted_iota(jnp.int32, shape, dimension)


def pack_strips(tiles, head):
    slot = iota(1) // STRIP
    packed = None
    for at, tile in enumerate(tiles):
        turned = pltpu.roll(tile, (STRIP * at + head) & (LANES - 1), 1)
        packed = turned if packed is None else jnp.where(slot == at, turned, packed)
    return packed


class Grid:
    def __init__(self, block, counts):
        self.cx, self.cy, self.cz = block
        self.gx, self.gy, self.gz = counts
        self.x_pairs = ("odd", "even") if self.gx > 2 else ("even",)
        self.y_pairs = ("even", "odd") if self.gy > 2 else ("even",)
        self.rows = self.cy + ROWS * len(self.y_pairs)
        self.layers = self.cx + 2 * HALO
        self.tiles_y = self.cy // ROWS

    def pairs(self, count, kind):
        start = 0 if kind == "even" else 1
        out = []
        for i in range(start, count - 1, 2):
            out += [(i, i + 1), (i + 1, i)]
        return out

    def pieces(self):
        out = [(("y", b), FIELDS * self.cx) for b in self.y_pairs]
        out += [(("x", a), LAYERS * self.tiles_y) for a in self.x_pairs]
        out += [(("d", a, b), CORNERS) for b in self.y_pairs for a in self.x_pairs]
        return out

    def shape(self, name):
        if name[0] == "x":
            return (LAYERS, self.cy, self.cz)
        if name[0] == "y":
            return (FIELDS, self.cx, ROWS, self.cz)
        return (CORNERS, ROWS, self.cz)


def above(axis, kind):
    parity = lax.rem(lax.axis_index(axis), 2)
    return parity == (0 if kind == "even" else 1)


def pack_kernel(grid, *refs):
    fields = refs[0]
    outs = refs[1:]
    sub = iota(0)
    for (name, _), out in zip(grid.pieces(), outs):
        if name[0] == "x":
            high = above("gx", name[1])
            for f in range(FIELDS):
                n = DEPTHS[f]
                start = jnp.where(high, grid.cx - n, 0)
                out[OFFSETS[f] : OFFSETS[f + 1]] = fields[f, pl.ds(start, n)]
        elif name[0] == "y":
            row = pl.multiple_of(jnp.where(above("gy", name[1]), grid.cy - ROWS, 0), ROWS)
            for f in range(FIELDS):
                out[f] = fields[f, :, pl.ds(row, ROWS), :]
        else:
            high = above("gx", name[1])
            up = above("gy", name[2])
            row = pl.multiple_of(jnp.where(up, grid.cy - ROWS, 0), ROWS)

            def tile(field, distance):
                layer = jnp.where(high, grid.cx - distance, distance - 1)
                return fields[field, layer, pl.ds(row, ROWS), :]

            for i, parts in enumerate(CORNER_TILES):
                packed = None
                for f, d, n, first in parts:
                    whole = tile(f, d)
                    turned = jnp.where(
                        up,
                        pltpu.roll(whole, (first + n) % ROWS, 0),
                        pltpu.roll(whole, first, 0) if first else whole,
                    )
                    packed = turned if packed is None else jnp.where(sub < first, packed, turned)
                out[i] = packed


def own_strip_kernel(grid, after, fields, own):
    head = jnp.where(lax.axis_index("gz") == 0, STRIP, 0)
    tiles = [(f, x, r) for f in range(FIELDS) for x in range(grid.cx) for r in range(grid.tiles_y)]
    for g in range(groups(len(tiles))):
        part = []
        for f, x, r in tiles[16 * g : 16 * g + 16]:
            part.append(fields[f, x, ROWS * r : ROWS * r + ROWS, :])
        own[g] = pack_strips(part, head)


def piece_tile(name, ref, at, grid):
    if name[0] == "x":
        r = at % grid.tiles_y
        return ref[at // grid.tiles_y, ROWS * r : ROWS * r + ROWS, :]
    if name[0] == "y":
        return ref[at // grid.cx, at % grid.cx]
    return ref[at]


def strip_kernel(grid, pieces, base, refs, out):
    head = jnp.where(lax.axis_index("gz") == 0, STRIP, 0)
    for (name, count), ref in zip(pieces, refs):
        for g in range(groups(count)):
            tiles = [
                piece_tile(name, ref, at, grid) for at in range(16 * g, min(16 * g + 16, count))
            ]
            out[base + g] = pack_strips(tiles, head)
        base += groups(count)


def face_strip_kernel(grid, pieces, *refs):
    own, out = refs[2], refs[-1]
    out[0 : own.shape[0]] = own[...]
    strip_kernel(grid, pieces, own.shape[0], refs[3:-1], out)


def slot_kernel(
    width,
    cz,
    cells_ref,
    writers_ref,
    site_ref,
    wavelet_ref,
    lanes_ref,
    rows_ref,
    spans_ref,
    force_ref,
):
    force_ref[0 : wavelet_ref.shape[0], 0 : wavelet_ref.shape[1]] = wavelet_ref[...]
    count = cells_ref.shape[1]
    cells = cells_ref[...]
    writers = writers_ref[...]
    padded = max(LANES, width)
    writer = iota(0, (padded, count))
    named = (writer == writers).astype(jnp.float32)
    fewer = (writers < writer).astype(jnp.float32)
    earlier = (iota(0, (count, count)) < iota(1, (count, count))).astype(jnp.float32)
    before = jnp.dot(
        named.astype(jnp.bfloat16), earlier.astype(jnp.bfloat16), preferred_element_type=jnp.float32
    )
    start = jnp.sum(fewer, axis=1, keepdims=True)
    rank = jnp.sum((before + start) * named, axis=0, keepdims=True).astype(jnp.int32)
    ones = jnp.ones((16, count), jnp.bfloat16)

    def across(marks):
        return lax.dot_general(
            ones,
            marks.astype(jnp.bfloat16),
            (((1,), (1,)), ((), ())),
            preferred_element_type=jnp.float32,
        ).astype(jnp.int32)

    first = across(fewer)[0:ROWS]
    spans_ref[0:ROWS, :] = jnp.where(iota(0, first.shape) == 1, site_ref[0], first)
    spans_ref[ROWS : 2 * ROWS, :] = across(named)[0:ROWS]
    which = iota(0, (16, count))
    values = jnp.where(which == 0, lax.rem(cells, cz), jnp.where(which == 1, lax.div(cells, cz), 0))
    values = values.astype(jnp.float32).astype(jnp.bfloat16)
    for n in range(0, count, SLOT_STEP):
        hit = (iota(0, (SLOT_STEP, count)) + n == rank).astype(jnp.float32)
        table = lax.dot_general(
            values,
            hit.astype(jnp.bfloat16),
            (((1,), (1,)), ((), ())),
            preferred_element_type=jnp.float32,
        ).astype(jnp.int32)
        marks = (iota(0, (cz, SLOT_STEP)) == table[0:1]).astype(jnp.float32).astype(jnp.bfloat16)
        lanes_ref[0:cz, n : n + SLOT_STEP] = marks
        lanes_ref[cz : 2 * cz, n : n + SLOT_STEP] = marks
        rows_ref[:, n : n + SLOT_STEP] = jnp.broadcast_to(table[1:2], (ROWS, SLOT_STEP))


def edge(grid, up):
    if len(grid.y_pairs) > 1:
        return lambda tile: tile
    sub = iota(0)
    keep = jnp.logical_or(sub < jnp.where(up, 6, 0), sub >= jnp.where(up, 8, 2))
    return lambda tile: jnp.where(keep, tile, 0.0)


def halo_row(grid, up):
    if len(grid.y_pairs) == 1:
        return grid.cy
    return pl.multiple_of(jnp.where(up, grid.cy, grid.cy + ROWS), ROWS)


def lay_own(grid, ext, own):
    cx, cy = grid.cx, grid.cy
    for f in range(FIELDS):
        for x in list(range(HALO)) + list(range(HALO + cx, grid.layers)):
            for row in range(cy, grid.rows, ROWS):
                ext[f, x, row : row + ROWS, :] = jnp.zeros((ROWS, grid.cz), jnp.float32)
    at = 0
    for f in range(FIELDS):
        for x in range(cx):
            for r in range(grid.tiles_y):
                ext[f, HALO + x, ROWS * r : ROWS * r + ROWS, :] = own(at)
                at += 1


def lay_halos(grid, ext, arrived):
    cx, cy = grid.cx, grid.cy
    for (name, count), tile_of in zip(grid.pieces(), arrived):
        if name[0] == "x":
            high = above("gx", name[1])
            at = 0
            for f in range(FIELDS):
                start = jnp.where(high, HALO + cx, HALO - DEPTHS[f])
                for d in range(DEPTHS[f]):
                    for r in range(grid.tiles_y):
                        ext[f, start + d, ROWS * r : ROWS * r + ROWS, :] = tile_of(at)
                        at += 1
            continue
        up = above("gy", name[-1])
        clear = edge(grid, up)
        place = halo_row(grid, up)
        if name[0] == "y":
            for f in range(FIELDS):
                for x in range(cx):
                    ext[f, HALO + x, pl.ds(place, ROWS), :] = clear(tile_of(f * cx + x))
            continue
        high = above("gx", name[1])

        def put(field, distance, tile):
            layer = jnp.where(high, HALO + cx - 1 + distance, HALO - distance)
            ext[field, layer, pl.ds(place, ROWS), :] = clear(tile)

        for i, parts in enumerate(CORNER_TILES):
            tile = tile_of(i)
            for f, d, n, first in parts:
                turned = jnp.where(
                    up,
                    pltpu.roll(tile, ROWS - first, 0) if first else tile,
                    pltpu.roll(tile, (-first - n) % ROWS, 0),
                )
                put(f, d, turned)


def known_lanes():
    lead = jnp.where(lax.axis_index("gz") == 0, 0, LANES - STRIP)
    lane = iota(1)
    return lead, jnp.logical_and(lane >= lead, lane < lead + STRIP)


def unpack(ref, base, at):
    lead, known = known_lanes()
    turned = pltpu.roll(ref[base + at // 16], (lead - STRIP * (at % 16)) & (LANES - 1), 1)
    return jnp.where(known, turned, 0.0)


def begin_kernel(grid, *refs):
    fields, ext = refs

    def own(at):
        x, r = at // grid.tiles_y % grid.cx, at % grid.tiles_y
        return fields[at // (grid.tiles_y * grid.cx), x, ROWS * r : ROWS * r + ROWS, :]

    lay_own(grid, ext, own)


def assemble_kernel(grid, *refs):
    arrived, ext = refs[1:-1], refs[-1]
    tiles = [
        functools.partial(piece_tile, name, ref, grid=grid)
        for (name, _), ref in zip(grid.pieces(), arrived)
    ]
    lay_halos(grid, ext, tiles)


def main_kernel(grid, width, capacity, *refs):
    strips, lanes_ref, rows_ref, spans_vmem, force_vmem = refs[1:6]
    ext, velocity_out, table_out = refs[6:9]
    beside, sampled, compact, wavelet_ref, spans_ref, sems = refs[9:]
    copies = (
        pltpu.make_async_copy(force_vmem, wavelet_ref, sems.at[0]),
        pltpu.make_async_copy(spans_vmem, spans_ref, sems.at[1]),
    )
    for copy in copies:
        copy.start()
    rows = grid.rows
    cx, cy, cz = grid.cx, grid.cy, grid.cz
    half = lax.axis_index("gz")
    sub = iota(0)
    lane = iota(1)
    lay_own(grid, beside, functools.partial(unpack, strips, 0))
    bases = [groups(FIELDS * cx * grid.tiles_y)]
    for _, count in grid.pieces():
        bases.append(bases[-1] + groups(count))
    lay_halos(grid, beside, [functools.partial(unpack, strips, base) for base in bases[:-1]])
    lane_all = iota(1, (rows, cz))

    def pair(field, x):
        return ext[field, x], beside[field, x]

    def add(a, b):
        return a[0] + b[0], a[1] + b[1]

    def sub_(a, b):
        return a[0] - b[0], a[1] - b[1]

    def along_x(field, x):
        return (
            sub_(pair(field, x + 1), pair(field, x)),
            sub_(pair(field, x + 2), pair(field, x - 1)),
        )

    def moved_y(a, offset):
        return tuple(pltpu.roll(v, -offset % rows, 0) for v in a)

    def moved_z(a, offset):
        own = pltpu.roll(a[0], -offset % cz, 1)
        far = pltpu.roll(a[1], -offset % cz, 1)
        inside = lane_all[: own.shape[0]]
        inside = inside < cz - offset if offset > 0 else inside >= -offset
        return jnp.where(inside, own, far), jnp.where(inside, far, own)

    def forward(a, move):
        return sub_(move(a, 1), a), sub_(move(a, 2), move(a, -1))

    def backward(a, move):
        return sub_(a, move(a, -1)), sub_(move(a, 1), move(a, -2))

    def total(*terms):
        near, far = terms[0]
        for other_near, other_far in terms[1:]:
            near, far = add(near, other_near), add(far, other_far)
        return tuple(27.0 * p - q for p, q in zip(near, far))

    scale = TIME_STEP / 24.0

    def velocity_layer(x):
        y = x + 1
        sxy_x, sxz_x = pair(SXY, x), pair(SXZ, x)
        rate_x = total(along_x(SXX, x), backward(sxy_x, moved_y), backward(sxz_x, moved_z))
        syz = pair(SYZ, y)
        rate_y = total(
            along_x(SXY, y - 1), forward(pair(SYY, y), moved_y), backward(syz, moved_z)
        )
        rate_z = total(
            along_x(SXZ, y - 1), backward(syz, moved_y), forward(pair(SZZ, y), moved_z)
        )
        for h, block in enumerate((ext, beside)):
            b = scale * block[BUOY, x]
            block[VX, x] = block[VX, x] + b * rate_x[h]
            b = scale * block[BUOY, y]
            block[VY, y] = block[VY, y] + b * rate_y[h]
            block[VZ, y] = block[VZ, y] + b * rate_z[h]

    def stress_layer(x, last=False):
        kept = cy if last else rows

        def cut(a):
            return tuple(v[:kept] for v in a)

        def across_y(move, a):
            return tuple(cut(v) for v in move(a, moved_y))

        def along(move, a):
            return move(cut(a), moved_z)

        def beyond(field, at):
            return tuple(cut(v) for v in along_x(field, at))

        vx, vy, vz = pair(VX, x), pair(VY, x), pair(VZ, x)
        gxx = total(beyond(VX, x - 1))
        gyy = total(across_y(backward, vy))
        gzz = total(along(backward, vz))
        gxy = total(across_y(forward, vx), beyond(VY, x))
        gxz = total(along(forward, vx), beyond(VZ, x))
        gyz = total(along(forward, vy), across_y(forward, vz))
        for h, block in enumerate((ext,) if last else (ext, beside)):
            shear = scale * block[MU, x, 0:kept]
            volume = scale * block[LAM, x, 0:kept] * (gxx[h] + gyy[h] + gzz[h])
            twice = 2.0 * shear
            for f, change in (
                (SXX, twice * gxx[h] + volume),
                (SYY, twice * gyy[h] + volume),
                (SZZ, twice * gzz[h] + volume),
                (SXY, shear * gxy[h]),
                (SXZ, shear * gxz[h]),
                (SYZ, shear * gyz[h]),
            ):
                block[f, x, 0:kept] = block[f, x, 0:kept] + change

    def loop(first, last, body):
        def step(x, carry):
            body(x)
            return carry

        lax.fori_loop(HALO + first, HALO + last + 1, step, 0, unroll=True)

    loop(-5, cx + 3, velocity_layer)
    for copy in copies:
        copy.wait()
    site = spans_ref[1, 0]
    total_y, total_z = cy * grid.gy, cz * grid.gz
    site_x = lax.div(site, total_y * total_z) - lax.axis_index("gx") * cx
    site_y = lax.rem(lax.div(site, total_z), total_y) - lax.axis_index("gy") * cy
    site_z = lax.rem(site, total_z)
    near = jnp.logical_and(site_x >= -HALO, site_x < cx + HALO)
    near = jnp.logical_and(near, jnp.logical_and(site_y >= -ROWS, site_y < cy + ROWS))
    site_row = jnp.where(site_y < 0, site_y + rows, site_y)

    def inject(step):
        x = site_x + HALO
        row = pl.multiple_of(lax.div(site_row, ROWS) * ROWS, ROWS)
        here = jnp.logical_and(sub == lax.rem(site_row, ROWS), lane == lax.rem(site_z, cz))
        own = lax.div(site_z, cz) == half
        for mine, block in ((True, ext), (False, beside)):

            @pl.when(jnp.logical_and(near, own if mine else jnp.logical_not(own)))
            def _():
                amount = jnp.where(here, TIME_STEP * block[BUOY, x, pl.ds(row, ROWS), :], 0.0)
                for c in range(3):
                    block[VX + c, x, pl.ds(row, ROWS), :] = (
                        block[VX + c, x, pl.ds(row, ROWS), :] + amount * wavelet_ref[step, c]
                    )

    def strain_layer(step, x):
        lam = ext[LAM, x, 0:cy, :]
        shear = ext[MU, x, 0:cy, :]
        parts = [ext[f, x, 0:cy, :] for f in range(6)]
        shrink = lam / (3.0 * lam + 2.0 * shear) * (parts[0] + parts[1] + parts[2])
        inverse = 0.5 / shear
        for f in range(6):
            value = (parts[f] - shrink if f < 3 else parts[f]) * inverse
            head = value.astype(jnp.bfloat16)
            tail = (value - head.astype(jnp.float32)).astype(jnp.bfloat16)
            row = pl.multiple_of((6 * step + f) * cx * cy + (x - HALO) * cy, cy)
            sampled[pl.ds(row, cy), 0:cz] = head
            sampled[pl.ds(row, cy), cz : 2 * cz] = tail

    block = cx * cy

    def sample(k, carry):
        where = pl.ds(pl.multiple_of(k * SLOT_STEP, SLOT_STEP), SLOT_STEP)
        to_lanes = pl.ds(pl.multiple_of(k * SLOT_STEP + LANES, LANES), SLOT_STEP)
        row = rows_ref[:, where]
        marks = [row == r * ROWS + iota(0, (ROWS, SLOT_STEP)) for r in range(block // ROWS)]
        for part in range(6 * STEPS // PART):
            found = jnp.dot(
                sampled[part * PART * block : (part + 1) * PART * block, :],
                lanes_ref[:, where],
                preferred_element_type=jnp.float32,
            )
            for f in range(PART):
                acc = jnp.zeros((ROWS, SLOT_STEP), jnp.float32)
                for r in range(block // ROWS):
                    tile = found[f * block + r * ROWS : f * block + r * ROWS + ROWS]
                    acc = acc + jnp.where(marks[r], tile, 0.0)
                to = part * PART + f
                compact[to : to + 1, to_lanes] = jnp.sum(acc, axis=0, keepdims=True)
        return carry

    def spread():
        values = 6 * STEPS
        lanes_at = iota(1, (values, LANES))
        for t in range(width * capacity // LANES):
            out = jnp.zeros((values, LANES), jnp.float32)
            for w in range(t * LANES // capacity, -(-(t + 1) * LANES // capacity)):
                skip = t * LANES - w * capacity
                start = spans_ref[0, w] + skip + LANES
                base = pl.multiple_of(lax.div(start, LANES) * LANES, LANES)
                shift = lax.rem(start, LANES)
                near = pltpu.roll(compact[0:values, pl.ds(base, LANES)], LANES - shift, 1)
                far = pltpu.roll(compact[0:values, pl.ds(base + LANES, LANES)], LANES - shift, 1)
                place = lanes_at + skip
                mine = jnp.logical_and(place >= 0, place < spans_ref[ROWS, w])
                out = jnp.where(mine, jnp.where(lanes_at < LANES - shift, near, far), out)
            per = 256 // LANES
            table_out[t // per, :, t % per * LANES : (t % per + 1) * LANES] = out

    inject(0)
    loop(-3, cx + 2, stress_layer)
    loop(0, cx - 1, functools.partial(strain_layer, 0))
    loop(-2, cx, velocity_layer)
    inject(1)
    leaving = pltpu.make_async_copy(
        ext.at[VX : VX + 3, HALO : HALO + cx, 0:cy, :], velocity_out, sems.at[2]
    )
    leaving.start()
    loop(0, cx - 1, functools.partial(stress_layer, last=True))
    loop(0, cx - 1, functools.partial(strain_layer, 1))
    lax.fori_loop(0, lanes_ref.shape[1] // SLOT_STEP, sample, 0, unroll=True)
    spread()
    leaving.wait()


def per_device(
    velocity_start, stress_start, material, force_site, force_wavelet, save_cells, save_writer
):
    counts = tuple(lax.axis_size(axis) for axis in ("gx", "gy", "gz"))
    grid = Grid(velocity_start.shape[1:], counts)
    pieces = grid.pieces()
    params = pltpu.CompilerParams(vmem_limit_bytes=VMEM_LIMIT)
    own_tiles = FIELDS * grid.cx * grid.tiles_y
    fields = sum(
        lax.pad(part, jnp.float32(0.0), [(first, FIELDS - first - part.shape[0], 0)] + [(0, 0, 0)] * 3)
        for first, part in ((SXX, stress_start), (VX, velocity_start), (LAM, material))
    )
    packed = pl.pallas_call(
        lambda *refs: pack_kernel(grid, *refs),
        out_shape=[f32(*grid.shape(name)) for name, _ in pieces],
        in_specs=[VMEM],
        out_specs=[VMEM] * len(pieces),
        compiler_params=params,
        name="pack_halos",
    )(fields)
    swap = [(0, 1), (1, 0)]
    arrived = []
    for (name, _), piece in zip(pieces, packed):
        if name[0] == "x":
            arrived.append(lax.ppermute(piece, "gx", grid.pairs(grid.gx, name[1])))
        elif name[0] == "y":
            arrived.append(lax.ppermute(piece, "gy", grid.pairs(grid.gy, name[1])))
        else:
            pairs = [
                (a * grid.gy + b, c * grid.gy + d)
                for a, c in grid.pairs(grid.gx, name[1])
                for b, d in grid.pairs(grid.gy, name[2])
            ]
            arrived.append(lax.ppermute(piece, ("gx", "gy"), pairs))
    count = save_cells.size
    width = grid.gx * grid.gy
    capacity = max(2, 2 * count // width)
    slots = width * capacity
    lanes, rows, spans, force = pl.pallas_call(
        functools.partial(slot_kernel, width, grid.cz),
        out_shape=[
            jax.ShapeDtypeStruct((2 * grid.cz, count), jnp.bfloat16),
            jax.ShapeDtypeStruct((ROWS, count), jnp.int32),
            jax.ShapeDtypeStruct((2 * ROWS, max(LANES, width)), jnp.int32),
            f32(ROWS, LANES),
        ],
        in_specs=[VMEM] * 2 + [SMEM, VMEM],
        out_specs=[VMEM] * 4,
        compiler_params=params,
        cost_estimate=IDLE,
        name="slot_tables",
    )(save_cells.reshape(1, count), save_writer.reshape(1, count), force_site, force_wavelet)

    own_strips = pl.pallas_call(
        functools.partial(own_strip_kernel, grid),
        out_shape=f32(groups(own_tiles), ROWS, LANES),
        in_specs=[VMEM] * 2,
        out_specs=VMEM,
        compiler_params=params,
        cost_estimate=IDLE,
        name="pack_own_strips",
    )(rows, fields)

    extended = f32(FIELDS, grid.layers, grid.rows, grid.cz)
    block = pl.pallas_call(
        lambda *refs: begin_kernel(grid, *refs),
        out_shape=extended,
        in_specs=[VMEM],
        out_specs=VMEM,
        compiler_params=params,
        cost_estimate=IDLE,
        name="begin_block",
    )(fields)

    faces = len(grid.y_pairs) + len(grid.x_pairs)
    first_corner = groups(own_tiles) + sum(groups(c) for _, c in pieces[:faces])
    all_strips = f32(first_corner + sum(groups(c) for _, c in pieces[faces:]), ROWS, LANES)
    strips = pl.pallas_call(
        functools.partial(face_strip_kernel, grid, pieces[:faces]),
        out_shape=all_strips,
        in_specs=[VMEM] * (faces + 3),
        out_specs=VMEM,
        compiler_params=params,
        name="pack_face_strips",
    )(rows, block, own_strips, *arrived[:faces])
    strips = pl.pallas_call(
        lambda *refs: strip_kernel(grid, pieces[faces:], first_corner, refs[1:-1], refs[-1]),
        out_shape=all_strips,
        in_specs=[VMEM] * (1 + len(pieces) - faces),
        out_specs=VMEM,
        input_output_aliases={0: 0},
        compiler_params=params,
        name="pack_corner_strips",
    )(strips, *arrived[faces:])
    strips = lax.ppermute(strips, "gz", swap)

    block = pl.pallas_call(
        lambda *refs: assemble_kernel(grid, *refs),
        out_shape=extended,
        in_specs=[VMEM] * (1 + len(pieces)),
        out_specs=VMEM,
        input_output_aliases={0: 0},
        compiler_params=params,
        name="assemble",
    )(block, *arrived)

    _, velocity, table = pl.pallas_call(
        functools.partial(main_kernel, grid, width, capacity),
        out_shape=[
            extended,
            f32(*velocity_start.shape),
            f32(slots // 256, 6 * STEPS, 256),
        ],
        in_specs=[VMEM] * 6,
        out_specs=[VMEM, HBM, VMEM],
        scratch_shapes=[
            pltpu.VMEM(extended.shape, jnp.float32),
            pltpu.VMEM((STEPS * 6 * grid.cx * grid.cy, 2 * grid.cz), jnp.bfloat16),
            pltpu.VMEM((16, count + 4 * LANES), jnp.float32),
            pltpu.SMEM(force.shape, jnp.float32),
            pltpu.SMEM(spans.shape, jnp.int32),
            pltpu.SemaphoreType.DMA((3,)),
        ],
        input_output_aliases={0: 0},
        compiler_params=params,
        name="two_steps",
    )(block, strips, lanes, rows, spans, force)

    values = 6 * STEPS
    if capacity != 256:
        table = table.transpose(1, 0, 2).reshape(values, width, capacity).transpose(1, 0, 2)
    sent = lax.all_to_all(table, ("gx", "gy"), split_axis=0, concat_axis=0, tiled=True)
    return velocity, sent.transpose(1, 0, 2).reshape(1, values, slots)


def solution(mesh):
    in_specs = (
        P(None, ("runs", "gx"), "gy", "gz"),
        P(None, ("runs", "gx"), "gy", "gz"),
        P(None, ("runs", "gx"), "gy", "gz"),
        P("runs"),
        P("runs", None),
        P(("runs", "gx"), "gy", "gz", None),
        P(("runs", "gx"), "gy", "gz", None, None),
    )
    out_specs = (P(None, ("runs", "gx"), "gy", "gz"), P(("runs", "gz"), None, ("gx", "gy")))
    return jax.shard_map(
        per_device, mesh=mesh, in_specs=in_specs, out_specs=out_specs, check_vma=False
    )
```

```python
import functools

import jax
import jax.numpy as jnp
from jax import lax
from jax.experimental import pallas as pl
from jax.experimental.pallas import tpu as pltpu
from jax.sharding import PartitionSpec as P

STEPS = 2
TIME_STEP = 0.12

SXX, SYY, SZZ, SXY, SXZ, SYZ, VX, VY, VZ, LAM, MU, BUOY = range(12)
FIELDS = 12
DEPTHS = (6, 5, 5, 6, 6, 5, 5, 5, 5, 3, 3, 5)
OFFSETS = tuple(sum(DEPTHS[:f]) for f in range(FIELDS + 1))
HALO = 6
LAYERS = OFFSETS[-1]
ROWS = 8
STRIP = 8
LANES = 128
CORNER_ROWS = {f: (5, 5, 3, 2, 2) for f in (SXX, SYY, SXY, SXZ, SYZ)}
CORNER_ROWS.update({f: (3, 3, 2) for f in (SZZ, VX, VY, VZ, BUOY)})
CORNER_ROWS.update({f: (2, 2) for f in (LAM, MU)})


def corner_tiles():
    parts = [(n, f, d + 1) for f, counts in CORNER_ROWS.items() for d, n in enumerate(counts)]
    tiles = []
    for n, f, d in sorted(parts, reverse=True):
        for tile in tiles:
            used = sum(part[2] for part in tile)
            if used + n <= ROWS:
                tile.append((f, d, n, used))
                break
        else:
            tiles.append([(f, d, n, 0)])
    return tiles


CORNER_TILES = corner_tiles()
CORNERS = len(CORNER_TILES)
SLOT_STEP = 256
VMEM_LIMIT = 40 * 1024 * 1024
PART = 6
VMEM = pl.BlockSpec(memory_space=pltpu.VMEM)
HBM = pl.BlockSpec(memory_space=pltpu.HBM)
SMEM = pl.BlockSpec(memory_space=pltpu.SMEM)
IDLE = pl.CostEstimate(flops=0, bytes_accessed=0, transcendentals=0)


def f32(*shape):
    return jax.ShapeDtypeStruct(shape, jnp.float32)


def groups(count):
    return -(-count // (LANES // STRIP))


def iota(dimension, shape=(ROWS, LANES)):
    return lax.broadcasted_iota(jnp.int32, shape, dimension)


def pack_strips(tiles, head):
    slot = iota(1) // STRIP
    packed = None
    for at, tile in enumerate(tiles):
        turned = pltpu.roll(tile, (STRIP * at + head) & (LANES - 1), 1)
        packed = turned if packed is None else jnp.where(slot == at, turned, packed)
    within = iota(1) % STRIP
    first = jnp.where(head == 0, 0, STRIP - HALO)
    sent = jnp.logical_and(within >= first, within < first + HALO)
    return jnp.where(sent, packed, 0.0)


class Fields:
    def __init__(self, moving, material):
        self.parts = moving, material

    def __getitem__(self, key):
        if key[0] < LAM:
            return self.parts[0][key]
        return self.parts[1][(key[0] - LAM, *key[1:])]


class Grid:
    def __init__(self, block, counts):
        self.cx, self.cy, self.cz = block
        self.gx, self.gy, self.gz = counts
        self.x_pairs = ("odd", "even") if self.gx > 2 else ("even",)
        self.y_pairs = ("even", "odd") if self.gy > 2 else ("even",)
        self.rows = self.cy + ROWS * len(self.y_pairs)
        self.layers = self.cx + 2 * HALO
        self.tiles_y = self.cy // ROWS

    def pairs(self, count, kind):
        start = 0 if kind == "even" else 1
        out = []
        for i in range(start, count - 1, 2):
            out += [(i, i + 1), (i + 1, i)]
        return out

    def pieces(self):
        out = [(("y", b), FIELDS * self.cx) for b in self.y_pairs]
        out += [(("x", a), LAYERS * self.tiles_y) for a in self.x_pairs]
        out += [(("d", a, b), CORNERS) for b in self.y_pairs for a in self.x_pairs]
        return out

    def shape(self, name):
        if name[0] == "x":
            return (LAYERS, self.cy, self.cz)
        if name[0] == "y":
            return (FIELDS, self.cx, ROWS, self.cz)
        return (CORNERS, ROWS, self.cz)


def above(axis, kind):
    parity = lax.rem(lax.axis_index(axis), 2)
    return parity == (0 if kind == "even" else 1)


def pack_kernel(grid, *refs):
    fields = Fields(*refs[:2])
    outs = refs[2:]
    sub = iota(0)
    for (name, _), out in zip(grid.pieces(), outs):
        if name[0] == "x":
            high = above("gx", name[1])
            for f in range(FIELDS):
                n = DEPTHS[f]
                start = jnp.where(high, grid.cx - n, 0)
                out[OFFSETS[f] : OFFSETS[f + 1]] = fields[f, pl.ds(start, n)]
        elif name[0] == "y":
            row = pl.multiple_of(jnp.where(above("gy", name[1]), grid.cy - ROWS, 0), ROWS)
            for f in range(FIELDS):
                out[f] = fields[f, :, pl.ds(row, ROWS), :]
        else:
            high = above("gx", name[1])
            up = above("gy", name[2])
            row = pl.multiple_of(jnp.where(up, grid.cy - ROWS, 0), ROWS)

            def tile(field, distance):
                layer = jnp.where(high, grid.cx - distance, distance - 1)
                return fields[field, layer, pl.ds(row, ROWS), :]

            for i, parts in enumerate(CORNER_TILES):
                packed = None
                for f, d, n, first in parts:
                    whole = tile(f, d)
                    turned = jnp.where(
                        up,
                        pltpu.roll(whole, (first + n) % ROWS, 0),
                        pltpu.roll(whole, first, 0) if first else whole,
                    )
                    packed = turned if packed is None else jnp.where(sub < first, packed, turned)
                out[i] = packed


def own_strip_kernel(grid, after, moving, material, own):
    fields = Fields(moving, material)
    head = jnp.where(lax.axis_index("gz") == 0, STRIP, 0)
    tiles = [(f, x, r) for f in range(FIELDS) for x in range(grid.cx) for r in range(grid.tiles_y)]
    for g in range(groups(len(tiles))):
        part = []
        for f, x, r in tiles[16 * g : 16 * g + 16]:
            part.append(fields[f, x, ROWS * r : ROWS * r + ROWS, :])
        own[g] = pack_strips(part, head)


def piece_tile(name, ref, at, grid):
    if name[0] == "x":
        r = at % grid.tiles_y
        return ref[at // grid.tiles_y, ROWS * r : ROWS * r + ROWS, :]
    if name[0] == "y":
        return ref[at // grid.cx, at % grid.cx]
    return ref[at]


def strip_kernel(grid, pieces, base, refs, out):
    head = jnp.where(lax.axis_index("gz") == 0, STRIP, 0)
    for (name, count), ref in zip(pieces, refs):
        for g in range(groups(count)):
            tiles = [
                piece_tile(name, ref, at, grid) for at in range(16 * g, min(16 * g + 16, count))
            ]
            out[base + g] = pack_strips(tiles, head)
        base += groups(count)


def face_strip_kernel(grid, pieces, *refs):
    own, out = refs[2], refs[-1]
    out[0 : own.shape[0]] = own[...]
    strip_kernel(grid, pieces, own.shape[0], refs[3:-1], out)


def slot_kernel(
    width,
    cz,
    cells_ref,
    writers_ref,
    site_ref,
    wavelet_ref,
    lanes_ref,
    rows_ref,
    spans_ref,
    force_ref,
):
    force_ref[0 : wavelet_ref.shape[0], 0 : wavelet_ref.shape[1]] = wavelet_ref[...]
    count = cells_ref.shape[1]
    cells = cells_ref[...]
    writers = writers_ref[...]
    padded = max(LANES, width)
    writer = iota(0, (padded, count))
    named = (writer == writers).astype(jnp.float32)
    fewer = (writers < writer).astype(jnp.float32)
    earlier = (iota(0, (count, count)) < iota(1, (count, count))).astype(jnp.float32)
    before = jnp.dot(
        named.astype(jnp.bfloat16), earlier.astype(jnp.bfloat16), preferred_element_type=jnp.float32
    )
    start = jnp.sum(fewer, axis=1, keepdims=True)
    rank = jnp.sum((before + start) * named, axis=0, keepdims=True).astype(jnp.int32)
    ones = jnp.ones((16, count), jnp.bfloat16)

    def across(marks):
        return lax.dot_general(
            ones,
            marks.astype(jnp.bfloat16),
            (((1,), (1,)), ((), ())),
            preferred_element_type=jnp.float32,
        ).astype(jnp.int32)

    first = across(fewer)[0:ROWS]
    spans_ref[0:ROWS, :] = jnp.where(iota(0, first.shape) == 1, site_ref[0], first)
    spans_ref[ROWS : 2 * ROWS, :] = across(named)[0:ROWS]
    which = iota(0, (16, count))
    values = jnp.where(which == 0, lax.rem(cells, cz), jnp.where(which == 1, lax.div(cells, cz), 0))
    values = values.astype(jnp.float32).astype(jnp.bfloat16)
    for n in range(0, count, SLOT_STEP):
        hit = (iota(0, (SLOT_STEP, count)) + n == rank).astype(jnp.float32)
        table = lax.dot_general(
            values,
            hit.astype(jnp.bfloat16),
            (((1,), (1,)), ((), ())),
            preferred_element_type=jnp.float32,
        ).astype(jnp.int32)
        marks = (iota(0, (cz, SLOT_STEP)) == table[0:1]).astype(jnp.float32).astype(jnp.bfloat16)
        lanes_ref[0:cz, n : n + SLOT_STEP] = marks
        lanes_ref[cz : 2 * cz, n : n + SLOT_STEP] = marks
        rows_ref[:, n : n + SLOT_STEP] = jnp.broadcast_to(table[1:2], (ROWS, SLOT_STEP))


def edge(grid, up):
    if len(grid.y_pairs) > 1:
        return lambda tile: tile
    sub = iota(0)
    keep = jnp.logical_or(sub < jnp.where(up, 6, 0), sub >= jnp.where(up, 8, 2))
    return lambda tile: jnp.where(keep, tile, 0.0)


def halo_row(grid, up):
    if len(grid.y_pairs) == 1:
        return grid.cy
    return pl.multiple_of(jnp.where(up, grid.cy, grid.cy + ROWS), ROWS)


def lay_own(grid, ext, own):
    cx, cy = grid.cx, grid.cy
    for f in range(FIELDS):
        for x in list(range(HALO)) + list(range(HALO + cx, grid.layers)):
            for row in range(cy, grid.rows, ROWS):
                ext[f, x, row : row + ROWS, :] = jnp.zeros((ROWS, grid.cz), jnp.float32)
    at = 0
    for f in range(FIELDS):
        for x in range(cx):
            for r in range(grid.tiles_y):
                ext[f, HALO + x, ROWS * r : ROWS * r + ROWS, :] = own(at)
                at += 1


def lay_halos(grid, ext, arrived):
    cx, cy = grid.cx, grid.cy
    for (name, count), tile_of in zip(grid.pieces(), arrived):
        if name[0] == "x":
            high = above("gx", name[1])
            at = 0
            for f in range(FIELDS):
                start = jnp.where(high, HALO + cx, HALO - DEPTHS[f])
                for d in range(DEPTHS[f]):
                    for r in range(grid.tiles_y):
                        ext[f, start + d, ROWS * r : ROWS * r + ROWS, :] = tile_of(at)
                        at += 1
            continue
        up = above("gy", name[-1])
        clear = edge(grid, up)
        place = halo_row(grid, up)
        if name[0] == "y":
            for f in range(FIELDS):
                for x in range(cx):
                    ext[f, HALO + x, pl.ds(place, ROWS), :] = clear(tile_of(f * cx + x))
            continue
        high = above("gx", name[1])

        def put(field, distance, tile):
            layer = jnp.where(high, HALO + cx - 1 + distance, HALO - distance)
            ext[field, layer, pl.ds(place, ROWS), :] = clear(tile)

        for i, parts in enumerate(CORNER_TILES):
            tile = tile_of(i)
            for f, d, n, first in parts:
                turned = jnp.where(
                    up,
                    pltpu.roll(tile, ROWS - first, 0) if first else tile,
                    pltpu.roll(tile, (-first - n) % ROWS, 0),
                )
                put(f, d, turned)


def unpack(ref, base, at):
    lead = jnp.where(lax.axis_index("gz") == 0, 0, LANES - STRIP)
    return pltpu.roll(ref[base + at // 16], (lead - STRIP * (at % 16)) & (LANES - 1), 1)


def begin_kernel(grid, *refs):
    fields, ext = Fields(*refs[:2]), refs[2]

    def own(at):
        x, r = at // grid.tiles_y % grid.cx, at % grid.tiles_y
        return fields[at // (grid.tiles_y * grid.cx), x, ROWS * r : ROWS * r + ROWS, :]

    lay_own(grid, ext, own)


def assemble_kernel(grid, *refs):
    arrived, ext = refs[1:-1], refs[-1]
    tiles = [
        functools.partial(piece_tile, name, ref, grid=grid)
        for (name, _), ref in zip(grid.pieces(), arrived)
    ]
    lay_halos(grid, ext, tiles)


def main_kernel(grid, width, capacity, *refs):
    strips, lanes_ref, rows_ref, spans_vmem, force_vmem = refs[1:6]
    ext, velocity_out, table_out = refs[6:9]
    beside, sampled, compact, wavelet_ref, spans_ref, sems = refs[9:]
    copies = (
        pltpu.make_async_copy(force_vmem, wavelet_ref, sems.at[0]),
        pltpu.make_async_copy(spans_vmem, spans_ref, sems.at[1]),
    )
    for copy in copies:
        copy.start()
    rows = grid.rows
    cx, cy, cz = grid.cx, grid.cy, grid.cz
    half = lax.axis_index("gz")
    sub = iota(0)
    lane = iota(1)
    lay_own(grid, beside, functools.partial(unpack, strips, 0))
    bases = [groups(FIELDS * cx * grid.tiles_y)]
    for _, count in grid.pieces():
        bases.append(bases[-1] + groups(count))
    lay_halos(grid, beside, [functools.partial(unpack, strips, base) for base in bases[:-1]])
    lane_all = iota(1, (rows, cz))

    def pair(field, x):
        return ext[field, x], beside[field, x]

    def add(a, b):
        return a[0] + b[0], a[1] + b[1]

    def sub_(a, b):
        return a[0] - b[0], a[1] - b[1]

    def along_x(field, x):
        return (
            sub_(pair(field, x + 1), pair(field, x)),
            sub_(pair(field, x + 2), pair(field, x - 1)),
        )

    def moved_y(a, offset):
        return tuple(pltpu.roll(v, -offset % rows, 0) for v in a)

    def moved_z(a, offset):
        own = pltpu.roll(a[0], -offset % cz, 1)
        far = pltpu.roll(a[1], -offset % cz, 1)
        inside = lane_all[: own.shape[0]]
        inside = inside < cz - offset if offset > 0 else inside >= -offset
        return jnp.where(inside, own, far), jnp.where(inside, far, own)

    def forward(a, move):
        return sub_(move(a, 1), a), sub_(move(a, 2), move(a, -1))

    def backward(a, move):
        return sub_(a, move(a, -1)), sub_(move(a, 1), move(a, -2))

    def total(*terms):
        near, far = terms[0]
        for other_near, other_far in terms[1:]:
            near, far = add(near, other_near), add(far, other_far)
        return tuple(27.0 * p - q for p, q in zip(near, far))

    scale = TIME_STEP / 24.0

    def velocity_layer(x):
        y = x + 1
        sxy_x, sxz_x = pair(SXY, x), pair(SXZ, x)
        rate_x = total(along_x(SXX, x), backward(sxy_x, moved_y), backward(sxz_x, moved_z))
        syz = pair(SYZ, y)
        rate_y = total(
            along_x(SXY, y - 1), forward(pair(SYY, y), moved_y), backward(syz, moved_z)
        )
        rate_z = total(
            along_x(SXZ, y - 1), backward(syz, moved_y), forward(pair(SZZ, y), moved_z)
        )
        for h, block in enumerate((ext, beside)):
            b = scale * block[BUOY, x]
            block[VX, x] = block[VX, x] + b * rate_x[h]
            b = scale * block[BUOY, y]
            block[VY, y] = block[VY, y] + b * rate_y[h]
            block[VZ, y] = block[VZ, y] + b * rate_z[h]

    def stress_layer(x, last=False):
        kept = cy if last else rows

        def cut(a):
            return tuple(v[:kept] for v in a)

        def across_y(move, a):
            return tuple(cut(v) for v in move(a, moved_y))

        def along(move, a):
            return move(cut(a), moved_z)

        def beyond(field, at):
            return tuple(cut(v) for v in along_x(field, at))

        vx, vy, vz = pair(VX, x), pair(VY, x), pair(VZ, x)
        gxx = total(beyond(VX, x - 1))
        gyy = total(across_y(backward, vy))
        gzz = total(along(backward, vz))
        gxy = total(across_y(forward, vx), beyond(VY, x))
        gxz = total(along(forward, vx), beyond(VZ, x))
        gyz = total(along(forward, vy), across_y(forward, vz))
        for h, block in enumerate((ext,) if last else (ext, beside)):
            shear = scale * block[MU, x, 0:kept]
            volume = scale * block[LAM, x, 0:kept] * (gxx[h] + gyy[h] + gzz[h])
            twice = 2.0 * shear
            for f, change in (
                (SXX, twice * gxx[h] + volume),
                (SYY, twice * gyy[h] + volume),
                (SZZ, twice * gzz[h] + volume),
                (SXY, shear * gxy[h]),
                (SXZ, shear * gxz[h]),
                (SYZ, shear * gyz[h]),
            ):
                block[f, x, 0:kept] = block[f, x, 0:kept] + change

    def loop(first, last, body):
        def step(x, carry):
            body(x)
            return carry

        lax.fori_loop(HALO + first, HALO + last + 1, step, 0, unroll=True)

    loop(-5, cx + 3, velocity_layer)
    for copy in copies:
        copy.wait()
    site = spans_ref[1, 0]
    total_y, total_z = cy * grid.gy, cz * grid.gz
    site_x = lax.div(site, total_y * total_z) - lax.axis_index("gx") * cx
    site_y = lax.rem(lax.div(site, total_z), total_y) - lax.axis_index("gy") * cy
    site_z = lax.rem(site, total_z)
    near = jnp.logical_and(site_x >= -HALO, site_x < cx + HALO)
    near = jnp.logical_and(near, jnp.logical_and(site_y >= -ROWS, site_y < cy + ROWS))
    site_row = jnp.where(site_y < 0, site_y + rows, site_y)

    def inject(step):
        x = site_x + HALO
        row = pl.multiple_of(lax.div(site_row, ROWS) * ROWS, ROWS)
        here = jnp.logical_and(sub == lax.rem(site_row, ROWS), lane == lax.rem(site_z, cz))
        own = lax.div(site_z, cz) == half
        for mine, block in ((True, ext), (False, beside)):

            @pl.when(jnp.logical_and(near, own if mine else jnp.logical_not(own)))
            def _():
                amount = jnp.where(here, TIME_STEP * block[BUOY, x, pl.ds(row, ROWS), :], 0.0)
                for c in range(3):
                    block[VX + c, x, pl.ds(row, ROWS), :] = (
                        block[VX + c, x, pl.ds(row, ROWS), :] + amount * wavelet_ref[step, c]
                    )

    def strain_layer(step, x):
        lam = ext[LAM, x, 0:cy, :]
        shear = ext[MU, x, 0:cy, :]
        parts = [ext[f, x, 0:cy, :] for f in range(6)]
        shrink = lam / (3.0 * lam + 2.0 * shear) * (parts[0] + parts[1] + parts[2])
        inverse = 0.5 / shear
        for f in range(6):
            value = (parts[f] - shrink if f < 3 else parts[f]) * inverse
            head = value.astype(jnp.bfloat16)
            tail = (value - head.astype(jnp.float32)).astype(jnp.bfloat16)
            row = pl.multiple_of((6 * step + f) * cx * cy + (x - HALO) * cy, cy)
            sampled[pl.ds(row, cy), 0:cz] = head
            sampled[pl.ds(row, cy), cz : 2 * cz] = tail

    block = cx * cy

    def sample(k, carry):
        where = pl.ds(pl.multiple_of(k * SLOT_STEP, SLOT_STEP), SLOT_STEP)
        to_lanes = pl.ds(pl.multiple_of(k * SLOT_STEP + LANES, LANES), SLOT_STEP)
        row = rows_ref[:, where]
        marks = [row == r * ROWS + iota(0, (ROWS, SLOT_STEP)) for r in range(block // ROWS)]
        for part in range(6 * STEPS // PART):
            found = jnp.dot(
                sampled[part * PART * block : (part + 1) * PART * block, :],
                lanes_ref[:, where],
                preferred_element_type=jnp.float32,
            )
            for f in range(PART):
                acc = jnp.zeros((ROWS, SLOT_STEP), jnp.float32)
                for r in range(block // ROWS):
                    tile = found[f * block + r * ROWS : f * block + r * ROWS + ROWS]
                    acc = acc + jnp.where(marks[r], tile, 0.0)
                to = part * PART + f
                compact[to : to + 1, to_lanes] = jnp.sum(acc, axis=0, keepdims=True)
        return carry

    def spread():
        values = 6 * STEPS
        lanes_at = iota(1, (values, LANES))
        for t in range(width * capacity // LANES):
            out = jnp.zeros((values, LANES), jnp.float32)
            for w in range(t * LANES // capacity, -(-(t + 1) * LANES // capacity)):
                skip = t * LANES - w * capacity
                start = spans_ref[0, w] + skip + LANES
                base = pl.multiple_of(lax.div(start, LANES) * LANES, LANES)
                shift = lax.rem(start, LANES)
                near = pltpu.roll(compact[0:values, pl.ds(base, LANES)], LANES - shift, 1)
                far = pltpu.roll(compact[0:values, pl.ds(base + LANES, LANES)], LANES - shift, 1)
                place = lanes_at + skip
                mine = jnp.logical_and(place >= 0, place < spans_ref[ROWS, w])
                out = jnp.where(mine, jnp.where(lanes_at < LANES - shift, near, far), out)
            per = 256 // LANES
            table_out[t // per, :, t % per * LANES : (t % per + 1) * LANES] = out

    inject(0)
    loop(-3, cx + 2, stress_layer)
    loop(0, cx - 1, functools.partial(strain_layer, 0))
    loop(-2, cx, velocity_layer)
    inject(1)
    leaving = pltpu.make_async_copy(
        ext.at[VX : VX + 3, HALO : HALO + cx, 0:cy, :], velocity_out, sems.at[2]
    )
    leaving.start()
    loop(0, cx - 1, functools.partial(stress_layer, last=True))
    loop(0, cx - 1, functools.partial(strain_layer, 1))
    lax.fori_loop(0, lanes_ref.shape[1] // SLOT_STEP, sample, 0, unroll=True)
    spread()
    leaving.wait()


def per_device(
    velocity_start, stress_start, material, force_site, force_wavelet, save_cells, save_writer
):
    counts = tuple(lax.axis_size(axis) for axis in ("gx", "gy", "gz"))
    grid = Grid(velocity_start.shape[1:], counts)
    pieces = grid.pieces()
    params = pltpu.CompilerParams(vmem_limit_bytes=VMEM_LIMIT)
    own_tiles = FIELDS * grid.cx * grid.tiles_y
    fields = sum(
        lax.pad(part, jnp.float32(0.0), [(first, LAM - first - part.shape[0], 0)] + [(0, 0, 0)] * 3)
        for first, part in ((SXX, stress_start), (VX, velocity_start))
    )
    packed = pl.pallas_call(
        lambda *refs: pack_kernel(grid, *refs),
        out_shape=[f32(*grid.shape(name)) for name, _ in pieces],
        in_specs=[VMEM] * 2,
        out_specs=[VMEM] * len(pieces),
        compiler_params=params,
        name="pack_halos",
    )(fields, material)
    swap = [(0, 1), (1, 0)]
    arrived = []
    for (name, _), piece in zip(pieces, packed):
        if name[0] == "x":
            arrived.append(lax.ppermute(piece, "gx", grid.pairs(grid.gx, name[1])))
        elif name[0] == "y":
            arrived.append(lax.ppermute(piece, "gy", grid.pairs(grid.gy, name[1])))
        else:
            pairs = [
                (a * grid.gy + b, c * grid.gy + d)
                for a, c in grid.pairs(grid.gx, name[1])
                for b, d in grid.pairs(grid.gy, name[2])
            ]
            arrived.append(lax.ppermute(piece, ("gx", "gy"), pairs))
    count = save_cells.size
    width = grid.gx * grid.gy
    capacity = max(2, 2 * count // width)
    slots = width * capacity
    lanes, rows, spans, force = pl.pallas_call(
        functools.partial(slot_kernel, width, grid.cz),
        out_shape=[
            jax.ShapeDtypeStruct((2 * grid.cz, count), jnp.bfloat16),
            jax.ShapeDtypeStruct((ROWS, count), jnp.int32),
            jax.ShapeDtypeStruct((2 * ROWS, max(LANES, width)), jnp.int32),
            f32(ROWS, LANES),
        ],
        in_specs=[VMEM] * 2 + [SMEM, VMEM],
        out_specs=[VMEM] * 4,
        compiler_params=params,
        cost_estimate=IDLE,
        name="slot_tables",
    )(save_cells.reshape(1, count), save_writer.reshape(1, count), force_site, force_wavelet)

    own_strips = pl.pallas_call(
        functools.partial(own_strip_kernel, grid),
        out_shape=f32(groups(own_tiles), ROWS, LANES),
        in_specs=[VMEM] * 3,
        out_specs=VMEM,
        compiler_params=params,
        cost_estimate=IDLE,
        name="pack_own_strips",
    )(rows, fields, material)

    extended = f32(FIELDS, grid.layers, grid.rows, grid.cz)
    block = pl.pallas_call(
        lambda *refs: begin_kernel(grid, *refs),
        out_shape=extended,
        in_specs=[VMEM] * 2,
        out_specs=VMEM,
        compiler_params=params,
        cost_estimate=IDLE,
        name="begin_block",
    )(fields, material)

    faces = len(grid.y_pairs) + len(grid.x_pairs)
    first_corner = groups(own_tiles) + sum(groups(c) for _, c in pieces[:faces])
    all_strips = f32(first_corner + sum(groups(c) for _, c in pieces[faces:]), ROWS, LANES)
    strips = pl.pallas_call(
        functools.partial(face_strip_kernel, grid, pieces[:faces]),
        out_shape=all_strips,
        in_specs=[VMEM] * (faces + 3),
        out_specs=VMEM,
        compiler_params=params,
        name="pack_face_strips",
    )(rows, block, own_strips, *arrived[:faces])
    strips = pl.pallas_call(
        lambda *refs: strip_kernel(grid, pieces[faces:], first_corner, refs[1:-1], refs[-1]),
        out_shape=all_strips,
        in_specs=[VMEM] * (1 + len(pieces) - faces),
        out_specs=VMEM,
        input_output_aliases={0: 0},
        compiler_params=params,
        name="pack_corner_strips",
    )(strips, *arrived[faces:])
    strips = lax.ppermute(strips, "gz", swap)

    block = pl.pallas_call(
        lambda *refs: assemble_kernel(grid, *refs),
        out_shape=extended,
        in_specs=[VMEM] * (1 + len(pieces)),
        out_specs=VMEM,
        input_output_aliases={0: 0},
        compiler_params=params,
        name="assemble",
    )(block, *arrived)

    _, velocity, table = pl.pallas_call(
        functools.partial(main_kernel, grid, width, capacity),
        out_shape=[
            extended,
            f32(*velocity_start.shape),
            f32(slots // 256, 6 * STEPS, 256),
        ],
        in_specs=[VMEM] * 6,
        out_specs=[VMEM, HBM, VMEM],
        scratch_shapes=[
            pltpu.VMEM(extended.shape, jnp.float32),
            pltpu.VMEM((STEPS * 6 * grid.cx * grid.cy, 2 * grid.cz), jnp.bfloat16),
            pltpu.VMEM((16, count + 4 * LANES), jnp.float32),
            pltpu.SMEM(force.shape, jnp.float32),
            pltpu.SMEM(spans.shape, jnp.int32),
            pltpu.SemaphoreType.DMA((3,)),
        ],
        input_output_aliases={0: 0},
        compiler_params=params,
        name="two_steps",
    )(block, strips, lanes, rows, spans, force)

    values = 6 * STEPS
    if capacity != 256:
        table = table.transpose(1, 0, 2).reshape(values, width, capacity).transpose(1, 0, 2)
    sent = lax.all_to_all(table, ("gx", "gy"), split_axis=0, concat_axis=0, tiled=True)
    return velocity, sent.transpose(1, 0, 2).reshape(1, values, slots)


def solution(mesh):
    in_specs = (
        P(None, ("runs", "gx"), "gy", "gz"),
        P(None, ("runs", "gx"), "gy", "gz"),
        P(None, ("runs", "gx"), "gy", "gz"),
        P("runs"),
        P("runs", None),
        P(("runs", "gx"), "gy", "gz", None),
        P(("runs", "gx"), "gy", "gz", None, None),
    )
    out_specs = (P(None, ("runs", "gx"), "gy", "gz"), P(("runs", "gz"), None, ("gx", "gy")))
    return jax.shard_map(
        per_device, mesh=mesh, in_specs=in_specs, out_specs=out_specs, check_vma=False
    )
```

```python
import functools

import jax
import jax.numpy as jnp
from jax import lax
from jax.experimental import pallas as pl
from jax.experimental.pallas import tpu as pltpu
from jax.sharding import PartitionSpec as P

STEPS = 2
TIME_STEP = 0.12

SXX, SYY, SZZ, SXY, SXZ, SYZ, VX, VY, VZ, LAM, MU, BUOY = range(12)
FIELDS = 12
DEPTHS = (6, 5, 5, 6, 6, 5, 5, 5, 5, 3, 3, 5)
OFFSETS = tuple(sum(DEPTHS[:f]) for f in range(FIELDS + 1))
HALO = 6
LAYERS = OFFSETS[-1]
ROWS = 8
STRIP = 8
LANES = 128
CORNER_ROWS = {f: (5, 5, 3, 2, 2) for f in (SXX, SYY, SXY, SXZ, SYZ)}
CORNER_ROWS.update({f: (3, 3, 2) for f in (SZZ, VX, VY, VZ, BUOY)})
CORNER_ROWS.update({f: (2, 2) for f in (LAM, MU)})


def corner_tiles():
    parts = [(n, f, d + 1) for f, counts in CORNER_ROWS.items() for d, n in enumerate(counts)]
    tiles = []
    for n, f, d in sorted(parts, reverse=True):
        for tile in tiles:
            used = sum(part[2] for part in tile)
            if used + n <= ROWS:
                tile.append((f, d, n, used))
                break
        else:
            tiles.append([(f, d, n, 0)])
    return tiles


CORNER_TILES = corner_tiles()
CORNERS = len(CORNER_TILES)
SLOT_STEP = 256
VMEM_LIMIT = 40 * 1024 * 1024
PART = 6
VMEM = pl.BlockSpec(memory_space=pltpu.VMEM)
HBM = pl.BlockSpec(memory_space=pltpu.HBM)
SMEM = pl.BlockSpec(memory_space=pltpu.SMEM)
IDLE = pl.CostEstimate(flops=0, bytes_accessed=0, transcendentals=0)


def f32(*shape):
    return jax.ShapeDtypeStruct(shape, jnp.float32)


def groups(count):
    return -(-count // (LANES // STRIP))


def iota(dimension, shape=(ROWS, LANES)):
    return lax.broadcasted_iota(jnp.int32, shape, dimension)


def pack_strips(tiles, head):
    slot = iota(1) // STRIP
    packed = None
    for at, tile in enumerate(tiles):
        turned = pltpu.roll(tile, (STRIP * at + head) & (LANES - 1), 1)
        packed = turned if packed is None else jnp.where(slot == at, turned, packed)
    within = iota(1) % STRIP
    first = jnp.where(head == 0, 0, STRIP - HALO)
    sent = jnp.logical_and(within >= first, within < first + HALO)
    return jnp.where(sent, packed, 0.0)


class Grid:
    def __init__(self, block, counts):
        self.cx, self.cy, self.cz = block
        self.gx, self.gy, self.gz = counts
        self.x_pairs = ("odd", "even") if self.gx > 2 else ("even",)
        self.y_pairs = ("even", "odd") if self.gy > 2 else ("even",)
        self.rows = self.cy + ROWS * len(self.y_pairs)
        self.layers = self.cx + 2 * HALO
        self.tiles_y = self.cy // ROWS

    def pairs(self, count, kind):
        start = 0 if kind == "even" else 1
        out = []
        for i in range(start, count - 1, 2):
            out += [(i, i + 1), (i + 1, i)]
        return out

    def pieces(self):
        out = [(("y", b), FIELDS * self.cx) for b in self.y_pairs]
        out += [(("x", a), LAYERS * self.tiles_y) for a in self.x_pairs]
        out += [(("d", a, b), CORNERS) for b in self.y_pairs for a in self.x_pairs]
        return out

    def shape(self, name):
        if name[0] == "x":
            return (LAYERS, self.cy, self.cz)
        if name[0] == "y":
            return (FIELDS, self.cx, ROWS, self.cz)
        return (CORNERS, ROWS, self.cz)


def above(axis, kind):
    parity = lax.rem(lax.axis_index(axis), 2)
    return parity == (0 if kind == "even" else 1)


def pack_kernel(grid, *refs):
    fields = refs[0]
    outs = refs[1:]
    sub = iota(0)
    for (name, _), out in zip(grid.pieces(), outs):
        if name[0] == "x":
            high = above("gx", name[1])
            for f in range(FIELDS):
                n = DEPTHS[f]
                start = jnp.where(high, grid.cx - n, 0)
                out[OFFSETS[f] : OFFSETS[f + 1]] = fields[f, pl.ds(start, n)]
        elif name[0] == "y":
            row = pl.multiple_of(jnp.where(above("gy", name[1]), grid.cy - ROWS, 0), ROWS)
            for f in range(FIELDS):
                out[f] = fields[f, :, pl.ds(row, ROWS), :]
        else:
            high = above("gx", name[1])
            up = above("gy", name[2])
            row = pl.multiple_of(jnp.where(up, grid.cy - ROWS, 0), ROWS)

            def tile(field, distance):
                layer = jnp.where(high, grid.cx - distance, distance - 1)
                return fields[field, layer, pl.ds(row, ROWS), :]

            for i, parts in enumerate(CORNER_TILES):
                packed = None
                for f, d, n, first in parts:
                    whole = tile(f, d)
                    turned = jnp.where(
                        up,
                        pltpu.roll(whole, (first + n) % ROWS, 0),
                        pltpu.roll(whole, first, 0) if first else whole,
                    )
                    packed = turned if packed is None else jnp.where(sub < first, packed, turned)
                out[i] = packed


def own_strip_kernel(grid, after, fields, own):
    head = jnp.where(lax.axis_index("gz") == 0, STRIP, 0)
    tiles = [(f, x, r) for f in range(FIELDS) for x in range(grid.cx) for r in range(grid.tiles_y)]
    for g in range(groups(len(tiles))):
        part = []
        for f, x, r in tiles[16 * g : 16 * g + 16]:
            part.append(fields[f, x, ROWS * r : ROWS * r + ROWS, :])
        own[g] = pack_strips(part, head)


def piece_tile(name, ref, at, grid):
    if name[0] == "x":
        r = at % grid.tiles_y
        return ref[at // grid.tiles_y, ROWS * r : ROWS * r + ROWS, :]
    if name[0] == "y":
        return ref[at // grid.cx, at % grid.cx]
    return ref[at]


def strip_kernel(grid, pieces, base, refs, out):
    head = jnp.where(lax.axis_index("gz") == 0, STRIP, 0)
    for (name, count), ref in zip(pieces, refs):
        for g in range(groups(count)):
            tiles = [
                piece_tile(name, ref, at, grid) for at in range(16 * g, min(16 * g + 16, count))
            ]
            out[base + g] = pack_strips(tiles, head)
        base += groups(count)


def face_strip_kernel(grid, pieces, *refs):
    own, out = refs[2], refs[-1]
    out[0 : own.shape[0]] = own[...]
    strip_kernel(grid, pieces, own.shape[0], refs[3:-1], out)


def slot_kernel(
    width,
    cz,
    cells_ref,
    writers_ref,
    site_ref,
    wavelet_ref,
    lanes_ref,
    rows_ref,
    spans_ref,
    force_ref,
):
    force_ref[0 : wavelet_ref.shape[0], 0 : wavelet_ref.shape[1]] = wavelet_ref[...]
    count = cells_ref.shape[1]
    cells = cells_ref[...]
    writers = writers_ref[...]
    padded = max(LANES, width)
    writer = iota(0, (padded, count))
    named = (writer == writers).astype(jnp.float32)
    fewer = (writers < writer).astype(jnp.float32)
    earlier = (iota(0, (count, count)) < iota(1, (count, count))).astype(jnp.float32)
    before = jnp.dot(
        named.astype(jnp.bfloat16), earlier.astype(jnp.bfloat16), preferred_element_type=jnp.float32
    )
    start = jnp.sum(fewer, axis=1, keepdims=True)
    rank = jnp.sum((before + start) * named, axis=0, keepdims=True).astype(jnp.int32)
    ones = jnp.ones((16, count), jnp.bfloat16)

    def across(marks):
        return lax.dot_general(
            ones,
            marks.astype(jnp.bfloat16),
            (((1,), (1,)), ((), ())),
            preferred_element_type=jnp.float32,
        ).astype(jnp.int32)

    first = across(fewer)[0:ROWS]
    spans_ref[0:ROWS, :] = jnp.where(iota(0, first.shape) == 1, site_ref[0], first)
    spans_ref[ROWS : 2 * ROWS, :] = across(named)[0:ROWS]
    which = iota(0, (16, count))
    values = jnp.where(which == 0, lax.rem(cells, cz), jnp.where(which == 1, lax.div(cells, cz), 0))
    values = values.astype(jnp.float32).astype(jnp.bfloat16)
    for n in range(0, count, SLOT_STEP):
        hit = (iota(0, (SLOT_STEP, count)) + n == rank).astype(jnp.float32)
        table = lax.dot_general(
            values,
            hit.astype(jnp.bfloat16),
            (((1,), (1,)), ((), ())),
            preferred_element_type=jnp.float32,
        ).astype(jnp.int32)
        marks = (iota(0, (cz, SLOT_STEP)) == table[0:1]).astype(jnp.float32).astype(jnp.bfloat16)
        lanes_ref[0:cz, n : n + SLOT_STEP] = marks
        lanes_ref[cz : 2 * cz, n : n + SLOT_STEP] = marks
        rows_ref[:, n : n + SLOT_STEP] = jnp.broadcast_to(table[1:2], (ROWS, SLOT_STEP))


def edge(grid, up):
    if len(grid.y_pairs) > 1:
        return lambda tile: tile
    sub = iota(0)
    keep = jnp.logical_or(sub < jnp.where(up, 6, 0), sub >= jnp.where(up, 8, 2))
    return lambda tile: jnp.where(keep, tile, 0.0)


def halo_row(grid, up):
    if len(grid.y_pairs) == 1:
        return grid.cy
    return pl.multiple_of(jnp.where(up, grid.cy, grid.cy + ROWS), ROWS)


def lay_own(grid, ext, own):
    cx, cy = grid.cx, grid.cy
    for f in range(FIELDS):
        for x in list(range(HALO)) + list(range(HALO + cx, grid.layers)):
            for row in range(cy, grid.rows, ROWS):
                ext[f, x, row : row + ROWS, :] = jnp.zeros((ROWS, grid.cz), jnp.float32)
    at = 0
    for f in range(FIELDS):
        for x in range(cx):
            for r in range(grid.tiles_y):
                ext[f, HALO + x, ROWS * r : ROWS * r + ROWS, :] = own(at)
                at += 1


def lay_halos(grid, ext, arrived):
    cx, cy = grid.cx, grid.cy
    for (name, count), tile_of in zip(grid.pieces(), arrived):
        if name[0] == "x":
            high = above("gx", name[1])
            at = 0
            for f in range(FIELDS):
                start = jnp.where(high, HALO + cx, HALO - DEPTHS[f])
                for d in range(DEPTHS[f]):
                    for r in range(grid.tiles_y):
                        ext[f, start + d, ROWS * r : ROWS * r + ROWS, :] = tile_of(at)
                        at += 1
            continue
        up = above("gy", name[-1])
        clear = edge(grid, up)
        place = halo_row(grid, up)
        if name[0] == "y":
            for f in range(FIELDS):
                for x in range(cx):
                    ext[f, HALO + x, pl.ds(place, ROWS), :] = clear(tile_of(f * cx + x))
            continue
        high = above("gx", name[1])

        def put(field, distance, tile):
            layer = jnp.where(high, HALO + cx - 1 + distance, HALO - distance)
            ext[field, layer, pl.ds(place, ROWS), :] = clear(tile)

        for i, parts in enumerate(CORNER_TILES):
            tile = tile_of(i)
            for f, d, n, first in parts:
                turned = jnp.where(
                    up,
                    pltpu.roll(tile, ROWS - first, 0) if first else tile,
                    pltpu.roll(tile, (-first - n) % ROWS, 0),
                )
                put(f, d, turned)


def unpack(ref, base, at):
    lead = jnp.where(lax.axis_index("gz") == 0, 0, LANES - STRIP)
    return pltpu.roll(ref[base + at // 16], (lead - STRIP * (at % 16)) & (LANES - 1), 1)


def begin_kernel(grid, *refs):
    fields, ext = refs

    def own(at):
        x, r = at // grid.tiles_y % grid.cx, at % grid.tiles_y
        return fields[at // (grid.tiles_y * grid.cx), x, ROWS * r : ROWS * r + ROWS, :]

    lay_own(grid, ext, own)


def assemble_kernel(grid, *refs):
    arrived, ext = refs[1:-1], refs[-1]
    tiles = [
        functools.partial(piece_tile, name, ref, grid=grid)
        for (name, _), ref in zip(grid.pieces(), arrived)
    ]
    lay_halos(grid, ext, tiles)


def main_kernel(grid, width, capacity, *refs):
    strips, lanes_ref, rows_ref, spans_vmem, force_vmem = refs[1:6]
    ext, velocity_out, table_out = refs[6:9]
    beside, sampled, compact, wavelet_ref, spans_ref, sems = refs[9:]
    copies = (
        pltpu.make_async_copy(force_vmem, wavelet_ref, sems.at[0]),
        pltpu.make_async_copy(spans_vmem, spans_ref, sems.at[1]),
    )
    for copy in copies:
        copy.start()
    rows = grid.rows
    cx, cy, cz = grid.cx, grid.cy, grid.cz
    half = lax.axis_index("gz")
    sub = iota(0)
    lane = iota(1)
    lay_own(grid, beside, functools.partial(unpack, strips, 0))
    bases = [groups(FIELDS * cx * grid.tiles_y)]
    for _, count in grid.pieces():
        bases.append(bases[-1] + groups(count))
    lay_halos(grid, beside, [functools.partial(unpack, strips, base) for base in bases[:-1]])
    lane_all = iota(1, (rows, cz))

    def pair(field, x):
        return ext[field, x], beside[field, x]

    def add(a, b):
        return a[0] + b[0], a[1] + b[1]

    def sub_(a, b):
        return a[0] - b[0], a[1] - b[1]

    def along_x(field, x):
        return (
            sub_(pair(field, x + 1), pair(field, x)),
            sub_(pair(field, x + 2), pair(field, x - 1)),
        )

    def moved_y(a, offset):
        return tuple(pltpu.roll(v, -offset % rows, 0) for v in a)

    def moved_z(a, offset):
        own = pltpu.roll(a[0], -offset % cz, 1)
        far = pltpu.roll(a[1], -offset % cz, 1)
        inside = lane_all[: own.shape[0]]
        inside = inside < cz - offset if offset > 0 else inside >= -offset
        return jnp.where(inside, own, far), jnp.where(inside, far, own)

    def forward(a, move):
        return sub_(move(a, 1), a), sub_(move(a, 2), move(a, -1))

    def backward(a, move):
        return sub_(a, move(a, -1)), sub_(move(a, 1), move(a, -2))

    def total(*terms):
        near, far = terms[0]
        for other_near, other_far in terms[1:]:
            near, far = add(near, other_near), add(far, other_far)
        return tuple(27.0 * p - q for p, q in zip(near, far))

    scale = TIME_STEP / 24.0

    def velocity_layer(x):
        y = x + 1
        sxy_x, sxz_x = pair(SXY, x), pair(SXZ, x)
        rate_x = total(along_x(SXX, x), backward(sxy_x, moved_y), backward(sxz_x, moved_z))
        syz = pair(SYZ, y)
        rate_y = total(
            along_x(SXY, y - 1), forward(pair(SYY, y), moved_y), backward(syz, moved_z)
        )
        rate_z = total(
            along_x(SXZ, y - 1), backward(syz, moved_y), forward(pair(SZZ, y), moved_z)
        )
        for h, block in enumerate((ext, beside)):
            b = scale * block[BUOY, x]
            block[VX, x] = block[VX, x] + b * rate_x[h]
            b = scale * block[BUOY, y]
            block[VY, y] = block[VY, y] + b * rate_y[h]
            block[VZ, y] = block[VZ, y] + b * rate_z[h]

    def stress_layer(x, last=False):
        kept = cy if last else rows

        def cut(a):
            return tuple(v[:kept] for v in a)

        def across_y(move, a):
            return tuple(cut(v) for v in move(a, moved_y))

        def along(move, a):
            return move(cut(a), moved_z)

        def beyond(field, at):
            return tuple(cut(v) for v in along_x(field, at))

        vx, vy, vz = pair(VX, x), pair(VY, x), pair(VZ, x)
        gxx = total(beyond(VX, x - 1))
        gyy = total(across_y(backward, vy))
        gzz = total(along(backward, vz))
        gxy = total(across_y(forward, vx), beyond(VY, x))
        gxz = total(along(forward, vx), beyond(VZ, x))
        gyz = total(along(forward, vy), across_y(forward, vz))
        for h, block in enumerate((ext,) if last else (ext, beside)):
            shear = scale * block[MU, x, 0:kept]
            volume = scale * block[LAM, x, 0:kept] * (gxx[h] + gyy[h] + gzz[h])
            twice = 2.0 * shear
            for f, change in (
                (SXX, twice * gxx[h] + volume),
                (SYY, twice * gyy[h] + volume),
                (SZZ, twice * gzz[h] + volume),
                (SXY, shear * gxy[h]),
                (SXZ, shear * gxz[h]),
                (SYZ, shear * gyz[h]),
            ):
                block[f, x, 0:kept] = block[f, x, 0:kept] + change

    def loop(first, last, body):
        def step(x, carry):
            body(x)
            return carry

        lax.fori_loop(HALO + first, HALO + last + 1, step, 0, unroll=True)

    loop(-5, cx + 3, velocity_layer)
    for copy in copies:
        copy.wait()
    site = spans_ref[1, 0]
    total_y, total_z = cy * grid.gy, cz * grid.gz
    site_x = lax.div(site, total_y * total_z) - lax.axis_index("gx") * cx
    site_y = lax.rem(lax.div(site, total_z), total_y) - lax.axis_index("gy") * cy
    site_z = lax.rem(site, total_z)
    near = jnp.logical_and(site_x >= -HALO, site_x < cx + HALO)
    near = jnp.logical_and(near, jnp.logical_and(site_y >= -ROWS, site_y < cy + ROWS))
    site_row = jnp.where(site_y < 0, site_y + rows, site_y)

    def inject(step):
        x = site_x + HALO
        row = pl.multiple_of(lax.div(site_row, ROWS) * ROWS, ROWS)
        here = jnp.logical_and(sub == lax.rem(site_row, ROWS), lane == lax.rem(site_z, cz))
        own = lax.div(site_z, cz) == half
        for mine, block in ((True, ext), (False, beside)):

            @pl.when(jnp.logical_and(near, own if mine else jnp.logical_not(own)))
            def _():
                amount = jnp.where(here, TIME_STEP * block[BUOY, x, pl.ds(row, ROWS), :], 0.0)
                for c in range(3):
                    block[VX + c, x, pl.ds(row, ROWS), :] = (
                        block[VX + c, x, pl.ds(row, ROWS), :] + amount * wavelet_ref[step, c]
                    )

    def strain_layer(step, x):
        lam = ext[LAM, x, 0:cy, :]
        shear = ext[MU, x, 0:cy, :]
        parts = [ext[f, x, 0:cy, :] for f in range(6)]
        shrink = lam / (3.0 * lam + 2.0 * shear) * (parts[0] + parts[1] + parts[2])
        inverse = 0.5 / shear
        for f in range(6):
            value = (parts[f] - shrink if f < 3 else parts[f]) * inverse
            head = value.astype(jnp.bfloat16)
            tail = (value - head.astype(jnp.float32)).astype(jnp.bfloat16)
            row = pl.multiple_of((6 * step + f) * cx * cy + (x - HALO) * cy, cy)
            sampled[pl.ds(row, cy), 0:cz] = head
            sampled[pl.ds(row, cy), cz : 2 * cz] = tail

    block = cx * cy

    def sample(k, carry):
        where = pl.ds(pl.multiple_of(k * SLOT_STEP, SLOT_STEP), SLOT_STEP)
        to_lanes = pl.ds(pl.multiple_of(k * SLOT_STEP + LANES, LANES), SLOT_STEP)
        row = rows_ref[:, where]
        marks = [row == r * ROWS + iota(0, (ROWS, SLOT_STEP)) for r in range(block // ROWS)]
        for part in range(6 * STEPS // PART):
            found = jnp.dot(
                sampled[part * PART * block : (part + 1) * PART * block, :],
                lanes_ref[:, where],
                preferred_element_type=jnp.float32,
            )
            for f in range(PART):
                acc = jnp.zeros((ROWS, SLOT_STEP), jnp.float32)
                for r in range(block // ROWS):
                    tile = found[f * block + r * ROWS : f * block + r * ROWS + ROWS]
                    acc = acc + jnp.where(marks[r], tile, 0.0)
                to = part * PART + f
                compact[to : to + 1, to_lanes] = jnp.sum(acc, axis=0, keepdims=True)
        return carry

    def spread():
        values = 6 * STEPS
        lanes_at = iota(1, (values, LANES))
        for t in range(width * capacity // LANES):
            out = jnp.zeros((values, LANES), jnp.float32)
            for w in range(t * LANES // capacity, -(-(t + 1) * LANES // capacity)):
                skip = t * LANES - w * capacity
                start = spans_ref[0, w] + skip + LANES
                base = pl.multiple_of(lax.div(start, LANES) * LANES, LANES)
                shift = lax.rem(start, LANES)
                near = pltpu.roll(compact[0:values, pl.ds(base, LANES)], LANES - shift, 1)
                far = pltpu.roll(compact[0:values, pl.ds(base + LANES, LANES)], LANES - shift, 1)
                place = lanes_at + skip
                mine = jnp.logical_and(place >= 0, place < spans_ref[ROWS, w])
                out = jnp.where(mine, jnp.where(lanes_at < LANES - shift, near, far), out)
            per = 256 // LANES
            table_out[t // per, :, t % per * LANES : (t % per + 1) * LANES] = out

    inject(0)
    loop(-3, cx + 2, stress_layer)
    loop(0, cx - 1, functools.partial(strain_layer, 0))
    loop(-2, cx, velocity_layer)
    inject(1)
    leaving = pltpu.make_async_copy(
        ext.at[VX : VX + 3, HALO : HALO + cx, 0:cy, :], velocity_out, sems.at[2]
    )
    leaving.start()
    loop(0, cx - 1, functools.partial(stress_layer, last=True))
    loop(0, cx - 1, functools.partial(strain_layer, 1))
    lax.fori_loop(0, lanes_ref.shape[1] // SLOT_STEP, sample, 0, unroll=True)
    spread()
    leaving.wait()


def per_device(
    velocity_start, stress_start, material, force_site, force_wavelet, save_cells, save_writer
):
    counts = tuple(lax.axis_size(axis) for axis in ("gx", "gy", "gz"))
    grid = Grid(velocity_start.shape[1:], counts)
    pieces = grid.pieces()
    params = pltpu.CompilerParams(vmem_limit_bytes=VMEM_LIMIT)
    own_tiles = FIELDS * grid.cx * grid.tiles_y
    fields = sum(
        lax.pad(part, jnp.float32(0.0), [(first, FIELDS - first - part.shape[0], 0)] + [(0, 0, 0)] * 3)
        for first, part in ((SXX, stress_start), (VX, velocity_start), (LAM, material))
    )
    packed = pl.pallas_call(
        lambda *refs: pack_kernel(grid, *refs),
        out_shape=[f32(*grid.shape(name)) for name, _ in pieces],
        in_specs=[VMEM],
        out_specs=[VMEM] * len(pieces),
        compiler_params=params,
        name="pack_halos",
    )(fields)
    swap = [(0, 1), (1, 0)]
    arrived = []
    for (name, _), piece in zip(pieces, packed):
        if name[0] == "x":
            arrived.append(lax.ppermute(piece, "gx", grid.pairs(grid.gx, name[1])))
        elif name[0] == "y":
            arrived.append(lax.ppermute(piece, "gy", grid.pairs(grid.gy, name[1])))
        else:
            pairs = [
                (a * grid.gy + b, c * grid.gy + d)
                for a, c in grid.pairs(grid.gx, name[1])
                for b, d in grid.pairs(grid.gy, name[2])
            ]
            arrived.append(lax.ppermute(piece, ("gx", "gy"), pairs))
    count = save_cells.size
    width = grid.gx * grid.gy
    capacity = max(2, 2 * count // width)
    slots = width * capacity
    lanes, rows, spans, force = pl.pallas_call(
        functools.partial(slot_kernel, width, grid.cz),
        out_shape=[
            jax.ShapeDtypeStruct((2 * grid.cz, count), jnp.bfloat16),
            jax.ShapeDtypeStruct((ROWS, count), jnp.int32),
            jax.ShapeDtypeStruct((2 * ROWS, max(LANES, width)), jnp.int32),
            f32(ROWS, LANES),
        ],
        in_specs=[VMEM] * 2 + [SMEM, VMEM],
        out_specs=[VMEM] * 4,
        compiler_params=params,
        cost_estimate=IDLE,
        name="slot_tables",
    )(save_cells.reshape(1, count), save_writer.reshape(1, count), force_site, force_wavelet)

    own_strips = pl.pallas_call(
        functools.partial(own_strip_kernel, grid),
        out_shape=f32(groups(own_tiles), ROWS, LANES),
        in_specs=[VMEM] * 2,
        out_specs=VMEM,
        compiler_params=params,
        cost_estimate=IDLE,
        name="pack_own_strips",
    )(rows, fields)

    extended = f32(FIELDS, grid.layers, grid.rows, grid.cz)
    block = pl.pallas_call(
        lambda *refs: begin_kernel(grid, *refs),
        out_shape=extended,
        in_specs=[VMEM],
        out_specs=VMEM,
        compiler_params=params,
        cost_estimate=IDLE,
        name="begin_block",
    )(fields)

    faces = len(grid.y_pairs) + len(grid.x_pairs)
    first_corner = groups(own_tiles) + sum(groups(c) for _, c in pieces[:faces])
    all_strips = f32(first_corner + sum(groups(c) for _, c in pieces[faces:]), ROWS, LANES)
    strips = pl.pallas_call(
        functools.partial(face_strip_kernel, grid, pieces[:faces]),
        out_shape=all_strips,
        in_specs=[VMEM] * (faces + 3),
        out_specs=VMEM,
        compiler_params=params,
        name="pack_face_strips",
    )(rows, block, own_strips, *arrived[:faces])
    strips = pl.pallas_call(
        lambda *refs: strip_kernel(grid, pieces[faces:], first_corner, refs[1:-1], refs[-1]),
        out_shape=all_strips,
        in_specs=[VMEM] * (1 + len(pieces) - faces),
        out_specs=VMEM,
        input_output_aliases={0: 0},
        compiler_params=params,
        name="pack_corner_strips",
    )(strips, *arrived[faces:])
    strips = lax.ppermute(strips, "gz", swap)

    block = pl.pallas_call(
        lambda *refs: assemble_kernel(grid, *refs),
        out_shape=extended,
        in_specs=[VMEM] * (1 + len(pieces)),
        out_specs=VMEM,
        input_output_aliases={0: 0},
        compiler_params=params,
        name="assemble",
    )(block, *arrived)

    _, velocity, table = pl.pallas_call(
        functools.partial(main_kernel, grid, width, capacity),
        out_shape=[
            extended,
            f32(*velocity_start.shape),
            f32(slots // 256, 6 * STEPS, 256),
        ],
        in_specs=[VMEM] * 6,
        out_specs=[VMEM, HBM, VMEM],
        scratch_shapes=[
            pltpu.VMEM(extended.shape, jnp.float32),
            pltpu.VMEM((STEPS * 6 * grid.cx * grid.cy, 2 * grid.cz), jnp.bfloat16),
            pltpu.VMEM((16, count + 4 * LANES), jnp.float32),
            pltpu.SMEM(force.shape, jnp.float32),
            pltpu.SMEM(spans.shape, jnp.int32),
            pltpu.SemaphoreType.DMA((3,)),
        ],
        input_output_aliases={0: 0},
        compiler_params=params,
        name="two_steps",
    )(block, strips, lanes, rows, spans, force)

    values = 6 * STEPS
    if capacity != 256:
        table = table.transpose(1, 0, 2).reshape(values, width, capacity).transpose(1, 0, 2)
    sent = lax.all_to_all(table, ("gx", "gy"), split_axis=0, concat_axis=0, tiled=True)
    return velocity, sent.transpose(1, 0, 2).reshape(1, values, slots)


def solution(mesh):
    in_specs = (
        P(None, ("runs", "gx"), "gy", "gz"),
        P(None, ("runs", "gx"), "gy", "gz"),
        P(None, ("runs", "gx"), "gy", "gz"),
        P("runs"),
        P("runs", None),
        P(("runs", "gx"), "gy", "gz", None),
        P(("runs", "gx"), "gy", "gz", None, None),
    )
    out_specs = (P(None, ("runs", "gx"), "gy", "gz"), P(("runs", "gz"), None, ("gx", "gy")))
    return jax.shard_map(
        per_device, mesh=mesh, in_specs=in_specs, out_specs=out_specs, check_vma=False
    )
```
